32 devices in a mesh: groups: 2 (over y), row: 4 (over z), col: 4 (over x, core).
Axes of the slice: x: 2, y: 2, z: 4, core: 2. Of those that a mesh axis runs over, the one named last changes fastest.
Arguments:
- queries: bfloat16 [8, 512, 512], P(('groups', 'col'), 'row'), parts along dimension 0, may hold values from -6 to 6
- keys: bfloat16 [8, 512, 128], P(('groups', 'row'), 'col'), parts along dimension 0, may hold values from -6 to 6
- values: bfloat16 [8, 512, 128], P(('groups', 'row'), 'col'), parts along dimension 0, may hold values from -6 to 6
- block_list: int32 [8, 4, 4, 4], P('groups'), parts along dimension 0, may hold values from 0 to 3, as said below
- block_count: int32 [8, 4, 4], P('groups'), parts along dimension 0, may hold values from 0 to 4, as said below
Outputs:
- attended: bfloat16 [8, 512, 512], P(('groups', 'col'), 'row'), parts along dimension 0
The draws below stay inside these ranges and needn't reach their ends.
There are 2 independent parts, one for each index of `groups`. The reference program is written for one: setup_inputs(seed, part) draws one part's arguments, and reference() takes and returns one part's arrays. A program takes and returns all parts, laid end to end along the dimension named above; each array names one. Nothing has to cross between parts.
Inputs may be any that keep to these rules, and one draw needn't show every extreme that they name: For query block i = c * 4 + q, the first block_count[c, q, r] entries of block_list[c, q, r] are distinct positions j in increasing order of key blocks r * 4 + j that do not lie after block i; block i itself is always listed in its panel; the remaining entries are other positions of the panel and carry no meaning. `block_count`: some query block lists all 4 blocks of some panel in every draw.
All inputs are finite; a program needn't handle non-finite values.
Results may differ from the reference program's by a relative error of at most 0.0036.
Values may be sent and summed in bfloat16 or wider, within the bound.
No kernel may reach another device: no remote copies, remote signals or barrier semaphores. Data moves between devices by JAX's collectives and lax.ppermute only.
A program may use at most 64 MiB of HBM per device.

```python
import jax
import jax.numpy as jnp
from jax import lax

BLOCK = 128
HD = 128
GROUP = 4
QP = 512
KP = 512
QBP = 4
KBP = 4
SEQ = 2048
N_ROW = 4
N_COL = 4


def active_blocks(key):
    total_blocks = SEQ // BLOCK
    vert_key, slash_key = jax.random.split(jax.random.fold_in(key, 11))
    vertical = jax.random.randint(vert_key, (total_blocks,), 0, 8) == 0
    vertical = vertical.at[0].set(True)
    slash_hit = jax.random.randint(slash_key, (total_blocks,), 0, 16) == 0
    query_index = jnp.arange(total_blocks, dtype=jnp.int32)[:, None]
    key_index = jnp.arange(total_blocks, dtype=jnp.int32)[None, :]
    distance = query_index - key_index
    near = distance < KBP
    diagonal_hit = slash_hit[jnp.clip(distance, 0, total_blocks - 1)]
    active = (distance >= 0) & (near | vertical[None, :] | diagonal_hit)
    return active.reshape(N_COL, QBP, N_ROW, KBP)


def draw_block_count(key, part):
    return jnp.sum(active_blocks(key).astype(jnp.int32), axis=-1).astype(jnp.int32)


def draw_block_list(key, part):
    active = active_blocks(key).astype(jnp.int32)
    order_key = (1 - active) * KBP + jnp.arange(KBP, dtype=jnp.int32)
    return jnp.argsort(order_key, axis=-1, stable=True).astype(jnp.int32)


def drawn_pattern(key):
    return jax.random.bernoulli(jax.random.fold_in(key, 23), 0.5, (HD,)).astype(jnp.float32) * 2.0 - 1.0


def half_columns():
    return jnp.arange(HD, dtype=jnp.int32) < HD // 2


def far_positions():
    return (3 * SEQ // 8 + 7, 7 * SEQ // 8 + 7)


def draw_queries(key, part):
    base_key = jax.random.fold_in(key, 5)
    pattern = drawn_pattern(key)
    flat = jax.random.normal(base_key, (SEQ, GROUP * HD), jnp.float32)
    chosen_cols = half_columns()
    for position in far_positions():
        flat = flat.at[position, :HD].set(jnp.where(chosen_cols, 6.0 * pattern, flat[position, :HD]))
    flat = jnp.clip(flat, -6.0, 6.0)
    return flat.reshape(N_COL, QP, GROUP * HD).astype(jnp.bfloat16)


def draw_keys(key, part):
    base_key = jax.random.fold_in(key, 6)
    pattern = drawn_pattern(key)
    flat = jax.random.normal(base_key, (SEQ, HD), jnp.float32)
    chosen_cols = half_columns()
    sink_scale = 4.0
    sink_shrink = 2.0 * HD ** 0.5 / (6.0 * sink_scale * (HD // 2))
    flat = flat.at[0].set(jnp.where(chosen_cols, sink_scale * pattern, flat[0]))
    flat = flat.at[1].set(jnp.where(chosen_cols, sink_scale * (1.0 - sink_shrink) * pattern, flat[1]))
    flat = jnp.clip(flat, -6.0, 6.0)
    return flat.reshape(N_ROW, KP, HD).astype(jnp.bfloat16)


def block_levels(stream_key, extent, pieces, least, largest):
    factor_of = 1.0
    for dim, blocks in pieces:
        steps = jax.random.uniform(jax.random.fold_in(jax.random.fold_in(stream_key, 6), dim), (blocks,), jnp.float32, least / len(pieces), largest / len(pieces))
        factor_of = factor_of * jnp.repeat(jnp.exp(steps), extent[dim] // blocks).reshape((-1,) + (1,) * (len(extent) - 1 - dim))
    return factor_of


def centred(stream_key, dims, scale, reach, shards=(), held_as=jnp.bfloat16):
    gain = block_levels(stream_key, dims, shards, -0.22, 0.18) if shards else 1.0
    values = jax.random.normal(stream_key, dims, jnp.float32) * scale * gain
    return jnp.minimum(jnp.maximum(values, -reach), reach).astype(held_as)


def setup_inputs(seed: int = 0, part: int = 0) -> dict:
    key_list = jax.random.split(jax.random.key(seed), 6)
    part_keys = jax.random.split(jax.random.fold_in(key_list[5], part), 6)
    queries = draw_queries(jax.random.fold_in(jax.random.fold_in(key_list[5], part), 71), part)
    keys = draw_keys(jax.random.fold_in(jax.random.fold_in(key_list[5], part), 71), part)
    values = centred(part_keys[2], (N_ROW, KP, HD), 1.0, 6.0, ((0, 4), (1, 4)))
    block_list = draw_block_list(jax.random.fold_in(jax.random.fold_in(key_list[5], part), 71), part)
    block_count = draw_block_count(jax.random.fold_in(jax.random.fold_in(key_list[5], part), 71), part)
    return dict(queries=queries, keys=keys, values=values, block_list=block_list, block_count=block_count)


floor_score = -1.0e30


def attend_tile(query_blocks, slot_lists, slot_counts, first_block, key_blocks, value_blocks, key_start):
    number = query_blocks.shape[0]
    block_rows = query_blocks.shape[1]
    heads = query_blocks.shape[2]
    head_size = query_blocks.shape[3]
    query_pos = (first_block * block_rows + jnp.arange(number * block_rows, dtype=jnp.int32)).reshape(number, block_rows)
    offsets = jnp.arange(block_rows, dtype=jnp.int32)
    score_scale = 1.0 / (head_size ** 0.5)
    query_wide = query_blocks.astype(jnp.float32)
    start_state = (jnp.full((number, block_rows, heads), floor_score, jnp.float32),
                   jnp.zeros((number, block_rows, heads), jnp.float32),
                   jnp.zeros((number, block_rows, heads, head_size), jnp.float32))

    def advance(slot_index, state):
        run_max, run_sum, run_acc = state
        chosen = lax.dynamic_index_in_dim(slot_lists, slot_index, 1, keepdims=False).astype(jnp.int32)
        keys_now = jnp.take(key_blocks, chosen, axis=0).astype(jnp.float32)
        values_now = jnp.take(value_blocks, chosen, axis=0).astype(jnp.float32)
        scores = jnp.einsum("nqgd,nkd->nqgk", query_wide, keys_now, precision=lax.Precision.HIGHEST) * score_scale
        key_pos = key_start + chosen[:, None] * block_rows + offsets[None, :]
        usable = (slot_index < slot_counts)[:, None, None, None] & (query_pos[:, :, None, None] >= key_pos[:, None, None, :])
        scores = jnp.where(usable, scores, floor_score)
        new_max = jnp.maximum(run_max, jnp.max(scores, axis=-1))
        decay = jnp.exp(run_max - new_max)
        weights = jnp.where(usable, jnp.exp(scores - new_max[..., None]), 0.0)
        run_sum = run_sum * decay + jnp.sum(weights, axis=-1)
        rounded = lax.optimization_barrier(weights.astype(jnp.bfloat16)).astype(jnp.float32)
        mixed = jnp.einsum("nqgk,nkd->nqgd", rounded, values_now, precision=lax.Precision.HIGHEST)
        run_acc = run_acc * decay[..., None] + mixed
        return new_max, run_sum, run_acc

    bound = jnp.max(slot_counts).astype(jnp.int32)
    final_max, final_sum, final_acc = lax.fori_loop(jnp.int32(0), bound, advance, start_state)
    rows = number * block_rows
    return final_acc.reshape(rows, heads, head_size), final_max.reshape(rows, heads), final_sum.reshape(rows, heads)


def reference(queries, keys, values, block_list, block_count):
    key_grid = keys.reshape(N_ROW, KBP, BLOCK, HD)
    value_grid = values.reshape(N_ROW, KBP, BLOCK, HD)

    def one_query_panel(col_index):
        query_blocks = lax.dynamic_index_in_dim(queries, col_index, 0, keepdims=False).reshape(QBP, BLOCK, GROUP, HD)
        panel_lists = lax.dynamic_index_in_dim(block_list, col_index, 0, keepdims=False)
        panel_counts = lax.dynamic_index_in_dim(block_count, col_index, 0, keepdims=False)
        first_block = col_index * QBP

        def one_key_panel(state, panel_index):
            top, numer, denom = state
            part_acc, part_max, part_sum = attend_tile(
                query_blocks,
                lax.dynamic_index_in_dim(panel_lists, panel_index, 1, keepdims=False),
                lax.dynamic_index_in_dim(panel_counts, panel_index, 1, keepdims=False),
                first_block,
                lax.dynamic_index_in_dim(key_grid, panel_index, 0, keepdims=False),
                lax.dynamic_index_in_dim(value_grid, panel_index, 0, keepdims=False),
                panel_index * KP)
            new_top = jnp.maximum(top, part_max)
            old_weight = jnp.exp(top - new_top)
            part_weight = jnp.exp(part_max - new_top)
            numer = numer * old_weight[..., None] + part_acc * part_weight[..., None]
            denom = denom * old_weight + part_sum * part_weight
            return (new_top, numer, denom), None

        start_state = (jnp.full((QP, GROUP), floor_score, jnp.float32),
                       jnp.zeros((QP, GROUP, HD), jnp.float32),
                       jnp.zeros((QP, GROUP), jnp.float32))
        final_state, unused = lax.scan(one_key_panel, start_state, jnp.arange(N_ROW, dtype=jnp.int32))
        top, numer, denom = final_state
        return (numer / denom[..., None]).reshape(QP, GROUP * HD).astype(jnp.bfloat16)

    return lax.map(one_query_panel, jnp.arange(N_COL, dtype=jnp.int32))
```

```python
import functools
import math

import jax
import jax.numpy as jnp
from jax import lax
from jax.experimental import pallas as pl
from jax.experimental.pallas import tpu as pltpu
from jax.sharding import PartitionSpec as P

BLOCK = 128

floor_score = -1e30


def pack_kernel(k_ref, v_ref, out_ref):
    head_size = k_ref.shape[2]
    for s in range(k_ref.shape[1] // BLOCK):
        rows = pl.ds(s * BLOCK, BLOCK)
        out_ref[s, :BLOCK, :] = k_ref[0, rows, :]
        out_ref[s, BLOCK:, :] = v_ref[0, rows, :].T


def attend_kernel(heads, q_ref, kv_ref, list_hbm, count_hbm, out_ref,
                  qt_ref, score_ref, acc_ref, list_ref, count_ref, order_ref, sems):
    head_size = qt_ref.shape[0]
    width = qt_ref.shape[1]
    panels, slots = list_ref.shape
    own_blocks = q_ref.shape[1] // BLOCK
    col_index = lax.axis_index("col")
    row_index = lax.axis_index("row")
    blocks_per_panel = list_hbm.shape[1]
    factor = math.log2(math.e) / head_size**0.5

    for s in range(own_blocks):
        in_panel = row_index * own_blocks + s
        block = col_index * blocks_per_panel + in_panel
        copies = (
            pltpu.make_async_copy(list_hbm.at[col_index, in_panel], list_ref, sems.at[0]),
            pltpu.make_async_copy(count_hbm.at[col_index, in_panel], count_ref, sems.at[1]),
        )
        for copy in copies:
            copy.start()
        rows = pl.ds(s * BLOCK, BLOCK)
        for h in range(heads):
            cols = pl.ds(h * head_size, head_size)
            qt_ref[:, pl.ds(h * BLOCK, BLOCK)] = q_ref[0, rows, cols].T
        for copy in copies:
            copy.wait()

        def put_panel(r, total):
            def put(n, unused):
                order_ref[total + n] = r * slots + list_ref[r, n]
                return unused
            lax.fori_loop(0, count_ref[r], put, 0)
            return total + count_ref[r]

        total = lax.fori_loop(0, panels, put_panel, 0)

        def score(t, top):
            which = order_ref[t]
            found = jnp.dot(kv_ref[which, :BLOCK, :], qt_ref[...], preferred_element_type=jnp.float32)
            offset = (block - which) * BLOCK
            key_at = lax.broadcasted_iota(jnp.int32, (BLOCK, width), 0)
            query_at = lax.broadcasted_iota(jnp.int32, (BLOCK, width), 1) % BLOCK + offset
            found = jnp.where(query_at >= key_at, found, floor_score)
            score_ref[t] = found
            return jnp.maximum(top, jnp.max(found.reshape(BLOCK // 8, 8, width), axis=0))

        top = lax.fori_loop(0, total, score, jnp.full((8, width), floor_score, jnp.float32))
        top = jnp.max(top, axis=0, keepdims=True) * factor
        acc_ref[...] = jnp.zeros_like(acc_ref)

        def mix(t, denom):
            which = order_ref[t]
            weights = jnp.exp2(score_ref[t] * factor - top)
            acc_ref[...] += jnp.dot(kv_ref[which, BLOCK:, :], weights.astype(jnp.bfloat16), preferred_element_type=jnp.float32)
            return denom + jnp.sum(weights.reshape(BLOCK // 8, 8, width), axis=0)

        denom = lax.fori_loop(0, total, mix, jnp.zeros((8, width), jnp.float32))
        final = acc_ref[...] / jnp.sum(denom, axis=0, keepdims=True)
        for h in range(heads):
            cols = pl.ds(h * head_size, head_size)
            out_ref[0, rows, cols] = final[:, h * BLOCK:(h + 1) * BLOCK].T.astype(out_ref.dtype)


def per_device(queries, keys, values, block_list, block_count):
    head_size = keys.shape[2]
    heads = queries.shape[2] // head_size
    own_keys = keys.shape[1]
    vmem = pl.BlockSpec(memory_space=pltpu.VMEM)
    anywhere = pl.BlockSpec(memory_space=pl.ANY)
    packed = pl.pallas_call(
        pack_kernel,
        out_shape=jax.ShapeDtypeStruct((own_keys // BLOCK, 2 * BLOCK, head_size), keys.dtype),
        in_specs=[vmem, vmem],
        out_specs=vmem,
        name="pack",
    )(keys, values)
    gathered = lax.all_gather(packed, ("row", "col"), axis=0, tiled=True)
    blocks = gathered.shape[0]
    panels, slots = block_list.shape[2:]
    return pl.pallas_call(
        functools.partial(attend_kernel, heads),
        out_shape=jax.ShapeDtypeStruct(queries.shape, jnp.bfloat16),
        in_specs=[vmem, vmem, anywhere, anywhere],
        out_specs=vmem,
        scratch_shapes=[
            pltpu.VMEM((head_size, heads * BLOCK), jnp.bfloat16),
            pltpu.VMEM((blocks, BLOCK, heads * BLOCK), jnp.float32),
            pltpu.VMEM((head_size, heads * BLOCK), jnp.float32),
            pltpu.SMEM((panels, slots), jnp.int32),
            pltpu.SMEM((panels,), jnp.int32),
            pltpu.SMEM((blocks,), jnp.int32),
            pltpu.SemaphoreType.DMA((2,)),
        ],
        compiler_params=pltpu.CompilerParams(vmem_limit_bytes=56 * 1024 * 1024),
        name="attend",
    )(queries, gathered, block_list, block_count)


def solution(mesh):
    placed = (
        P(("groups", "col"), "row", None),
        P(("groups", "row"), "col", None),
        P(("groups", "row"), "col", None),
        P("groups", None, None, None),
        P("groups", None, None),
    )
    return jax.shard_map(
        per_device,
        mesh=mesh,
        in_specs=placed,
        out_specs=P(("groups", "col"), "row", None),
        check_vma=False,
    )
```

```python
import functools
import math

import jax
import jax.numpy as jnp
from jax import lax
from jax.experimental import pallas as pl
from jax.experimental.pallas import tpu as pltpu
from jax.sharding import PartitionSpec as P

BLOCK = 128

floor_score = -1e30


def pack_kernel(k_ref, v_ref, out_ref):
    head_size = k_ref.shape[2]
    for s in range(k_ref.shape[1] // BLOCK):
        rows = pl.ds(s * BLOCK, BLOCK)
        out_ref[s, :BLOCK, :] = k_ref[0, rows, :]
        out_ref[s, BLOCK:, :] = v_ref[0, rows, :].T


def attend_kernel(heads, q_ref, kv_ref, list_hbm, count_hbm, out_ref,
                  qt_ref, score_ref, acc_ref, list_ref, count_ref, order_ref, sems):
    head_size = qt_ref.shape[0]
    width = qt_ref.shape[1]
    panels, slots = list_ref.shape
    own_blocks = q_ref.shape[1] // BLOCK
    col_index = lax.axis_index("col")
    row_index = lax.axis_index("row")
    blocks_per_panel = list_hbm.shape[1]
    factor = math.log2(math.e) / head_size**0.5

    for s in range(own_blocks):
        in_panel = row_index * own_blocks + s
        block = col_index * blocks_per_panel + in_panel
        copies = (
            pltpu.make_async_copy(list_hbm.at[col_index, in_panel], list_ref, sems.at[0]),
            pltpu.make_async_copy(count_hbm.at[col_index, in_panel], count_ref, sems.at[1]),
        )
        for copy in copies:
            copy.start()
        rows = pl.ds(s * BLOCK, BLOCK)
        for h in range(heads):
            cols = pl.ds(h * head_size, head_size)
            qt_ref[:, pl.ds(h * BLOCK, BLOCK)] = q_ref[0, rows, cols].T
        for copy in copies:
            copy.wait()

        def put_panel(r, total):
            def put(n, unused):
                order_ref[total + n] = r * slots + list_ref[r, n]
                return unused
            lax.fori_loop(0, count_ref[r], put, 0)
            return total + count_ref[r]

        total = lax.fori_loop(0, panels, put_panel, 0)

        def score(t, top):
            which = order_ref[t]
            found = jnp.dot(kv_ref[which, :BLOCK, :], qt_ref[...], preferred_element_type=jnp.float32)
            offset = (block - which) * BLOCK
            key_at = lax.broadcasted_iota(jnp.int32, (BLOCK, width), 0)
            query_at = lax.broadcasted_iota(jnp.int32, (BLOCK, width), 1) % BLOCK + offset
            found = jnp.where(query_at >= key_at, found, floor_score)
            score_ref[t] = found
            return jnp.maximum(top, jnp.max(found.reshape(BLOCK // 8, 8, width), axis=0))

        top = lax.fori_loop(0, total, score, jnp.full((8, width), floor_score, jnp.float32))
        top = jnp.max(top, axis=0, keepdims=True) * factor
        acc_ref[...] = jnp.zeros_like(acc_ref)

        def mix(t, denom):
            which = order_ref[t]
            weights = jnp.exp2(score_ref[t] * factor - top)
            acc_ref[...] += jnp.dot(kv_ref[which, BLOCK:, :], weights.astype(jnp.bfloat16), preferred_element_type=jnp.float32)
            return denom + jnp.sum(weights.reshape(BLOCK // 8, 8, width), axis=0)

        denom = lax.fori_loop(0, total, mix, jnp.zeros((8, width), jnp.float32))
        final = acc_ref[...] / jnp.sum(denom, axis=0, keepdims=True)
        for h in range(heads):
            cols = pl.ds(h * head_size, head_size)
            out_ref[0, rows, cols] = final[:, h * BLOCK:(h + 1) * BLOCK].T.astype(out_ref.dtype)


def per_device(queries, keys, values, block_list, block_count):
    head_size = keys.shape[2]
    heads = queries.shape[2] // head_size
    own_keys = keys.shape[1]
    vmem = pl.BlockSpec(memory_space=pltpu.VMEM)
    anywhere = pl.BlockSpec(memory_space=pl.ANY)
    packed = pl.pallas_call(
        pack_kernel,
        out_shape=jax.ShapeDtypeStruct((own_keys // BLOCK, 2 * BLOCK, head_size), keys.dtype),
        in_specs=[vmem, vmem],
        out_specs=vmem,
        name="pack",
    )(keys, values)
    packed = packed.reshape(1, -1, head_size)
    gathered = lax.all_gather(packed, ("row", "col"), axis=1, tiled=True)
    gathered = gathered.reshape(-1, 2 * BLOCK, head_size)
    blocks = gathered.shape[0]
    panels, slots = block_list.shape[2:]
    return pl.pallas_call(
        functools.partial(attend_kernel, heads),
        out_shape=jax.ShapeDtypeStruct(queries.shape, jnp.bfloat16),
        in_specs=[vmem, vmem, anywhere, anywhere],
        out_specs=vmem,
        scratch_shapes=[
            pltpu.VMEM((head_size, heads * BLOCK), jnp.bfloat16),
            pltpu.VMEM((blocks, BLOCK, heads * BLOCK), jnp.float32),
            pltpu.VMEM((head_size, heads * BLOCK), jnp.float32),
            pltpu.SMEM((panels, slots), jnp.int32),
            pltpu.SMEM((panels,), jnp.int32),
            pltpu.SMEM((blocks,), jnp.int32),
            pltpu.SemaphoreType.DMA((2,)),
        ],
        compiler_params=pltpu.CompilerParams(vmem_limit_bytes=56 * 1024 * 1024),
        name="attend",
    )(queries, gathered, block_list, block_count)


def solution(mesh):
    placed = (
        P(("groups", "col"), "row", None),
        P(("groups", "row"), "col", None),
        P(("groups", "row"), "col", None),
        P("groups", None, None, None),
        P("groups", None, None),
    )
    return jax.shard_map(
        per_device,
        mesh=mesh,
        in_specs=placed,
        out_specs=P(("groups", "col"), "row", None),
        check_vma=False,
    )
```

```python
import functools
import math

import jax
import jax.numpy as jnp
from jax import lax
from jax.experimental import pallas as pl
from jax.experimental.pallas import tpu as pltpu
from jax.sharding import PartitionSpec as P

BLOCK = 128

floor_score = -1e30


def pack_kernel(k_ref, v_ref, out_ref):
    head_size = k_ref.shape[2]
    for s in range(k_ref.shape[1] // BLOCK):
        rows = pl.ds(s * BLOCK, BLOCK)
        out_ref[s, :BLOCK, :] = k_ref[0, rows, :]
        out_ref[s, BLOCK:, :] = v_ref[0, rows, :].T


def attend_kernel(heads, places, q_ref, *refs):
    blocks_in = refs[:len(places)]
    (list_hbm, count_hbm, out_ref, kv_ref, qt_ref, score_ref, acc_ref,
     list_ref, count_ref, order_ref, sems) = refs[len(places):]
    head_size = qt_ref.shape[0]
    width = qt_ref.shape[1]
    panels, slots = list_ref.shape
    own_blocks = q_ref.shape[1] // BLOCK
    col_index = lax.axis_index("col")
    row_index = lax.axis_index("row")
    blocks_per_panel = list_hbm.shape[1]
    factor = math.log2(math.e) / head_size**0.5
    cols = lax.axis_size("col")
    rows_ax = lax.axis_size("row")

    for (row_back, chip_back, other), block_in in zip(places, blocks_in):
        from_row = lax.rem(row_index + rows_ax - row_back, rows_ax)
        core = lax.rem(col_index, 2)
        chip = lax.rem(col_index // 2 + cols // 2 - chip_back, cols // 2)
        from_col = chip * 2 + (1 - core if other else core)
        per = block_in.shape[0]
        first = (from_row * cols + from_col) * per
        for s in range(per):
            kv_ref[first + s] = block_in[s]

    for s in range(own_blocks):
        in_panel = row_index * own_blocks + s
        block = col_index * blocks_per_panel + in_panel
        copies = (
            pltpu.make_async_copy(list_hbm.at[col_index, in_panel], list_ref, sems.at[0]),
            pltpu.make_async_copy(count_hbm.at[col_index, in_panel], count_ref, sems.at[1]),
        )
        for copy in copies:
            copy.start()
        rows = pl.ds(s * BLOCK, BLOCK)
        for h in range(heads):
            at = pl.ds(h * head_size, head_size)
            qt_ref[:, pl.ds(h * BLOCK, BLOCK)] = q_ref[0, rows, at].T
        for copy in copies:
            copy.wait()

        def put_panel(r, total):
            def put(n, unused):
                order_ref[total + n] = r * slots + list_ref[r, n]
                return unused
            lax.fori_loop(0, count_ref[r], put, 0)
            return total + count_ref[r]

        total = lax.fori_loop(0, panels, put_panel, 0)

        def score(t, top):
            which = order_ref[t]
            found = jnp.dot(kv_ref[which, :BLOCK, :], qt_ref[...], preferred_element_type=jnp.float32)
            offset = (block - which) * BLOCK
            key_at = lax.broadcasted_iota(jnp.int32, (BLOCK, width), 0)
            query_at = lax.broadcasted_iota(jnp.int32, (BLOCK, width), 1) % BLOCK + offset
            found = jnp.where(query_at >= key_at, found, floor_score)
            score_ref[t] = found
            return jnp.maximum(top, jnp.max(found.reshape(BLOCK // 8, 8, width), axis=0))

        top = lax.fori_loop(0, total, score, jnp.full((8, width), floor_score, jnp.float32))
        top = jnp.max(top, axis=0, keepdims=True) * factor
        acc_ref[...] = jnp.zeros_like(acc_ref)

        def mix(t, denom):
            which = order_ref[t]
            weights = jnp.exp2(score_ref[t] * factor - top)
            acc_ref[...] += jnp.dot(kv_ref[which, BLOCK:, :], weights.astype(jnp.bfloat16), preferred_element_type=jnp.float32)
            return denom + jnp.sum(weights.reshape(BLOCK // 8, 8, width), axis=0)

        denom = lax.fori_loop(0, total, mix, jnp.zeros((8, width), jnp.float32))
        final = acc_ref[...] / jnp.sum(denom, axis=0, keepdims=True)
        for h in range(heads):
            at = pl.ds(h * head_size, head_size)
            out_ref[0, rows, at] = final[:, h * BLOCK:(h + 1) * BLOCK].T.astype(out_ref.dtype)


def per_device(queries, keys, values, block_list, block_count):
    head_size = keys.shape[2]
    heads = queries.shape[2] // head_size
    own_keys = keys.shape[1]
    rows = lax.axis_size("row")
    cols = lax.axis_size("col")
    chips = cols // 2
    vmem = pl.BlockSpec(memory_space=pltpu.VMEM)
    anywhere = pl.BlockSpec(memory_space=pl.ANY)
    packed = pl.pallas_call(
        pack_kernel,
        out_shape=jax.ShapeDtypeStruct((own_keys // BLOCK, 2 * BLOCK, head_size), keys.dtype),
        in_specs=[vmem, vmem],
        out_specs=vmem,
        name="pack",
    )(keys, values)
    parts = {(0, 0, 0): packed}
    for back in range(1, rows):
        parts[back, 0, 0] = lax.ppermute(packed, "row", [(i, (i + back) % rows) for i in range(rows)])
    for back in range(rows):
        for chip in range(1, chips):
            perm = [(i, (i + 2 * chip) % cols) for i in range(cols)]
            parts[back, chip, 0] = lax.ppermute(parts[back, 0, 0], "col", perm)
    for back in range(rows):
        for chip in range(chips):
            perm = [(i, i ^ 1) for i in range(cols)]
            parts[back, chip, 1] = lax.ppermute(parts[back, chip, 0], "col", perm)
    places = tuple(parts)
    blocks = len(places) * packed.shape[0]
    panels, slots = block_list.shape[2:]
    scratch_bytes = blocks * BLOCK * (heads * BLOCK * 4 + 2 * head_size * 2)
    return pl.pallas_call(
        functools.partial(attend_kernel, heads, places),
        out_shape=jax.ShapeDtypeStruct(queries.shape, jnp.bfloat16),
        in_specs=[vmem] * (1 + len(places)) + [anywhere, anywhere],
        out_specs=vmem,
        scratch_shapes=[
            pltpu.VMEM((blocks, 2 * BLOCK, head_size), jnp.bfloat16),
            pltpu.VMEM((head_size, heads * BLOCK), jnp.bfloat16),
            pltpu.VMEM((blocks, BLOCK, heads * BLOCK), jnp.float32),
            pltpu.VMEM((head_size, heads * BLOCK), jnp.float32),
            pltpu.SMEM((panels, slots), jnp.int32),
            pltpu.SMEM((panels,), jnp.int32),
            pltpu.SMEM((blocks,), jnp.int32),
            pltpu.SemaphoreType.DMA((2,)),
        ],
        compiler_params=pltpu.CompilerParams(vmem_limit_bytes=scratch_bytes + 3 * 1024 * 1024),
        name="attend",
    )(queries, *parts.values(), block_list, block_count)


def solution(mesh):
    placed = (
        P(("groups", "col"), "row", None),
        P(("groups", "row"), "col", None),
        P(("groups", "row"), "col", None),
        P("groups", None, None, None),
        P("groups", None, None),
    )
    return jax.shard_map(
        per_device,
        mesh=mesh,
        in_specs=placed,
        out_specs=P(("groups", "col"), "row", None),
        check_vma=False,
    )
```

```python
import functools
import math

import jax
import jax.numpy as jnp
from jax import lax
from jax.experimental import pallas as pl
from jax.experimental.pallas import tpu as pltpu
from jax.sharding import PartitionSpec as P

BLOCK = 128
CORES = 2

floor_score = -1e30


def pack_block(out_ref, slot, keys, values):
    out_ref[slot, :BLOCK, :] = keys
    out_ref[slot, BLOCK:, :] = values.T


def pack_kernel(own_ref, k_ref, v_ref, out_ref):
    per = own_ref.shape[0]
    out_ref[:per] = own_ref[...]
    for s in range(per):
        rows = pl.ds(s * BLOCK, BLOCK)
        pack_block(out_ref, per + s, k_ref[0, rows, :], v_ref[0, rows, :])


def join_kernel(first_ref, second_ref, out_ref):
    held = first_ref.shape[0]
    out_ref[:held] = first_ref[...]
    out_ref[held:] = second_ref[...]


def prepare_kernel(heads, q_hbm, k_hbm, v_hbm, list_hbm, count_hbm, own_ref, qt_ref, order_ref,
                   q_ref, k_ref, v_ref, list_ref, count_ref, sems):
    own_blocks, head_size = qt_ref.shape[:2]
    panels, slots = list_ref.shape[1:]
    col_index = lax.axis_index("col")
    first = lax.axis_index("row") * own_blocks
    sources = (
        k_hbm,
        v_hbm,
        q_hbm,
        list_hbm.at[col_index, pl.ds(first, own_blocks)],
        count_hbm.at[col_index, pl.ds(first, own_blocks)],
    )
    copies = [
        pltpu.make_async_copy(source, dest, sems.at[n])
        for n, (source, dest) in enumerate(zip(sources, (k_ref, v_ref, q_ref, list_ref, count_ref)))
    ]
    for copy in copies:
        copy.start()
    for copy in copies:
        copy.wait()
    for s in range(own_ref.shape[0]):
        rows = pl.ds(s * BLOCK, BLOCK)
        pack_block(own_ref, s, k_ref[0, rows, :], v_ref[0, rows, :])
    for s in range(own_blocks):
        for h in range(heads):
            tile = q_ref[0, pl.ds(s * BLOCK, BLOCK), pl.ds(h * head_size, head_size)]
            qt_ref[s, :, pl.ds(h * BLOCK, BLOCK)] = tile.T

        def put_panel(r, total):
            def put(n, unused):
                order_ref[s, total + n] = r * slots + list_ref[s, r, n]
                return unused

            lax.fori_loop(0, count_ref[s, r], put, 0)
            return total + count_ref[s, r]

        order_ref[s, panels * slots] = lax.fori_loop(0, panels, put_panel, 0)


def attend_kernel(heads, places, qt_ref, order_hbm, *refs):
    pieces = refs[: len(places)]
    out_ref, kv_ref, score_ref, acc_ref, order_ref, sem = refs[len(places) :]
    own_blocks, head_size, width = qt_ref.shape
    col_index = lax.axis_index("col")
    row_index = lax.axis_index("row")
    cols = lax.axis_size("col")
    per = kv_ref.shape[0] // (cols * lax.axis_size("row"))
    blocks = order_ref.shape[1] - 1
    factor = math.log2(math.e) / head_size**0.5

    copy = pltpu.make_async_copy(order_hbm, order_ref, sem)
    copy.start()
    for piece, where in zip(pieces, places):
        for n, (row_flip, col_flip) in enumerate(where):
            first = ((row_index ^ row_flip) * cols + (col_index ^ col_flip)) * per
            for s in range(per):
                kv_ref[first + s] = piece[n * per + s]
    copy.wait()

    for s in range(own_blocks):
        rows = pl.ds(s * BLOCK, BLOCK)
        last = order_ref[s, blocks] - 1

        def score(t, top, found=None):
            which = order_ref[s, t]
            found = jnp.dot(kv_ref[which, :BLOCK, :], qt_ref[s], preferred_element_type=jnp.float32)
            score_ref[t] = found
            return jnp.maximum(top, jnp.max(found.reshape(BLOCK // 8, 8, width), axis=0))

        top = lax.fori_loop(0, last, score, jnp.full((8, width), floor_score, jnp.float32))
        found = jnp.dot(kv_ref[order_ref[s, last], :BLOCK, :], qt_ref[s], preferred_element_type=jnp.float32)
        key_at = lax.broadcasted_iota(jnp.int32, (BLOCK, width), 0)
        query_at = lax.broadcasted_iota(jnp.int32, (BLOCK, width), 1) % BLOCK
        found = jnp.where(query_at >= key_at, found, floor_score)
        score_ref[last] = found
        top = jnp.maximum(top, jnp.max(found.reshape(BLOCK // 8, 8, width), axis=0))
        top = jnp.max(top, axis=0, keepdims=True) * factor
        acc_ref[...] = jnp.zeros_like(acc_ref)

        def mix(t, denom):
            which = order_ref[s, t]
            weights = jnp.exp2(score_ref[t] * factor - top)
            acc_ref[...] += jnp.dot(
                kv_ref[which, BLOCK:, :], weights.astype(jnp.bfloat16), preferred_element_type=jnp.float32
            )
            return denom + jnp.sum(weights.reshape(BLOCK // 8, 8, width), axis=0)

        denom = lax.fori_loop(0, last + 1, mix, jnp.zeros((8, width), jnp.float32))
        final = acc_ref[...] / jnp.sum(denom, axis=0, keepdims=True)
        for h in range(heads):
            at = pl.ds(h * head_size, head_size)
            out_ref[0, rows, at] = final[:, h * BLOCK : (h + 1) * BLOCK].T.astype(out_ref.dtype)


def swap(array, axis, flip):
    size = lax.axis_size(axis)
    return lax.ppermute(array, axis, [(i, i ^ flip) for i in range(size)])


def per_device(queries, keys, values, block_list, block_count):
    head_size = keys.shape[2]
    heads = queries.shape[2] // head_size
    own_blocks = queries.shape[1] // BLOCK
    per = keys.shape[1] // BLOCK
    rows = lax.axis_size("row")
    cols = lax.axis_size("col")
    panels, slots = block_list.shape[2:]
    blocks = panels * slots
    vmem = pl.BlockSpec(memory_space=pltpu.VMEM)
    smem = pl.BlockSpec(memory_space=pltpu.SMEM)
    hbm = pl.BlockSpec(memory_space=pltpu.HBM)
    anywhere = pl.BlockSpec(memory_space=pl.ANY)

    flip = rows // 2
    came = (swap(keys, "row", flip), swap(values, "row", flip))
    own, queries_across, order = pl.pallas_call(
        functools.partial(prepare_kernel, heads),
        out_shape=(
            jax.ShapeDtypeStruct((per, 2 * BLOCK, head_size), keys.dtype),
            jax.ShapeDtypeStruct((own_blocks, head_size, heads * BLOCK), queries.dtype),
            jax.ShapeDtypeStruct((own_blocks, blocks + 1), jnp.int32),
        ),
        in_specs=[hbm] * 5,
        out_specs=(vmem, vmem, smem),
        scratch_shapes=[
            pltpu.VMEM(queries.shape, queries.dtype),
            pltpu.VMEM(keys.shape, keys.dtype),
            pltpu.VMEM(values.shape, values.dtype),
            pltpu.SMEM((own_blocks, panels, slots), jnp.int32),
            pltpu.SMEM((own_blocks, panels), jnp.int32),
            pltpu.SemaphoreType.DMA((5,)),
        ],
        name="prepare",
    )(queries, keys, values, block_list, block_count)
    held = pl.pallas_call(
        pack_kernel,
        out_shape=jax.ShapeDtypeStruct((2 * per, 2 * BLOCK, head_size), keys.dtype),
        in_specs=[vmem] * 3,
        out_specs=vmem,
        name="pack",
    )(own, *came)
    place = [(0, 0), (flip, 0)]
    while flip > 2:
        flip //= 2
        came = swap(held, "row", flip)
        held = pl.pallas_call(
            join_kernel,
            out_shape=jax.ShapeDtypeStruct((2 * held.shape[0],) + held.shape[1:], held.dtype),
            in_specs=[vmem, vmem],
            out_specs=vmem,
            name="join",
        )(held, came)
        place += [(r ^ flip, c) for r, c in place]
    pieces = [(held, place)]
    if flip > 1:
        pieces.append((swap(held, "row", 1), [(r ^ 1, c) for r, c in place]))
    flip = CORES
    while flip < cols:
        pieces += [(swap(held, "col", flip), [(r, c ^ flip) for r, c in place]) for held, place in pieces]
        flip *= 2
    pieces += [(swap(held, "col", 1), [(r, c ^ 1) for r, c in place]) for held, place in pieces]

    held, places = zip(*pieces)
    scratch_bytes = blocks * BLOCK * (heads * BLOCK * 4 + 2 * head_size * 2)
    return pl.pallas_call(
        functools.partial(attend_kernel, heads, places),
        out_shape=jax.ShapeDtypeStruct(queries.shape, jnp.bfloat16),
        in_specs=[vmem, anywhere] + [vmem] * len(held),
        out_specs=vmem,
        scratch_shapes=[
            pltpu.VMEM((blocks, 2 * BLOCK, head_size), jnp.bfloat16),
            pltpu.VMEM((blocks, BLOCK, heads * BLOCK), jnp.float32),
            pltpu.VMEM((head_size, heads * BLOCK), jnp.float32),
            pltpu.SMEM((own_blocks, blocks + 1), jnp.int32),
            pltpu.SemaphoreType.DMA,
        ],
        compiler_params=pltpu.CompilerParams(vmem_limit_bytes=scratch_bytes + 3 * 1024 * 1024),
        name="attend",
    )(queries_across, order, *held)


def solution(mesh):
    placed = (
        P(("groups", "col"), "row", None),
        P(("groups", "row"), "col", None),
        P(("groups", "row"), "col", None),
        P("groups", None, None, None),
        P("groups", None, None),
    )
    return jax.shard_map(
        per_device,
        mesh=mesh,
        in_specs=placed,
        out_specs=P(("groups", "col"), "row", None),
        check_vma=False,
    )
```

```python
import functools
import math

import jax
import jax.numpy as jnp
from jax import lax
from jax.experimental import pallas as pl
from jax.experimental.pallas import tpu as pltpu
from jax.sharding import PartitionSpec as P

BLOCK = 128
CORES = 2

floor_score = -1e30


def pack_kernel(k_hbm, v_hbm, out_ref, sems):
    copies = []
    for s in range(out_ref.shape[0]):
        rows = pl.ds(s * BLOCK, BLOCK)
        for n, source in enumerate((k_hbm, v_hbm)):
            dest = out_ref.at[s, pl.ds(n * BLOCK, BLOCK), :]
            copies.append(pltpu.make_async_copy(source.at[0, rows, :], dest, sems.at[s, n]))
    for copy in copies:
        copy.start()
    for copy in copies:
        copy.wait()


def join_kernel(first_ref, second_ref, out_ref):
    held = first_ref.shape[0]
    out_ref[:held] = first_ref[...]
    out_ref[held:] = second_ref[...]


def prepare_kernel(heads, q_ref, list_hbm, count_hbm, qt_ref, order_ref, list_ref, count_ref, sems):
    own_blocks, head_size = qt_ref.shape[:2]
    panels, slots = list_ref.shape[1:]
    col_index = lax.axis_index("col")
    first = lax.axis_index("row") * own_blocks
    copies = (
        pltpu.make_async_copy(list_hbm.at[col_index, pl.ds(first, own_blocks)], list_ref, sems.at[0]),
        pltpu.make_async_copy(count_hbm.at[col_index, pl.ds(first, own_blocks)], count_ref, sems.at[1]),
    )
    for copy in copies:
        copy.start()
    for s in range(own_blocks):
        for h in range(heads):
            tile = q_ref[0, pl.ds(s * BLOCK, BLOCK), pl.ds(h * head_size, head_size)]
            qt_ref[s, :, pl.ds(h * BLOCK, BLOCK)] = tile.T
    for copy in copies:
        copy.wait()
    for s in range(own_blocks):

        def put_panel(r, total):
            def put(n, unused):
                order_ref[s, total + n] = r * slots + list_ref[s, r, n]
                return unused

            lax.fori_loop(0, count_ref[s, r], put, 0)
            return total + count_ref[s, r]

        order_ref[s, panels * slots] = lax.fori_loop(0, panels, put_panel, 0)


def attend_kernel(heads, places, qt_ref, order_hbm, *refs):
    pieces = refs[: len(places)]
    out_ref, kv_ref, score_ref, acc_ref, order_ref, sem = refs[len(places) :]
    own_blocks, head_size, width = qt_ref.shape
    col_index = lax.axis_index("col")
    row_index = lax.axis_index("row")
    cols = lax.axis_size("col")
    per = kv_ref.shape[0] // (cols * lax.axis_size("row"))
    blocks = order_ref.shape[1] - 1
    factor = math.log2(math.e) / head_size**0.5

    copy = pltpu.make_async_copy(order_hbm, order_ref, sem)
    copy.start()
    for piece, where in zip(pieces, places):
        for n, (row_flip, col_flip) in enumerate(where):
            first = ((row_index ^ row_flip) * cols + (col_index ^ col_flip)) * per
            for s in range(per):
                kv_ref[first + s] = piece[n * per + s]
    copy.wait()

    for s in range(own_blocks):
        rows = pl.ds(s * BLOCK, BLOCK)
        last = order_ref[s, blocks] - 1

        def score(t, top, found=None):
            which = order_ref[s, t]
            found = jnp.dot(kv_ref[which, :BLOCK, :], qt_ref[s], preferred_element_type=jnp.float32)
            score_ref[t] = found
            return jnp.maximum(top, jnp.max(found.reshape(BLOCK // 8, 8, width), axis=0))

        top = lax.fori_loop(0, last, score, jnp.full((8, width), floor_score, jnp.float32))
        found = jnp.dot(kv_ref[order_ref[s, last], :BLOCK, :], qt_ref[s], preferred_element_type=jnp.float32)
        key_at = lax.broadcasted_iota(jnp.int32, (BLOCK, width), 0)
        query_at = lax.broadcasted_iota(jnp.int32, (BLOCK, width), 1) % BLOCK
        found = jnp.where(query_at >= key_at, found, floor_score)
        score_ref[last] = found
        top = jnp.maximum(top, jnp.max(found.reshape(BLOCK // 8, 8, width), axis=0))
        top = jnp.max(top, axis=0, keepdims=True) * factor
        acc_ref[...] = jnp.zeros_like(acc_ref)

        def mix(t, denom):
            which = order_ref[s, t]
            weights = jnp.exp2(score_ref[t] * factor - top)
            acc_ref[...] += lax.dot_general(
                kv_ref[which, BLOCK:, :],
                weights.astype(jnp.bfloat16),
                (((0,), (0,)), ((), ())),
                preferred_element_type=jnp.float32,
            )
            return denom + jnp.sum(weights.reshape(BLOCK // 8, 8, width), axis=0)

        denom = lax.fori_loop(0, last + 1, mix, jnp.zeros((8, width), jnp.float32))
        final = acc_ref[...] / jnp.sum(denom, axis=0, keepdims=True)
        for h in range(heads):
            at = pl.ds(h * head_size, head_size)
            out_ref[0, rows, at] = final[:, h * BLOCK : (h + 1) * BLOCK].T.astype(out_ref.dtype)


def swap(array, axis, flip):
    size = lax.axis_size(axis)
    return lax.ppermute(array, axis, [(i, i ^ flip) for i in range(size)])


def per_device(queries, keys, values, block_list, block_count):
    head_size = keys.shape[2]
    heads = queries.shape[2] // head_size
    own_blocks = queries.shape[1] // BLOCK
    per = keys.shape[1] // BLOCK
    rows = lax.axis_size("row")
    cols = lax.axis_size("col")
    panels, slots = block_list.shape[2:]
    blocks = panels * slots
    vmem = pl.BlockSpec(memory_space=pltpu.VMEM)
    smem = pl.BlockSpec(memory_space=pltpu.SMEM)
    anywhere = pl.BlockSpec(memory_space=pl.ANY)
    small = pltpu.CompilerParams(vmem_limit_bytes=4 * 1024 * 1024)

    held = pl.pallas_call(
        pack_kernel,
        out_shape=jax.ShapeDtypeStruct((per, 2 * BLOCK, head_size), keys.dtype),
        in_specs=[anywhere, anywhere],
        out_specs=anywhere,
        scratch_shapes=[pltpu.SemaphoreType.DMA((per, 2))],
        compiler_params=pltpu.CompilerParams(vmem_limit_bytes=60 * 1024 * 1024),
        name="pack",
    )(keys, values)
    queries_across, order = pl.pallas_call(
        functools.partial(prepare_kernel, heads),
        out_shape=(
            jax.ShapeDtypeStruct((own_blocks, head_size, heads * BLOCK), queries.dtype),
            jax.ShapeDtypeStruct((own_blocks, blocks + 1), jnp.int32),
        ),
        in_specs=[vmem, anywhere, anywhere],
        out_specs=(vmem, smem),
        scratch_shapes=[
            pltpu.SMEM((own_blocks, panels, slots), jnp.int32),
            pltpu.SMEM((own_blocks, panels), jnp.int32),
            pltpu.SemaphoreType.DMA((2,)),
        ],
        compiler_params=small,
        name="prepare",
    )(queries, block_list, block_count)

    flip = rows // 2
    place = [(0, 0)]
    while flip > 2:
        held = pl.pallas_call(
            join_kernel,
            out_shape=jax.ShapeDtypeStruct((2 * held.shape[0],) + held.shape[1:], held.dtype),
            in_specs=[vmem, vmem],
            out_specs=vmem,
            compiler_params=small,
            name="join",
        )(held, swap(held, "row", flip))
        place += [(r ^ flip, c) for r, c in place]
        flip //= 2
    pieces = [(held, place)]
    while flip:
        if flip == 1:
            last, place = pieces[-1]
            last, queries_across, order = lax.optimization_barrier((last, queries_across, order))
            pieces[-1] = last, place
        pieces += [(swap(held, "row", flip), [(r ^ flip, c) for r, c in place]) for held, place in pieces]
        flip //= 2
    flip = CORES
    while flip < cols:
        pieces += [(swap(held, "col", flip), [(r, c ^ flip) for r, c in place]) for held, place in pieces]
        flip *= 2
    pieces += [(swap(held, "col", 1), [(r, c ^ 1) for r, c in place]) for held, place in pieces]

    held, places = zip(*pieces)
    scratch_bytes = blocks * BLOCK * (heads * BLOCK * 4 + 2 * head_size * 2)
    return pl.pallas_call(
        functools.partial(attend_kernel, heads, places),
        out_shape=jax.ShapeDtypeStruct(queries.shape, jnp.bfloat16),
        in_specs=[vmem, anywhere] + [vmem] * len(held),
        out_specs=vmem,
        scratch_shapes=[
            pltpu.VMEM((blocks, 2 * BLOCK, head_size), jnp.bfloat16),
            pltpu.VMEM((blocks, BLOCK, heads * BLOCK), jnp.float32),
            pltpu.VMEM((head_size, heads * BLOCK), jnp.float32),
            pltpu.SMEM((own_blocks, blocks + 1), jnp.int32),
            pltpu.SemaphoreType.DMA,
        ],
        compiler_params=pltpu.CompilerParams(vmem_limit_bytes=scratch_bytes + 3 * 1024 * 1024),
        name="attend",
    )(queries_across, order, *held)


def solution(mesh):
    placed = (
        P(("groups", "col"), "row", None),
        P(("groups", "row"), "col", None),
        P(("groups", "row"), "col", None),
        P("groups", None, None, None),
        P("groups", None, None),
    )
    return jax.shard_map(
        per_device,
        mesh=mesh,
        in_specs=placed,
        out_specs=P(("groups", "col"), "row", None),
        check_vma=False,
    )
```

```python
import functools
import math

import jax
import jax.numpy as jnp
from jax import lax
from jax.experimental import pallas as pl
from jax.experimental.pallas import tpu as pltpu
from jax.sharding import PartitionSpec as P

BLOCK = 128
CORES = 2

floor_score = -1e30


def pack_kernel(k_hbm, v_hbm, out_ref, v_ref, sems):
    blocks = out_ref.shape[0]
    copies = [pltpu.make_async_copy(v_hbm, v_ref, sems.at[blocks])]
    for s in range(blocks):
        rows = pl.ds(s * BLOCK, BLOCK)
        copies.append(pltpu.make_async_copy(k_hbm.at[0, rows, :], out_ref.at[s, pl.ds(0, BLOCK), :], sems.at[s]))
    for copy in copies:
        copy.start()
    copies[0].wait()
    for s in range(blocks):
        out_ref[s, BLOCK:, :] = v_ref[0, pl.ds(s * BLOCK, BLOCK), :].T
    for copy in copies[1:]:
        copy.wait()


def join_kernel(*refs):
    out_ref = refs[-1]
    first = 0
    for ref in refs[:-1]:
        out_ref[first : first + ref.shape[0]] = ref[...]
        first += ref.shape[0]


def prepare_kernel(heads, q_ref, list_hbm, count_hbm, qt_ref, order_ref, list_ref, count_ref, sems):
    own_blocks, head_size = qt_ref.shape[:2]
    panels, slots = list_ref.shape[1:]
    col_index = lax.axis_index("col")
    first = lax.axis_index("row") * own_blocks
    copies = (
        pltpu.make_async_copy(list_hbm.at[col_index, pl.ds(first, own_blocks)], list_ref, sems.at[0]),
        pltpu.make_async_copy(count_hbm.at[col_index, pl.ds(first, own_blocks)], count_ref, sems.at[1]),
    )
    for copy in copies:
        copy.start()
    for s in range(own_blocks):
        for h in range(heads):
            tile = q_ref[0, pl.ds(s * BLOCK, BLOCK), pl.ds(h * head_size, head_size)]
            qt_ref[s, :, pl.ds(h * BLOCK, BLOCK)] = tile.T
    for copy in copies:
        copy.wait()
    for s in range(own_blocks):

        def put_panel(r, total):
            def put(n, unused):
                order_ref[s, total + n] = r * slots + list_ref[s, r, n]
                return unused

            lax.fori_loop(0, count_ref[s, r], put, 0)
            return total + count_ref[s, r]

        order_ref[s, panels * slots] = lax.fori_loop(0, panels, put_panel, 0)


def attend_kernel(heads, places, qt_ref, order_hbm, *refs):
    pieces = refs[: len(places)]
    out_ref, kv_ref, score_ref, acc_ref, order_ref, sem = refs[len(places) :]
    own_blocks, head_size, width = qt_ref.shape
    col_index = lax.axis_index("col")
    row_index = lax.axis_index("row")
    cols = lax.axis_size("col")
    per = kv_ref.shape[0] // (cols * lax.axis_size("row"))
    blocks = order_ref.shape[1] - 1
    factor = math.log2(math.e) / head_size**0.5

    copy = pltpu.make_async_copy(order_hbm, order_ref, sem)
    copy.start()
    for piece, where in zip(pieces, places):
        for n, (row_flip, col_flip) in enumerate(where):
            first = ((row_index ^ row_flip) * cols + (col_index ^ col_flip)) * per
            for s in range(per):
                kv_ref[first + s] = piece[n * per + s]
    copy.wait()

    for s in range(own_blocks):
        rows = pl.ds(s * BLOCK, BLOCK)
        last = order_ref[s, blocks] - 1

        def score(t, top, found=None):
            which = order_ref[s, t]
            found = jnp.dot(kv_ref[which, :BLOCK, :], qt_ref[s], preferred_element_type=jnp.float32)
            score_ref[t] = found
            return jnp.maximum(top, jnp.max(found.reshape(BLOCK // 8, 8, width), axis=0))

        top = lax.fori_loop(0, last, score, jnp.full((8, width), floor_score, jnp.float32))
        found = jnp.dot(kv_ref[order_ref[s, last], :BLOCK, :], qt_ref[s], preferred_element_type=jnp.float32)
        key_at = lax.broadcasted_iota(jnp.int32, (BLOCK, width), 0)
        query_at = lax.broadcasted_iota(jnp.int32, (BLOCK, width), 1) % BLOCK
        found = jnp.where(query_at >= key_at, found, floor_score)
        score_ref[last] = found
        top = jnp.maximum(top, jnp.max(found.reshape(BLOCK // 8, 8, width), axis=0))
        top = jnp.max(top, axis=0, keepdims=True) * factor
        acc_ref[...] = jnp.zeros_like(acc_ref)

        def mix(t, denom):
            which = order_ref[s, t]
            weights = jnp.exp2(score_ref[t] * factor - top)
            acc_ref[...] += jnp.dot(
                kv_ref[which, BLOCK:, :], weights.astype(jnp.bfloat16), preferred_element_type=jnp.float32
            )
            return denom + jnp.sum(weights.reshape(BLOCK // 8, 8, width), axis=0)

        denom = lax.fori_loop(0, last + 1, mix, jnp.zeros((8, width), jnp.float32))
        final = acc_ref[...] / jnp.sum(denom, axis=0, keepdims=True)
        for h in range(heads):
            at = pl.ds(h * head_size, head_size)
            out_ref[0, rows, at] = final[:, h * BLOCK : (h + 1) * BLOCK].T.astype(out_ref.dtype)


def swap(piece, axis, flip):
    array, places = piece
    came = lax.ppermute(array, axis, [(i, i ^ flip) for i in range(lax.axis_size(axis))])
    if axis == "row":
        return came, [(r ^ flip, c) for r, c in places]
    return came, [(r, c ^ flip) for r, c in places]


def join_pieces(pieces):
    vmem = pl.BlockSpec(memory_space=pltpu.VMEM)
    first = pieces[0][0]
    blocks = sum(array.shape[0] for array, _ in pieces)
    array = pl.pallas_call(
        join_kernel,
        out_shape=jax.ShapeDtypeStruct((blocks,) + first.shape[1:], first.dtype),
        in_specs=[vmem] * len(pieces),
        out_specs=vmem,
        compiler_params=pltpu.CompilerParams(vmem_limit_bytes=4 * 1024 * 1024),
        name="join",
    )(*(array for array, _ in pieces))
    return array, [place for _, places in pieces for place in places]


def across(piece, cols):
    pieces = [piece]
    flip = CORES
    while flip < cols:
        pieces += [swap(one, "col", flip) for one in pieces]
        flip *= 2
    return pieces[1:]


def per_device(queries, keys, values, block_list, block_count):
    head_size = keys.shape[2]
    heads = queries.shape[2] // head_size
    own_blocks = queries.shape[1] // BLOCK
    per = keys.shape[1] // BLOCK
    rows = lax.axis_size("row")
    cols = lax.axis_size("col")
    panels, slots = block_list.shape[2:]
    blocks = panels * slots
    vmem = pl.BlockSpec(memory_space=pltpu.VMEM)
    smem = pl.BlockSpec(memory_space=pltpu.SMEM)
    anywhere = pl.BlockSpec(memory_space=pl.ANY)
    small = pltpu.CompilerParams(vmem_limit_bytes=4 * 1024 * 1024)

    packed = pl.pallas_call(
        pack_kernel,
        out_shape=jax.ShapeDtypeStruct((per, 2 * BLOCK, head_size), keys.dtype),
        in_specs=[anywhere, anywhere],
        out_specs=vmem,
        scratch_shapes=[pltpu.VMEM(values.shape, values.dtype), pltpu.SemaphoreType.DMA((per + 1,))],
        compiler_params=pltpu.CompilerParams(vmem_limit_bytes=60 * 1024 * 1024),
        name="pack",
    )(keys, values)

    own = (packed, [(0, 0)])
    flip = rows // 2
    while flip > 2:
        own = join_pieces([own, swap(own, "row", flip)])
        flip //= 2
    far = swap(own, "row", 2)
    near = swap(own, "row", 1)
    early = [own, near, far, *across(own, cols)]
    arrived = lax.optimization_barrier([array for array, _ in early[1:]])
    early[1:] = [(array, places) for array, (_, places) in zip(arrived, early[1:])]
    near, far = early[1:3]
    queries_across, order = pl.pallas_call(
        functools.partial(prepare_kernel, heads),
        out_shape=(
            jax.ShapeDtypeStruct((own_blocks, head_size, heads * BLOCK), queries.dtype),
            jax.ShapeDtypeStruct((own_blocks, blocks + 1), jnp.int32),
        ),
        in_specs=[vmem, anywhere, anywhere],
        out_specs=(vmem, smem),
        scratch_shapes=[
            pltpu.SMEM((own_blocks, panels, slots), jnp.int32),
            pltpu.SMEM((own_blocks, panels), jnp.int32),
            pltpu.SemaphoreType.DMA((2,)),
        ],
        compiler_params=small,
        name="prepare",
    )(queries, block_list, block_count)
    first = join_pieces(early)
    last = swap(far, "row", 1)
    second_hops = across(near, cols)
    arrived = lax.optimization_barrier([last[0]] + [array for array, _ in second_hops])
    last = (arrived[0], last[1])
    second_hops = [(array, places) for array, (_, places) in zip(arrived[1:], second_hops)]
    late = [last, *second_hops, *across(far, cols), *across(last, cols)]
    arrived, queries_across, order = lax.optimization_barrier((late[-1][0], queries_across, order))
    late[-1] = (arrived, late[-1][1])
    second = join_pieces(late)
    pieces = [first, second]
    pieces += [swap(piece, "col", 1) for piece in pieces]

    held, places = zip(*pieces)
    scratch_bytes = blocks * BLOCK * (heads * BLOCK * 4 + 2 * head_size * 2)
    return pl.pallas_call(
        functools.partial(attend_kernel, heads, places),
        out_shape=jax.ShapeDtypeStruct(queries.shape, jnp.bfloat16),
        in_specs=[vmem, anywhere] + [vmem] * len(held),
        out_specs=vmem,
        scratch_shapes=[
            pltpu.VMEM((blocks, 2 * BLOCK, head_size), jnp.bfloat16),
            pltpu.VMEM((blocks, BLOCK, heads * BLOCK), jnp.float32),
            pltpu.VMEM((head_size, heads * BLOCK), jnp.float32),
            pltpu.SMEM((own_blocks, blocks + 1), jnp.int32),
            pltpu.SemaphoreType.DMA,
        ],
        compiler_params=pltpu.CompilerParams(vmem_limit_bytes=scratch_bytes + 3 * 1024 * 1024),
        name="attend",
    )(queries_across, order, *held)


def solution(mesh):
    placed = (
        P(("groups", "col"), "row", None),
        P(("groups", "row"), "col", None),
        P(("groups", "row"), "col", None),
        P("groups", None, None, None),
        P("groups", None, None),
    )
    return jax.shard_map(
        per_device,
        mesh=mesh,
        in_specs=placed,
        out_specs=P(("groups", "col"), "row", None),
        check_vma=False,
    )
```

```python
import functools
import math

import jax
import jax.numpy as jnp
from jax import lax
from jax.experimental import pallas as pl
from jax.experimental.pallas import tpu as pltpu
from jax.sharding import PartitionSpec as P

BLOCK = 128
CORES = 2

floor_score = -1e30


def pack_kernel(k_hbm, v_hbm, out_ref, v_ref, sems):
    blocks = out_ref.shape[0]
    copies = [pltpu.make_async_copy(v_hbm, v_ref, sems.at[blocks])]
    for s in range(blocks):
        rows = pl.ds(s * BLOCK, BLOCK)
        copies.append(pltpu.make_async_copy(k_hbm.at[0, rows, :], out_ref.at[s, pl.ds(0, BLOCK), :], sems.at[s]))
    for copy in copies:
        copy.start()
    copies[0].wait()
    for s in range(blocks):
        out_ref[s, BLOCK:, :] = v_ref[0, pl.ds(s * BLOCK, BLOCK), :].T
    for copy in copies[1:]:
        copy.wait()


def join_kernel(*refs):
    out_ref = refs[-1]
    first = 0
    for ref in refs[:-1]:
        out_ref[first : first + ref.shape[0]] = ref[...]
        first += ref.shape[0]


def prepare_kernel(heads, per, places, q_ref, list_hbm, count_hbm, qt_ref, order_ref,
                   active_ref, list_ref, count_ref, sems):
    own_blocks, head_size = qt_ref.shape[:2]
    panels, slots = list_ref.shape[1:]
    end = order_ref.shape[2] - 2
    cols = lax.axis_size("col")
    col_index = lax.axis_index("col")
    row_index = lax.axis_index("row")
    first = row_index * own_blocks
    copies = (
        pltpu.make_async_copy(list_hbm.at[col_index, pl.ds(first, own_blocks)], list_ref, sems.at[0]),
        pltpu.make_async_copy(count_hbm.at[col_index, pl.ds(first, own_blocks)], count_ref, sems.at[1]),
    )
    for copy in copies:
        copy.start()
    for s in range(own_blocks):
        for h in range(heads):
            tile = q_ref[0, pl.ds(s * BLOCK, BLOCK), pl.ds(h * head_size, head_size)]
            qt_ref[s, :, pl.ds(h * BLOCK, BLOCK)] = tile.T
    for copy in copies:
        copy.wait()
    for s in range(own_blocks):
        diagonal = col_index * list_hbm.shape[1] + first + s
        for r in range(panels):
            for n in range(slots):
                active_ref[r * slots + n] = 0
            for n in reversed(range(slots)):
                active_ref[r * slots + list_ref[s, r, n]] = (n < count_ref[s, r]).astype(jnp.int32)
        for piece, where in enumerate(places):
            total = jnp.int32(0)
            diagonal_slot = jnp.int32(-1)
            for n, (row_flip, col_flip) in enumerate(where):
                for k in range(per):
                    block = ((row_index ^ row_flip) * cols + (col_index ^ col_flip)) * per + k
                    order_ref[s, piece, total] = n * per + k
                    on_diagonal = block == diagonal
                    diagonal_slot = jnp.where(on_diagonal, n * per + k, diagonal_slot)
                    total = total + jnp.where(on_diagonal, 0, active_ref[block])
            order_ref[s, piece, total] = diagonal_slot
            order_ref[s, piece, end] = total
            order_ref[s, piece, end + 1] = total + (diagonal_slot >= 0).astype(jnp.int32)


def partial_attention(s, first_piece, pieces, order_ref, qt_ref, score_ref, acc_ref):
    head_size, width = qt_ref.shape[1:]
    end = order_ref.shape[2] - 2
    factor = math.log2(math.e) / head_size**0.5
    top = jnp.full((8, width), floor_score, jnp.float32)
    at = jnp.int32(0)
    starts = []
    for n, piece in enumerate(pieces):
        starts.append(at)

        def score(t, top, n=n, piece=piece, at=at, masked=False):
            slot = order_ref[s, first_piece + n, t]
            found = jnp.dot(piece[slot, :BLOCK, :], qt_ref[s], preferred_element_type=jnp.float32)
            if masked:
                key_at = lax.broadcasted_iota(jnp.int32, (BLOCK, width), 0)
                query_at = lax.broadcasted_iota(jnp.int32, (BLOCK, width), 1) % BLOCK
                found = jnp.where(query_at >= key_at, found, floor_score)
            score_ref[at + t] = found
            return jnp.maximum(top, jnp.max(found.reshape(BLOCK // 8, 8, width), axis=0))

        plain = order_ref[s, first_piece + n, end]
        total = order_ref[s, first_piece + n, end + 1]
        top = lax.fori_loop(0, plain, score, top)
        top = lax.fori_loop(plain, total, functools.partial(score, masked=True), top)
        at = at + total
    top = jnp.max(top, axis=0, keepdims=True) * factor
    acc_ref[...] = jnp.zeros_like(acc_ref)
    denom = jnp.zeros((8, width), jnp.float32)
    for n, piece in enumerate(pieces):

        def mix(t, denom, n=n, piece=piece, at=starts[n]):
            slot = order_ref[s, first_piece + n, t]
            weights = jnp.exp2(score_ref[at + t] * factor - top)
            acc_ref[...] += jnp.dot(
                piece[slot, BLOCK:, :], weights.astype(jnp.bfloat16), preferred_element_type=jnp.float32
            )
            return denom + jnp.sum(weights.reshape(BLOCK // 8, 8, width), axis=0)

        denom = lax.fori_loop(0, order_ref[s, first_piece + n, end + 1], mix, denom)
    return top, jnp.sum(denom, axis=0, keepdims=True)


def early_kernel(qt_ref, order_hbm, *refs):
    acc_out, stats_out, score_ref, order_ref, sem = refs[-5:]
    pieces = refs[:-5]
    copy = pltpu.make_async_copy(order_hbm, order_ref, sem)
    copy.start()
    copy.wait()
    for s in range(qt_ref.shape[0]):
        top, denom = partial_attention(s, 0, pieces, order_ref, qt_ref, score_ref, acc_out.at[s])
        stats_out[s, 0:1] = top
        stats_out[s, 1:2] = denom


def late_kernel(heads, first_piece, qt_ref, order_hbm, acc_in, stats_in, *refs):
    out_ref, score_ref, acc_ref, order_ref, sem = refs[-5:]
    pieces = refs[:-5]
    head_size = qt_ref.shape[1]
    copy = pltpu.make_async_copy(order_hbm, order_ref, sem)
    copy.start()
    copy.wait()
    for s in range(qt_ref.shape[0]):
        rows = pl.ds(s * BLOCK, BLOCK)
        top, denom = partial_attention(s, first_piece, pieces, order_ref, qt_ref, score_ref, acc_ref)
        other_top, other_denom = stats_in[s, 0:1], stats_in[s, 1:2]
        overall = jnp.maximum(top, other_top)
        mine, other = jnp.exp2(top - overall), jnp.exp2(other_top - overall)
        share = 1.0 / (mine * denom + other * other_denom)
        final = acc_ref[...] * (mine * share) + acc_in[s] * (other * share)
        for h in range(heads):
            at = pl.ds(h * head_size, head_size)
            out_ref[0, rows, at] = final[:, h * BLOCK : (h + 1) * BLOCK].T.astype(out_ref.dtype)


def swap(piece, axis, flip):
    array, places = piece
    came = lax.ppermute(array, axis, [(i, i ^ flip) for i in range(lax.axis_size(axis))])
    if axis == "row":
        return came, [(r ^ flip, c) for r, c in places]
    return came, [(r, c ^ flip) for r, c in places]


def join_pieces(pieces):
    vmem = pl.BlockSpec(memory_space=pltpu.VMEM)
    first = pieces[0][0]
    blocks = sum(array.shape[0] for array, _ in pieces)
    array = pl.pallas_call(
        join_kernel,
        out_shape=jax.ShapeDtypeStruct((blocks,) + first.shape[1:], first.dtype),
        in_specs=[vmem] * len(pieces),
        out_specs=vmem,
        compiler_params=pltpu.CompilerParams(vmem_limit_bytes=4 * 1024 * 1024),
        name="join",
    )(*(array for array, _ in pieces))
    return array, [place for _, places in pieces for place in places]


def together(pieces, *others):
    arrays = lax.optimization_barrier([array for array, _ in pieces] + list(others))
    held = [(array, places) for array, (_, places) in zip(arrays, pieces)]
    return (held, *arrays[len(held) :]) if others else held


def across(piece, cols):
    pieces = [piece]
    flip = CORES
    while flip < cols:
        pieces += [swap(one, "col", flip) for one in pieces]
        flip *= 2
    return pieces[1:]


def per_device(queries, keys, values, block_list, block_count):
    head_size = keys.shape[2]
    heads = queries.shape[2] // head_size
    own_blocks = queries.shape[1] // BLOCK
    per = keys.shape[1] // BLOCK
    rows = lax.axis_size("row")
    cols = lax.axis_size("col")
    panels, slots = block_list.shape[2:]
    blocks = panels * slots
    vmem = pl.BlockSpec(memory_space=pltpu.VMEM)
    smem = pl.BlockSpec(memory_space=pltpu.SMEM)
    anywhere = pl.BlockSpec(memory_space=pl.ANY)
    small = pltpu.CompilerParams(vmem_limit_bytes=4 * 1024 * 1024)

    packed = pl.pallas_call(
        pack_kernel,
        out_shape=jax.ShapeDtypeStruct((per, 2 * BLOCK, head_size), keys.dtype),
        in_specs=[anywhere, anywhere],
        out_specs=vmem,
        scratch_shapes=[pltpu.VMEM(values.shape, values.dtype), pltpu.SemaphoreType.DMA((per + 1,))],
        compiler_params=pltpu.CompilerParams(vmem_limit_bytes=60 * 1024 * 1024),
        name="pack",
    )(keys, values)

    own = (packed, [(0, 0)])
    flip = rows // 2
    while flip > 2:
        own = join_pieces([own, swap(own, "row", flip)])
        flip //= 2
    near, far, opposite = (swap(own, "row", flip) for flip in (1, 2, 3))
    own_across = across(own, cols)
    near, *own_across = together([near, *own_across])
    near_across = across(near, cols)
    early_places = [place for _, where in (own, near, far, opposite, *own_across) for place in where]
    late_places = [
        (r, c ^ flip)
        for where in (near[1], far[1] + opposite[1])
        for flip in range(CORES, cols, CORES)
        for r, c in where
    ]
    places = [part for where in (early_places, late_places) for part in (where, [(r, c ^ 1) for r, c in where])]

    longest = max(len(where) for where in places) * per
    queries_across, order = pl.pallas_call(
        functools.partial(prepare_kernel, heads, per, places),
        out_shape=(
            jax.ShapeDtypeStruct((own_blocks, head_size, heads * BLOCK), queries.dtype),
            jax.ShapeDtypeStruct((own_blocks, len(places), longest + 3), jnp.int32),
        ),
        in_specs=[vmem, anywhere, anywhere],
        out_specs=(vmem, smem),
        scratch_shapes=[
            pltpu.SMEM((blocks,), jnp.int32),
            pltpu.SMEM((own_blocks, panels, slots), jnp.int32),
            pltpu.SMEM((own_blocks, panels), jnp.int32),
            pltpu.SemaphoreType.DMA((2,)),
        ],
        compiler_params=small,
        name="prepare",
    )(queries, block_list, block_count)
    (far, opposite, *near_across), queries_across, order = together([far, opposite, *near_across], queries_across, order)
    rest = join_pieces([far, opposite])
    early = join_pieces([own, near, rest, *own_across])

    width = heads * BLOCK
    scratch = [pltpu.VMEM((2 * longest, BLOCK, width), jnp.float32)]
    order_scratch = [pltpu.SMEM(order.shape, jnp.int32), pltpu.SemaphoreType.DMA]
    limit = pltpu.CompilerParams(vmem_limit_bytes=2 * longest * BLOCK * width * 4 + 4 * 1024 * 1024)
    acc, stats = pl.pallas_call(
        early_kernel,
        out_shape=(
            jax.ShapeDtypeStruct((own_blocks, head_size, width), jnp.float32),
            jax.ShapeDtypeStruct((own_blocks, 2, width), jnp.float32),
        ),
        in_specs=[vmem, anywhere, vmem, vmem],
        out_specs=(vmem, vmem),
        scratch_shapes=scratch + order_scratch,
        compiler_params=limit,
        cost_estimate=pl.CostEstimate(flops=10**9, bytes_accessed=2**21, transcendentals=2**20),
        name="early",
    )(queries_across, order, early[0], swap(early, "col", 1)[0])
    late, acc = together(near_across + across(rest, cols), acc)
    late = join_pieces(late)
    return pl.pallas_call(
        functools.partial(late_kernel, heads, 2),
        out_shape=jax.ShapeDtypeStruct(queries.shape, jnp.bfloat16),
        in_specs=[vmem, anywhere, vmem, vmem, vmem, vmem],
        out_specs=vmem,
        scratch_shapes=scratch + [pltpu.VMEM((head_size, width), jnp.float32)] + order_scratch,
        compiler_params=limit,
        name="late",
    )(queries_across, order, acc, stats, late[0], swap(late, "col", 1)[0])


def solution(mesh):
    placed = (
        P(("groups", "col"), "row", None),
        P(("groups", "row"), "col", None),
        P(("groups", "row"), "col", None),
        P("groups", None, None, None),
        P("groups", None, None),
    )
    return jax.shard_map(
        per_device,
        mesh=mesh,
        in_specs=placed,
        out_specs=P(("groups", "col"), "row", None),
        check_vma=False,
    )
```

```python
import functools
import math

import jax
import jax.numpy as jnp
from jax import lax
from jax.experimental import pallas as pl
from jax.experimental.pallas import tpu as pltpu
from jax.sharding import PartitionSpec as P

BLOCK = 128
CORES = 2

floor_score = -1e30


def join_kernel(transpose, *refs):
    out_ref = refs[-1]
    first = 0
    for ref in refs[:-1]:
        if not transpose:
            out_ref[first : first + ref.shape[0]] = ref[...]
        for n in range(ref.shape[0] if transpose else 0):
            out_ref[first + n, :BLOCK, :] = ref[n, :BLOCK, :]
            out_ref[first + n, BLOCK:, :] = ref[n, BLOCK:, :].T
        first += ref.shape[0]


def prepare_kernel(heads, per, places, q_ref, list_hbm, count_hbm, qt_ref, order_ref,
                   active_ref, list_ref, count_ref, sems):
    own_blocks, head_size = qt_ref.shape[:2]
    panels, slots = list_ref.shape[1:]
    end = order_ref.shape[2] - 2
    cols = lax.axis_size("col")
    col_index = lax.axis_index("col")
    row_index = lax.axis_index("row")
    first = row_index * own_blocks
    copies = (
        pltpu.make_async_copy(list_hbm.at[col_index, pl.ds(first, own_blocks)], list_ref, sems.at[0]),
        pltpu.make_async_copy(count_hbm.at[col_index, pl.ds(first, own_blocks)], count_ref, sems.at[1]),
    )
    for copy in copies:
        copy.start()
    for s in range(own_blocks):
        for h in range(heads):
            tile = q_ref[0, pl.ds(s * BLOCK, BLOCK), pl.ds(h * head_size, head_size)]
            qt_ref[s, :, pl.ds(h * BLOCK, BLOCK)] = tile.T
    for copy in copies:
        copy.wait()
    for s in range(own_blocks):
        diagonal = col_index * list_hbm.shape[1] + first + s
        for r in range(panels):
            for n in range(slots):
                active_ref[r * slots + n] = 0
            for n in reversed(range(slots)):
                active_ref[r * slots + list_ref[s, r, n]] = (n < count_ref[s, r]).astype(jnp.int32)
        for piece, where in enumerate(places):
            total = jnp.int32(0)
            diagonal_slot = jnp.int32(-1)
            for n, (row_flip, col_flip) in enumerate(where):
                for k in range(per):
                    block = ((row_index ^ row_flip) * cols + (col_index ^ col_flip)) * per + k
                    order_ref[s, piece, total] = n * per + k
                    on_diagonal = block == diagonal
                    diagonal_slot = jnp.where(on_diagonal, n * per + k, diagonal_slot)
                    total = total + jnp.where(on_diagonal, 0, active_ref[block])
            order_ref[s, piece, total] = diagonal_slot
            order_ref[s, piece, end] = total
            order_ref[s, piece, end + 1] = total + (diagonal_slot >= 0).astype(jnp.int32)


def partial_attention(s, first_piece, pieces, order_ref, qt_ref, score_ref, acc_ref):
    head_size, width = qt_ref.shape[1:]
    end = order_ref.shape[2] - 2
    factor = math.log2(math.e) / head_size**0.5
    top = jnp.full((8, width), floor_score, jnp.float32)
    at = jnp.int32(0)
    starts = []
    for n, piece in enumerate(pieces):
        starts.append(at)

        def score(t, top, n=n, piece=piece, at=at, masked=False):
            slot = order_ref[s, first_piece + n, t]
            found = jnp.dot(piece[slot, :BLOCK, :], qt_ref[s], preferred_element_type=jnp.float32)
            if masked:
                key_at = lax.broadcasted_iota(jnp.int32, (BLOCK, width), 0)
                query_at = lax.broadcasted_iota(jnp.int32, (BLOCK, width), 1) % BLOCK
                found = jnp.where(query_at >= key_at, found, floor_score)
            score_ref[at + t] = found
            return jnp.maximum(top, jnp.max(found.reshape(BLOCK // 8, 8, width), axis=0))

        plain = order_ref[s, first_piece + n, end]
        total = order_ref[s, first_piece + n, end + 1]
        top = lax.fori_loop(0, plain, score, top)
        top = lax.fori_loop(plain, total, functools.partial(score, masked=True), top)
        at = at + total
    top = jnp.max(top, axis=0, keepdims=True) * factor
    acc_ref[...] = jnp.zeros_like(acc_ref)
    denom = jnp.zeros((8, width), jnp.float32)
    for n, piece in enumerate(pieces):

        def mix(t, denom, n=n, piece=piece, at=starts[n]):
            slot = order_ref[s, first_piece + n, t]
            weights = jnp.exp2(score_ref[at + t] * factor - top)
            acc_ref[...] += jnp.dot(
                piece[slot, BLOCK:, :], weights.astype(jnp.bfloat16), preferred_element_type=jnp.float32
            )
            return denom + jnp.sum(weights.reshape(BLOCK // 8, 8, width), axis=0)

        denom = lax.fori_loop(0, order_ref[s, first_piece + n, end + 1], mix, denom)
    return top, jnp.sum(denom, axis=0, keepdims=True)


def attend_kernel(heads, first_piece, merges, ends, qt_ref, order_hbm, *refs):
    score_ref, acc_ref, order_ref, sem = refs[-4:]
    outs = refs[-5:-4] if ends else refs[-6:-4]
    ins = refs[: -4 - len(outs)]
    pieces = ins[2:] if merges else ins
    head_size = qt_ref.shape[1]
    copy = pltpu.make_async_copy(order_hbm, order_ref, sem)
    copy.start()
    copy.wait()
    for s in range(qt_ref.shape[0]):
        top, denom = partial_attention(s, first_piece, pieces, order_ref, qt_ref, score_ref, acc_ref)
        scale = other_scale = 1.0
        if merges:
            acc_in, stats_in = ins[:2]
            other_top, other_denom = stats_in[s, 0:1], stats_in[s, 1:2]
            overall = jnp.maximum(top, other_top)
            scale, other_scale = jnp.exp2(top - overall), jnp.exp2(other_top - overall)
            denom = scale * denom + other_scale * other_denom
            top = overall
        if ends:
            share = 1.0 / denom
            scale, other_scale = scale * share, other_scale * share
        acc = acc_ref[...] * scale
        if merges:
            acc = acc + acc_in[s] * other_scale
        if ends:
            rows = pl.ds(s * BLOCK, BLOCK)
            for h in range(heads):
                at = pl.ds(h * head_size, head_size)
                outs[0][0, rows, at] = acc[:, h * BLOCK : (h + 1) * BLOCK].T.astype(outs[0].dtype)
        else:
            outs[0][s] = acc
            outs[1][s, 0:1] = top
            outs[1][s, 1:2] = denom


def swap(piece, axis, flip):
    array, places = piece
    came = lax.ppermute(array, axis, [(i, i ^ flip) for i in range(lax.axis_size(axis))])
    if axis == "row":
        return came, [(r ^ flip, c) for r, c in places]
    return came, [(r, c ^ flip) for r, c in places]


def join_pieces(pieces, transpose=True):
    vmem = pl.BlockSpec(memory_space=pltpu.VMEM)
    first = pieces[0][0]
    blocks = sum(array.shape[0] for array, _ in pieces)
    array = pl.pallas_call(
        functools.partial(join_kernel, transpose),
        out_shape=jax.ShapeDtypeStruct((blocks,) + first.shape[1:], first.dtype),
        in_specs=[vmem] * len(pieces),
        out_specs=vmem,
        compiler_params=pltpu.CompilerParams(vmem_limit_bytes=4 * 1024 * 1024),
        name="join",
    )(*(array for array, _ in pieces))
    return array, [place for _, places in pieces for place in places]


def together(pieces, *others):
    arrays = lax.optimization_barrier([array for array, _ in pieces] + list(others))
    held = [(array, places) for array, (_, places) in zip(arrays, pieces)]
    return (held, *arrays[len(held) :]) if others else held


def across(piece, cols):
    pieces = [piece]
    flip = CORES
    while flip < cols:
        pieces += [swap(one, "col", flip) for one in pieces]
        flip *= 2
    return pieces[1:]


def per_device(queries, keys, values, block_list, block_count):
    head_size = keys.shape[2]
    heads = queries.shape[2] // head_size
    own_blocks = queries.shape[1] // BLOCK
    per = keys.shape[1] // BLOCK
    rows = lax.axis_size("row")
    cols = lax.axis_size("col")
    panels, slots = block_list.shape[2:]
    blocks = panels * slots
    vmem = pl.BlockSpec(memory_space=pltpu.VMEM)
    smem = pl.BlockSpec(memory_space=pltpu.SMEM)
    anywhere = pl.BlockSpec(memory_space=pl.ANY)
    small = pltpu.CompilerParams(vmem_limit_bytes=4 * 1024 * 1024)

    shape = (per, BLOCK, head_size)
    packed = jnp.concatenate([keys.reshape(shape), values.reshape(shape)], axis=1)

    own = (packed, [(0, 0)])
    flip = rows // 2
    while flip > 2:
        came = swap(own, "row", flip)
        own = jnp.concatenate([own[0], came[0]]), own[1] + came[1]
        flip //= 2
    near, far, opposite = (swap(own, "row", flip) for flip in (1, 2, 3))
    own_across = across(own, cols)
    near, *own_across = together([near, *own_across])
    near_across = across(near, cols)
    early = join_pieces([own, near, *own_across])
    early_pair = swap(early, "col", 1)
    late_places = [place for _, where in (far, opposite, *near_across) for place in where]
    last_places = [(r, c ^ flip) for flip in range(CORES, cols, CORES) for r, c in far[1] + opposite[1]]
    places = [part for where in (early[1], late_places, last_places) for part in (where, [(r, c ^ 1) for r, c in where])]

    longest = max(len(where) for where in places) * per
    queries_across, order = pl.pallas_call(
        functools.partial(prepare_kernel, heads, per, places),
        out_shape=(
            jax.ShapeDtypeStruct((own_blocks, head_size, heads * BLOCK), queries.dtype),
            jax.ShapeDtypeStruct((own_blocks, len(places), longest + 3), jnp.int32),
        ),
        in_specs=[vmem, anywhere, anywhere],
        out_specs=(vmem, smem),
        scratch_shapes=[
            pltpu.SMEM((blocks,), jnp.int32),
            pltpu.SMEM((own_blocks, panels, slots), jnp.int32),
            pltpu.SMEM((own_blocks, panels), jnp.int32),
            pltpu.SemaphoreType.DMA((2,)),
        ],
        compiler_params=small,
        name="prepare",
    )(queries, block_list, block_count)
    (far, opposite, *near_across), queries_across, order = together([far, opposite, *near_across], queries_across, order)
    rest = join_pieces([far, opposite], False)
    last = across(rest, cols)
    late = join_pieces([far, opposite, *near_across])
    late_pair = swap(late, "col", 1)

    width = heads * BLOCK
    held = 2 * max(len(early[1]), len(late_places), len(last_places)) * per

    def attend(name, first_piece, pieces, part=(), ends=False):
        whole = jax.ShapeDtypeStruct(queries.shape, jnp.bfloat16)
        parts = (
            jax.ShapeDtypeStruct((own_blocks, head_size, width), jnp.float32),
            jax.ShapeDtypeStruct((own_blocks, 2, width), jnp.float32),
        )
        return pl.pallas_call(
            functools.partial(attend_kernel, heads, first_piece, bool(part), ends),
            out_shape=whole if ends else parts,
            in_specs=[vmem, anywhere] + [vmem] * (len(part) + len(pieces)),
            out_specs=vmem if ends else (vmem, vmem),
            scratch_shapes=[
                pltpu.VMEM((held, BLOCK, width), jnp.float32),
                pltpu.VMEM((head_size, width), jnp.float32),
                pltpu.SMEM(order.shape, jnp.int32),
                pltpu.SemaphoreType.DMA,
            ],
            compiler_params=pltpu.CompilerParams(vmem_limit_bytes=held * BLOCK * width * 4 + 4 * 1024 * 1024),
            name=name,
        )(queries_across, order, *part, *(array for array, _ in pieces))

    part = attend("early", 0, [early, early_pair])
    part = attend("late", 2, [late, late_pair], part)
    last, *part = together(last, *part)
    last = join_pieces(last)
    return attend("last", 4, [last, swap(last, "col", 1)], part, ends=True)


def solution(mesh):
    placed = (
        P(("groups", "col"), "row", None),
        P(("groups", "row"), "col", None),
        P(("groups", "row"), "col", None),
        P("groups", None, None, None),
        P("groups", None, None),
    )
    return jax.shard_map(
        per_device,
        mesh=mesh,
        in_specs=placed,
        out_specs=P(("groups", "col"), "row", None),
        check_vma=False,
    )
```

```python
import functools
import math

import jax
import jax.numpy as jnp
from jax import lax
from jax.experimental import pallas as pl
from jax.experimental.pallas import tpu as pltpu
from jax.sharding import PartitionSpec as P

BLOCK = 128
CORES = 2

floor_score = -1e30


def join_kernel(transpose, *refs):
    out_ref = refs[-1]
    first = 0
    for ref in refs[:-1]:
        if not transpose:
            out_ref[first : first + ref.shape[0]] = ref[...]
        for n in range(ref.shape[0] if transpose else 0):
            out_ref[first + n, :BLOCK, :] = ref[n, :BLOCK, :]
            out_ref[first + n, BLOCK:, :] = ref[n, BLOCK:, :].T
        first += ref.shape[0]


def prepare_kernel(heads, per, places, q_ref, list_hbm, count_hbm, qt_ref, order_ref,
                   active_ref, list_ref, count_ref, sems):
    own_blocks, head_size = qt_ref.shape[:2]
    panels, slots = list_ref.shape[1:]
    end = order_ref.shape[2] - 2
    cols = lax.axis_size("col")
    col_index = lax.axis_index("col")
    row_index = lax.axis_index("row")
    first = row_index * own_blocks
    copies = (
        pltpu.make_async_copy(list_hbm.at[col_index, pl.ds(first, own_blocks)], list_ref, sems.at[0]),
        pltpu.make_async_copy(count_hbm.at[col_index, pl.ds(first, own_blocks)], count_ref, sems.at[1]),
    )
    for copy in copies:
        copy.start()
    for s in range(own_blocks):
        for h in range(heads):
            tile = q_ref[0, pl.ds(s * BLOCK, BLOCK), pl.ds(h * head_size, head_size)]
            qt_ref[s, :, pl.ds(h * BLOCK, BLOCK)] = tile.T
    for copy in copies:
        copy.wait()
    for s in range(own_blocks):
        diagonal = col_index * list_hbm.shape[1] + first + s
        for r in range(panels):
            for n in range(slots):
                active_ref[r * slots + n] = 0
            for n in reversed(range(slots)):
                active_ref[r * slots + list_ref[s, r, n]] = (n < count_ref[s, r]).astype(jnp.int32)
        for piece, where in enumerate(places):
            total = jnp.int32(0)
            diagonal_slot = jnp.int32(-1)
            for n, (row_flip, col_flip) in enumerate(where):
                for k in range(per):
                    block = ((row_index ^ row_flip) * cols + (col_index ^ col_flip)) * per + k
                    order_ref[s, piece, total] = n * per + k
                    on_diagonal = block == diagonal
                    diagonal_slot = jnp.where(on_diagonal, n * per + k, diagonal_slot)
                    total = total + jnp.where(on_diagonal, 0, active_ref[block])
            order_ref[s, piece, total] = diagonal_slot
            order_ref[s, piece, end] = total
            order_ref[s, piece, end + 1] = total + (diagonal_slot >= 0).astype(jnp.int32)


def partial_attention(s, first_piece, pieces, order_ref, qt_ref, score_ref, acc_ref):
    head_size, width = qt_ref.shape[1:]
    end = order_ref.shape[2] - 2
    factor = math.log2(math.e) / head_size**0.5
    top = jnp.full((8, width), floor_score, jnp.float32)
    at = jnp.int32(0)
    starts = []
    for n, piece in enumerate(pieces):
        starts.append(at)

        def score(t, top, n=n, piece=piece, at=at, masked=False):
            slot = order_ref[s, first_piece + n, t]
            found = jnp.dot(piece[slot, :BLOCK, :], qt_ref[s], preferred_element_type=jnp.float32)
            if masked:
                key_at = lax.broadcasted_iota(jnp.int32, (BLOCK, width), 0)
                query_at = lax.broadcasted_iota(jnp.int32, (BLOCK, width), 1) % BLOCK
                found = jnp.where(query_at >= key_at, found, floor_score)
            score_ref[at + t] = found
            return jnp.maximum(top, jnp.max(found.reshape(BLOCK // 8, 8, width), axis=0))

        plain = order_ref[s, first_piece + n, end]
        total = order_ref[s, first_piece + n, end + 1]
        top = lax.fori_loop(0, plain, score, top)
        top = lax.fori_loop(plain, total, functools.partial(score, masked=True), top)
        at = at + total
    top = jnp.max(top, axis=0, keepdims=True) * factor
    acc_ref[...] = jnp.zeros_like(acc_ref)
    denom = jnp.zeros((8, width), jnp.float32)
    for n, piece in enumerate(pieces):

        def mix(t, denom, n=n, piece=piece, at=starts[n]):
            slot = order_ref[s, first_piece + n, t]
            weights = jnp.exp2(score_ref[at + t] * factor - top)
            acc_ref[...] += jnp.dot(
                piece[slot, BLOCK:, :], weights.astype(jnp.bfloat16), preferred_element_type=jnp.float32
            )
            return denom + jnp.sum(weights.reshape(BLOCK // 8, 8, width), axis=0)

        denom = lax.fori_loop(0, order_ref[s, first_piece + n, end + 1], mix, denom)
    return top, jnp.sum(denom, axis=0, keepdims=True)


def attend_kernel(heads, first_piece, merges, ends, qt_ref, order_hbm, *refs):
    score_ref, acc_ref, order_ref, sem = refs[-4:]
    outs = refs[-5:-4] if ends else refs[-6:-4]
    ins = refs[: -4 - len(outs)]
    pieces = ins[2:] if merges else ins
    head_size = qt_ref.shape[1]
    copy = pltpu.make_async_copy(order_hbm, order_ref, sem)
    copy.start()
    copy.wait()
    for s in range(qt_ref.shape[0]):
        top, denom = partial_attention(s, first_piece, pieces, order_ref, qt_ref, score_ref, acc_ref)
        scale = other_scale = 1.0
        if merges:
            acc_in, stats_in = ins[:2]
            other_top, other_denom = stats_in[s, 0:1], stats_in[s, 1:2]
            overall = jnp.maximum(top, other_top)
            scale, other_scale = jnp.exp2(top - overall), jnp.exp2(other_top - overall)
            denom = scale * denom + other_scale * other_denom
            top = overall
        if ends:
            share = 1.0 / denom
            scale, other_scale = scale * share, other_scale * share
        acc = acc_ref[...] * scale
        if merges:
            acc = acc + acc_in[s] * other_scale
        if ends:
            rows = pl.ds(s * BLOCK, BLOCK)
            for h in range(heads):
                at = pl.ds(h * head_size, head_size)
                outs[0][0, rows, at] = acc[:, h * BLOCK : (h + 1) * BLOCK].T.astype(outs[0].dtype)
        else:
            outs[0][s] = acc
            outs[1][s, 0:1] = top
            outs[1][s, 1:2] = denom


def swap(piece, axis, flip):
    array, places = piece
    came = lax.ppermute(array, axis, [(i, i ^ flip) for i in range(lax.axis_size(axis))])
    if axis == "row":
        return came, [(r ^ flip, c) for r, c in places]
    return came, [(r, c ^ flip) for r, c in places]


def join_pieces(pieces, transpose=True):
    vmem = pl.BlockSpec(memory_space=pltpu.VMEM)
    first = pieces[0][0]
    blocks = sum(array.shape[0] for array, _ in pieces)
    array = pl.pallas_call(
        functools.partial(join_kernel, transpose),
        out_shape=jax.ShapeDtypeStruct((blocks,) + first.shape[1:], first.dtype),
        in_specs=[vmem] * len(pieces),
        out_specs=vmem,
        compiler_params=pltpu.CompilerParams(vmem_limit_bytes=4 * 1024 * 1024),
        name="join",
    )(*(array for array, _ in pieces))
    return array, [place for _, places in pieces for place in places]


def together(pieces, *others):
    arrays = lax.optimization_barrier([array for array, _ in pieces] + list(others))
    held = [(array, places) for array, (_, places) in zip(arrays, pieces)]
    return (held, *arrays[len(held) :]) if others else held


def across(piece, cols):
    pieces = [piece]
    flip = CORES
    while flip < cols:
        pieces += [swap(one, "col", flip) for one in pieces]
        flip *= 2
    return pieces[1:]


def per_device(queries, keys, values, block_list, block_count):
    head_size = keys.shape[2]
    heads = queries.shape[2] // head_size
    own_blocks = queries.shape[1] // BLOCK
    per = keys.shape[1] // BLOCK
    rows = lax.axis_size("row")
    cols = lax.axis_size("col")
    panels, slots = block_list.shape[2:]
    blocks = panels * slots
    vmem = pl.BlockSpec(memory_space=pltpu.VMEM)
    smem = pl.BlockSpec(memory_space=pltpu.SMEM)
    anywhere = pl.BlockSpec(memory_space=pl.ANY)
    small = pltpu.CompilerParams(vmem_limit_bytes=4 * 1024 * 1024)

    shape = (per, BLOCK, head_size)
    packed = jnp.concatenate([keys.reshape(shape), values.reshape(shape)], axis=1)

    own = (packed, [(0, 0)])
    flip = rows // 2
    while flip > 2:
        came = swap(own, "row", flip)
        own = jnp.concatenate([own[0], came[0]]), own[1] + came[1]
        flip //= 2
    near, far = (swap(own, "row", flip) for flip in (1, 2))
    near, late_own, *own_across = together([near, own, *across(own, cols)])
    near_across = across(near, cols)
    opposite = swap(late_own, "row", 3)
    far, *near_across = together([far, *near_across])
    far_across = across(far, cols)
    early = join_pieces([own, near, *own_across])
    early_pair = swap(early, "col", 1)
    middle = [opposite, far, *near_across, *far_across]
    late_places = [place for _, where in middle for place in where]
    last_places = [(r, c ^ flip) for flip in range(CORES, cols, CORES) for r, c in opposite[1]]
    places = [part for where in (early[1], late_places, last_places) for part in (where, [(r, c ^ 1) for r, c in where])]

    longest = max(len(where) for where in places) * per
    queries_across, order = pl.pallas_call(
        functools.partial(prepare_kernel, heads, per, places),
        out_shape=(
            jax.ShapeDtypeStruct((own_blocks, head_size, heads * BLOCK), queries.dtype),
            jax.ShapeDtypeStruct((own_blocks, len(places), longest + 3), jnp.int32),
        ),
        in_specs=[vmem, anywhere, anywhere],
        out_specs=(vmem, smem),
        scratch_shapes=[
            pltpu.SMEM((blocks,), jnp.int32),
            pltpu.SMEM((own_blocks, panels, slots), jnp.int32),
            pltpu.SMEM((own_blocks, panels), jnp.int32),
            pltpu.SemaphoreType.DMA((2,)),
        ],
        compiler_params=small,
        name="prepare",
    )(queries, block_list, block_count)
    middle, queries_across, order = together(middle, queries_across, order)
    last = across(middle[0], cols)
    late = join_pieces(middle)
    late_pair = swap(late, "col", 1)

    width = heads * BLOCK
    held = 2 * max(len(early[1]), len(late_places), len(last_places)) * per

    def attend(name, first_piece, pieces, part=(), ends=False):
        whole = jax.ShapeDtypeStruct(queries.shape, jnp.bfloat16)
        parts = (
            jax.ShapeDtypeStruct((own_blocks, head_size, width), jnp.float32),
            jax.ShapeDtypeStruct((own_blocks, 2, width), jnp.float32),
        )
        return pl.pallas_call(
            functools.partial(attend_kernel, heads, first_piece, bool(part), ends),
            out_shape=whole if ends else parts,
            in_specs=[vmem, anywhere] + [vmem] * (len(part) + len(pieces)),
            out_specs=vmem if ends else (vmem, vmem),
            scratch_shapes=[
                pltpu.VMEM((held, BLOCK, width), jnp.float32),
                pltpu.VMEM((head_size, width), jnp.float32),
                pltpu.SMEM(order.shape, jnp.int32),
                pltpu.SemaphoreType.DMA,
            ],
            compiler_params=pltpu.CompilerParams(vmem_limit_bytes=held * BLOCK * width * 4 + 4 * 1024 * 1024),
            name=name,
        )(queries_across, order, *part, *(array for array, _ in pieces))

    part = attend("early", 0, [early, early_pair])
    last, *part = together(last, *part)
    last = join_pieces(last)
    part = attend("late", 2, [late, late_pair], part)
    return attend("last", 4, [last, swap(last, "col", 1)], part, ends=True)


def solution(mesh):
    placed = (
        P(("groups", "col"), "row", None),
        P(("groups", "row"), "col", None),
        P(("groups", "row"), "col", None),
        P("groups", None, None, None),
        P("groups", None, None),
    )
    return jax.shard_map(
        per_device,
        mesh=mesh,
        in_specs=placed,
        out_specs=P(("groups", "col"), "row", None),
        check_vma=False,
    )
```

```python
import functools
import math

import jax
import jax.numpy as jnp
from jax import lax
from jax.experimental import pallas as pl
from jax.experimental.pallas import tpu as pltpu
from jax.sharding import PartitionSpec as P

BLOCK = 128
CORES = 2

floor_score = -1e30


def join_kernel(transpose, *refs):
    out_ref = refs[-1]
    first = 0
    for ref in refs[:-1]:
        if not transpose:
            out_ref[first : first + ref.shape[0]] = ref[...]
        for n in range(ref.shape[0] if transpose else 0):
            out_ref[first + n, :BLOCK, :] = ref[n, :BLOCK, :]
            out_ref[first + n, BLOCK:, :] = ref[n, BLOCK:, :].T
        first += ref.shape[0]


def prepare_kernel(heads, per, places, q_ref, list_hbm, count_hbm, qt_ref, order_ref,
                   active_ref, list_ref, count_ref, sems):
    own_blocks, head_size = qt_ref.shape[:2]
    panels, slots = list_ref.shape[1:]
    end = order_ref.shape[2] - 2
    cols = lax.axis_size("col")
    col_index = lax.axis_index("col")
    row_index = lax.axis_index("row")
    first = row_index * own_blocks
    copies = (
        pltpu.make_async_copy(list_hbm.at[col_index, pl.ds(first, own_blocks)], list_ref, sems.at[0]),
        pltpu.make_async_copy(count_hbm.at[col_index, pl.ds(first, own_blocks)], count_ref, sems.at[1]),
    )
    for copy in copies:
        copy.start()
    for s in range(own_blocks):
        for h in range(heads):
            tile = q_ref[0, pl.ds(s * BLOCK, BLOCK), pl.ds(h * head_size, head_size)]
            qt_ref[s, :, pl.ds(h * BLOCK, BLOCK)] = tile.T
    for copy in copies:
        copy.wait()
    for s in range(own_blocks):
        diagonal = col_index * list_hbm.shape[1] + first + s
        for r in range(panels):
            for n in range(slots):
                active_ref[r * slots + n] = 0
            for n in reversed(range(slots)):
                active_ref[r * slots + list_ref[s, r, n]] = (n < count_ref[s, r]).astype(jnp.int32)
        for piece, where in enumerate(places):
            total = jnp.int32(0)
            diagonal_slot = jnp.int32(-1)
            for n, (row_flip, col_flip) in enumerate(where):
                for k in range(per):
                    block = ((row_index ^ row_flip) * cols + (col_index ^ col_flip)) * per + k
                    order_ref[s, piece, total] = n * per + k
                    on_diagonal = block == diagonal
                    diagonal_slot = jnp.where(on_diagonal, n * per + k, diagonal_slot)
                    total = total + jnp.where(on_diagonal, 0, active_ref[block])
            order_ref[s, piece, total] = diagonal_slot
            order_ref[s, piece, end] = total
            order_ref[s, piece, end + 1] = total + (diagonal_slot >= 0).astype(jnp.int32)


def partial_attention(s, first_piece, pieces, order_ref, qt_ref, score_ref, acc_ref):
    head_size, width = qt_ref.shape[1:]
    end = order_ref.shape[2] - 2
    factor = math.log2(math.e) / head_size**0.5
    top = jnp.full((8, width), floor_score, jnp.float32)
    at = jnp.int32(0)
    starts = []
    for n, piece in enumerate(pieces):
        starts.append(at)

        def score(t, top, n=n, piece=piece, at=at, masked=False):
            slot = order_ref[s, first_piece + n, t]
            found = jnp.dot(piece[slot, :BLOCK, :], qt_ref[s], preferred_element_type=jnp.float32)
            if masked:
                key_at = lax.broadcasted_iota(jnp.int32, (BLOCK, width), 0)
                query_at = lax.broadcasted_iota(jnp.int32, (BLOCK, width), 1) % BLOCK
                found = jnp.where(query_at >= key_at, found, floor_score)
            score_ref[at + t] = found
            return jnp.maximum(top, jnp.max(found.reshape(BLOCK // 8, 8, width), axis=0))

        plain = order_ref[s, first_piece + n, end]
        total = order_ref[s, first_piece + n, end + 1]
        top = lax.fori_loop(0, plain, score, top)
        top = lax.fori_loop(plain, total, functools.partial(score, masked=True), top)
        at = at + total
    top = jnp.max(top, axis=0, keepdims=True) * factor
    acc_ref[...] = jnp.zeros_like(acc_ref)
    denom = jnp.zeros((8, width), jnp.float32)
    for n, piece in enumerate(pieces):

        def mix(t, denom, n=n, piece=piece, at=starts[n]):
            slot = order_ref[s, first_piece + n, t]
            weights = jnp.exp2(score_ref[at + t] * factor - top)
            acc_ref[...] += jnp.dot(
                piece[slot, BLOCK:, :], weights.astype(jnp.bfloat16), preferred_element_type=jnp.float32
            )
            return denom + jnp.sum(weights.reshape(BLOCK // 8, 8, width), axis=0)

        denom = lax.fori_loop(0, order_ref[s, first_piece + n, end + 1], mix, denom)
    return top, jnp.sum(denom, axis=0, keepdims=True)


def attend_kernel(heads, first_piece, merges, ends, qt_ref, order_hbm, *refs):
    score_ref, acc_ref, order_ref, sem = refs[-4:]
    outs = refs[-5:-4] if ends else refs[-6:-4]
    ins = refs[: -4 - len(outs)]
    pieces = ins[2:] if merges else ins
    head_size = qt_ref.shape[1]
    copy = pltpu.make_async_copy(order_hbm, order_ref, sem)
    copy.start()
    copy.wait()
    for s in range(qt_ref.shape[0]):
        top, denom = partial_attention(s, first_piece, pieces, order_ref, qt_ref, score_ref, acc_ref)
        scale = other_scale = 1.0
        if merges:
            acc_in, stats_in = ins[:2]
            other_top, other_denom = stats_in[s, 0:1], stats_in[s, 1:2]
            overall = jnp.maximum(top, other_top)
            scale, other_scale = jnp.exp2(top - overall), jnp.exp2(other_top - overall)
            denom = scale * denom + other_scale * other_denom
            top = overall
        if ends:
            share = 1.0 / denom
            scale, other_scale = scale * share, other_scale * share
        acc = acc_ref[...] * scale
        if merges:
            acc = acc + acc_in[s] * other_scale
        if ends:
            rows = pl.ds(s * BLOCK, BLOCK)
            for h in range(heads):
                at = pl.ds(h * head_size, head_size)
                outs[0][0, rows, at] = acc[:, h * BLOCK : (h + 1) * BLOCK].T.astype(outs[0].dtype)
        else:
            outs[0][s] = acc
            outs[1][s, 0:1] = top
            outs[1][s, 1:2] = denom


def swap(piece, axis, flip):
    array, places = piece
    came = lax.ppermute(array, axis, [(i, i ^ flip) for i in range(lax.axis_size(axis))])
    if axis == "row":
        return came, [(r ^ flip, c) for r, c in places]
    return came, [(r, c ^ flip) for r, c in places]


def join_pieces(pieces, transpose=True):
    vmem = pl.BlockSpec(memory_space=pltpu.VMEM)
    first = pieces[0][0]
    blocks = sum(array.shape[0] for array, _ in pieces)
    array = pl.pallas_call(
        functools.partial(join_kernel, transpose),
        out_shape=jax.ShapeDtypeStruct((blocks,) + first.shape[1:], first.dtype),
        in_specs=[vmem] * len(pieces),
        out_specs=vmem,
        compiler_params=pltpu.CompilerParams(vmem_limit_bytes=4 * 1024 * 1024),
        name="join",
    )(*(array for array, _ in pieces))
    return array, [place for _, places in pieces for place in places]


def together(pieces, *others):
    arrays = lax.optimization_barrier([array for array, _ in pieces] + list(others))
    held = [(array, places) for array, (_, places) in zip(arrays, pieces)]
    return (held, *arrays[len(held) :]) if others else held


def across(piece, cols):
    pieces = [piece]
    flip = CORES
    while flip < cols:
        pieces += [swap(one, "col", flip) for one in pieces]
        flip *= 2
    return pieces[1:]


def per_device(queries, keys, values, block_list, block_count):
    head_size = keys.shape[2]
    heads = queries.shape[2] // head_size
    own_blocks = queries.shape[1] // BLOCK
    per = keys.shape[1] // BLOCK
    rows = lax.axis_size("row")
    cols = lax.axis_size("col")
    panels, slots = block_list.shape[2:]
    blocks = panels * slots
    vmem = pl.BlockSpec(memory_space=pltpu.VMEM)
    smem = pl.BlockSpec(memory_space=pltpu.SMEM)
    anywhere = pl.BlockSpec(memory_space=pl.ANY)
    small = pltpu.CompilerParams(vmem_limit_bytes=4 * 1024 * 1024)

    shape = (per, BLOCK, head_size)
    packed = jnp.concatenate([keys.reshape(shape), values.reshape(shape)], axis=1)

    own = (packed, [(0, 0)])
    flip = rows // 2
    while flip > 2:
        came = swap(own, "row", flip)
        own = jnp.concatenate([own[0], came[0]]), own[1] + came[1]
        flip //= 2
    near, far, opposite = (swap(own, "row", flip) for flip in (1, 2, 3))
    own_across = across(own, cols)
    early_places = [place for _, where in (own, near, far, opposite, *own_across) for place in where]
    late_places = [(r, c ^ flip) for flip in range(CORES, cols, CORES) for r, c in near[1] + far[1] + opposite[1]]
    places = [part for where in (early_places, late_places) for part in (where, [(r, c ^ 1) for r, c in where])]

    longest = max(len(where) for where in places) * per
    queries_across, order = pl.pallas_call(
        functools.partial(prepare_kernel, heads, per, places),
        out_shape=(
            jax.ShapeDtypeStruct((own_blocks, head_size, heads * BLOCK), queries.dtype),
            jax.ShapeDtypeStruct((own_blocks, len(places), longest + 3), jnp.int32),
        ),
        in_specs=[vmem, anywhere, anywhere],
        out_specs=(vmem, smem),
        scratch_shapes=[
            pltpu.SMEM((blocks,), jnp.int32),
            pltpu.SMEM((own_blocks, panels, slots), jnp.int32),
            pltpu.SMEM((own_blocks, panels), jnp.int32),
            pltpu.SemaphoreType.DMA((2,)),
        ],
        compiler_params=small,
        name="prepare",
    )(queries, block_list, block_count)
    (opposite,), queries_across, order = together([opposite], queries_across, order)
    others = [near, far, opposite]
    last = across(join_pieces(others, False), cols)
    early = join_pieces([own, *others, *own_across])
    early_pair = swap(early, "col", 1)

    width = heads * BLOCK
    held = 2 * max(len(early_places), len(late_places)) * per

    def attend(name, first_piece, pieces, part=(), ends=False):
        whole = jax.ShapeDtypeStruct(queries.shape, jnp.bfloat16)
        parts = (
            jax.ShapeDtypeStruct((own_blocks, head_size, width), jnp.float32),
            jax.ShapeDtypeStruct((own_blocks, 2, width), jnp.float32),
        )
        return pl.pallas_call(
            functools.partial(attend_kernel, heads, first_piece, bool(part), ends),
            out_shape=whole if ends else parts,
            in_specs=[vmem, anywhere] + [vmem] * (len(part) + len(pieces)),
            out_specs=vmem if ends else (vmem, vmem),
            scratch_shapes=[
                pltpu.VMEM((held, BLOCK, width), jnp.float32),
                pltpu.VMEM((head_size, width), jnp.float32),
                pltpu.SMEM(order.shape, jnp.int32),
                pltpu.SemaphoreType.DMA,
            ],
            compiler_params=pltpu.CompilerParams(vmem_limit_bytes=held * BLOCK * width * 4 + 4 * 1024 * 1024),
            name=name,
        )(queries_across, order, *part, *(array for array, _ in pieces))

    part = attend("early", 0, [early, early_pair])
    last, *part = together(last, *part)
    last = join_pieces(last)
    return attend("last", 2, [last, swap(last, "col", 1)], part, ends=True)


def solution(mesh):
    placed = (
        P(("groups", "col"), "row", None),
        P(("groups", "row"), "col", None),
        P(("groups", "row"), "col", None),
        P("groups", None, None, None),
        P("groups", None, None),
    )
    return jax.shard_map(
        per_device,
        mesh=mesh,
        in_specs=placed,
        out_specs=P(("groups", "col"), "row", None),
        check_vma=False,
    )
```

```python
import functools
import math

import jax
import jax.numpy as jnp
from jax import lax
from jax.experimental import pallas as pl
from jax.experimental.pallas import tpu as pltpu
from jax.sharding import PartitionSpec as P

BLOCK = 128
CORES = 2

floor_score = -1e30


def join_kernel(transpose, *refs):
    out_ref = refs[-1]
    first = 0
    for ref in refs[:-1]:
        if not transpose:
            out_ref[first : first + ref.shape[0]] = ref[...]
        for n in range(ref.shape[0] if transpose else 0):
            out_ref[first + n, :BLOCK, :] = ref[n, :BLOCK, :]
            out_ref[first + n, BLOCK:, :] = ref[n, BLOCK:, :].T
        first += ref.shape[0]


def prepare_kernel(heads, per, places, q_ref, list_hbm, count_hbm, qt_ref, order_ref,
                   active_ref, list_ref, count_ref, sems):
    own_blocks, head_size = qt_ref.shape[:2]
    panels, slots = list_ref.shape[1:]
    end = order_ref.shape[2] - 2
    cols = lax.axis_size("col")
    col_index = lax.axis_index("col")
    row_index = lax.axis_index("row")
    first = row_index * own_blocks
    copies = (
        pltpu.make_async_copy(list_hbm.at[col_index, pl.ds(first, own_blocks)], list_ref, sems.at[0]),
        pltpu.make_async_copy(count_hbm.at[col_index, pl.ds(first, own_blocks)], count_ref, sems.at[1]),
    )
    for copy in copies:
        copy.start()
    for s in range(own_blocks):
        for h in range(heads):
            tile = q_ref[0, pl.ds(s * BLOCK, BLOCK), pl.ds(h * head_size, head_size)]
            qt_ref[s, :, pl.ds(h * BLOCK, BLOCK)] = tile.T
    for copy in copies:
        copy.wait()
    for s in range(own_blocks):
        diagonal = col_index * list_hbm.shape[1] + first + s
        for r in range(panels):
            for n in range(slots):
                active_ref[r * slots + n] = 0
            for n in reversed(range(slots)):
                active_ref[r * slots + list_ref[s, r, n]] = (n < count_ref[s, r]).astype(jnp.int32)
        for piece, where in enumerate(places):
            total = jnp.int32(0)
            diagonal_slot = jnp.int32(-1)
            for n, (row_flip, col_flip) in enumerate(where):
                for k in range(per):
                    block = ((row_index ^ row_flip) * cols + (col_index ^ col_flip)) * per + k
                    order_ref[s, piece, total] = n * per + k
                    on_diagonal = block == diagonal
                    diagonal_slot = jnp.where(on_diagonal, n * per + k, diagonal_slot)
                    total = total + jnp.where(on_diagonal, 0, active_ref[block])
            order_ref[s, piece, total] = diagonal_slot
            order_ref[s, piece, end] = total
            order_ref[s, piece, end + 1] = total + (diagonal_slot >= 0).astype(jnp.int32)


def partial_attention(s, first_piece, pieces, order_ref, qt_ref, score_ref, acc_ref):
    head_size, width = qt_ref.shape[1:]
    end = order_ref.shape[2] - 2
    factor = math.log2(math.e) / head_size**0.5
    top = jnp.full((8, width), floor_score, jnp.float32)
    at = jnp.int32(0)
    starts = []
    for n, piece in enumerate(pieces):
        starts.append(at)

        def score(t, top, n=n, piece=piece, at=at, masked=False):
            slot = order_ref[s, first_piece + n, t]
            found = jnp.dot(piece[slot, :BLOCK, :], qt_ref[s], preferred_element_type=jnp.float32)
            if masked:
                key_at = lax.broadcasted_iota(jnp.int32, (BLOCK, width), 0)
                query_at = lax.broadcasted_iota(jnp.int32, (BLOCK, width), 1) % BLOCK
                found = jnp.where(query_at >= key_at, found, floor_score)
            score_ref[at + t] = found
            return jnp.maximum(top, jnp.max(found.reshape(BLOCK // 8, 8, width), axis=0))

        plain = order_ref[s, first_piece + n, end]
        total = order_ref[s, first_piece + n, end + 1]
        top = lax.fori_loop(0, plain, score, top)
        top = lax.fori_loop(plain, total, functools.partial(score, masked=True), top)
        at = at + total
    top = jnp.max(top, axis=0, keepdims=True) * factor
    acc_ref[...] = jnp.zeros_like(acc_ref)
    denom = jnp.zeros((8, width), jnp.float32)
    for n, piece in enumerate(pieces):

        def mix(t, denom, n=n, piece=piece, at=starts[n]):
            slot = order_ref[s, first_piece + n, t]
            weights = jnp.exp2(score_ref[at + t] * factor - top)
            acc_ref[...] += jnp.dot(
                piece[slot, BLOCK:, :], weights.astype(jnp.bfloat16), preferred_element_type=jnp.float32
            )
            return denom + jnp.sum(weights.reshape(BLOCK // 8, 8, width), axis=0)

        denom = lax.fori_loop(0, order_ref[s, first_piece + n, end + 1], mix, denom)
    return top, jnp.sum(denom, axis=0, keepdims=True)


def attend_kernel(heads, first_piece, merges, ends, qt_ref, order_hbm, *refs):
    score_ref, acc_ref, order_ref, sem = refs[-4:]
    outs = refs[-5:-4] if ends else refs[-6:-4]
    ins = refs[: -4 - len(outs)]
    pieces = ins[2:] if merges else ins
    head_size = qt_ref.shape[1]
    copy = pltpu.make_async_copy(order_hbm, order_ref, sem)
    copy.start()
    copy.wait()
    for s in range(qt_ref.shape[0]):
        top, denom = partial_attention(s, first_piece, pieces, order_ref, qt_ref, score_ref, acc_ref)
        scale = other_scale = 1.0
        if merges:
            acc_in, stats_in = ins[:2]
            other_top, other_denom = stats_in[s, 0:1], stats_in[s, 1:2]
            overall = jnp.maximum(top, other_top)
            scale, other_scale = jnp.exp2(top - overall), jnp.exp2(other_top - overall)
            denom = scale * denom + other_scale * other_denom
            top = overall
        if ends:
            share = 1.0 / denom
            scale, other_scale = scale * share, other_scale * share
        acc = acc_ref[...] * scale
        if merges:
            acc = acc + acc_in[s] * other_scale
        if ends:
            rows = pl.ds(s * BLOCK, BLOCK)
            for h in range(heads):
                at = pl.ds(h * head_size, head_size)
                outs[0][0, rows, at] = acc[:, h * BLOCK : (h + 1) * BLOCK].T.astype(outs[0].dtype)
        else:
            outs[0][s] = acc
            outs[1][s, 0:1] = top
            outs[1][s, 1:2] = denom


def swap(piece, axis, flip):
    array, places = piece
    came = lax.ppermute(array, axis, [(i, i ^ flip) for i in range(lax.axis_size(axis))])
    if axis == "row":
        return came, [(r ^ flip, c) for r, c in places]
    return came, [(r, c ^ flip) for r, c in places]


def join_pieces(pieces, transpose=True):
    vmem = pl.BlockSpec(memory_space=pltpu.VMEM)
    first = pieces[0][0]
    blocks = sum(array.shape[0] for array, _ in pieces)
    array = pl.pallas_call(
        functools.partial(join_kernel, transpose),
        out_shape=jax.ShapeDtypeStruct((blocks,) + first.shape[1:], first.dtype),
        in_specs=[vmem] * len(pieces),
        out_specs=vmem,
        compiler_params=pltpu.CompilerParams(vmem_limit_bytes=4 * 1024 * 1024),
        name="join",
    )(*(array for array, _ in pieces))
    return array, [place for _, places in pieces for place in places]


def together(pieces, *others):
    arrays = lax.optimization_barrier([array for array, _ in pieces] + list(others))
    held = [(array, places) for array, (_, places) in zip(arrays, pieces)]
    return (held, *arrays[len(held) :]) if others else held


def across(piece, cols):
    pieces = [piece]
    flip = CORES
    while flip < cols:
        pieces += [swap(one, "col", flip) for one in pieces]
        flip *= 2
    return pieces[1:]


def per_device(queries, keys, values, block_list, block_count):
    head_size = keys.shape[2]
    heads = queries.shape[2] // head_size
    own_blocks = queries.shape[1] // BLOCK
    per = keys.shape[1] // BLOCK
    rows = lax.axis_size("row")
    cols = lax.axis_size("col")
    panels, slots = block_list.shape[2:]
    blocks = panels * slots
    vmem = pl.BlockSpec(memory_space=pltpu.VMEM)
    smem = pl.BlockSpec(memory_space=pltpu.SMEM)
    anywhere = pl.BlockSpec(memory_space=pl.ANY)
    small = pltpu.CompilerParams(vmem_limit_bytes=4 * 1024 * 1024)

    shape = (per, BLOCK, head_size)
    packed = jnp.concatenate([keys.reshape(shape), values.reshape(shape)], axis=1)

    own = (packed, [(0, 0)])
    flip = rows // 2
    while flip > 2:
        came = swap(own, "row", flip)
        own = jnp.concatenate([own[0], came[0]]), own[1] + came[1]
        flip //= 2
    near, far, opposite = (swap(own, "row", flip) for flip in (1, 2, 3))
    own_across = across(own, cols)
    early_places = [place for _, where in (own, *own_across, near, far, opposite) for place in where]
    late_places = [(r, c ^ flip) for flip in range(CORES, cols, CORES) for r, c in near[1] + far[1] + opposite[1]]
    places = [part for where in (early_places, late_places) for part in (where, [(r, c ^ 1) for r, c in where])]

    longest = max(len(where) for where in places) * per
    queries_across, order = pl.pallas_call(
        functools.partial(prepare_kernel, heads, per, places),
        out_shape=(
            jax.ShapeDtypeStruct((own_blocks, head_size, heads * BLOCK), queries.dtype),
            jax.ShapeDtypeStruct((own_blocks, len(places), longest + 3), jnp.int32),
        ),
        in_specs=[vmem, anywhere, anywhere],
        out_specs=(vmem, smem),
        scratch_shapes=[
            pltpu.SMEM((blocks,), jnp.int32),
            pltpu.SMEM((own_blocks, panels, slots), jnp.int32),
            pltpu.SMEM((own_blocks, panels), jnp.int32),
            pltpu.SemaphoreType.DMA((2,)),
        ],
        compiler_params=small,
        name="prepare",
    )(queries, block_list, block_count)
    (opposite,), queries_across, order = together([opposite], queries_across, order)
    others = [near, far, opposite]
    last = across(join_pieces(others, False), cols)
    halves = [join_pieces([own, *own_across]), join_pieces([near, far]), join_pieces([opposite])]
    early = join_pieces(halves, False)
    early_pair = join_pieces([swap(half, "col", 1) for half in halves], False)

    width = heads * BLOCK
    held = 2 * max(len(early_places), len(late_places)) * per

    def attend(name, first_piece, pieces, part=(), ends=False):
        whole = jax.ShapeDtypeStruct(queries.shape, jnp.bfloat16)
        parts = (
            jax.ShapeDtypeStruct((own_blocks, head_size, width), jnp.float32),
            jax.ShapeDtypeStruct((own_blocks, 2, width), jnp.float32),
        )
        return pl.pallas_call(
            functools.partial(attend_kernel, heads, first_piece, bool(part), ends),
            out_shape=whole if ends else parts,
            in_specs=[vmem, anywhere] + [vmem] * (len(part) + len(pieces)),
            out_specs=vmem if ends else (vmem, vmem),
            scratch_shapes=[
                pltpu.VMEM((held, BLOCK, width), jnp.float32),
                pltpu.VMEM((head_size, width), jnp.float32),
                pltpu.SMEM(order.shape, jnp.int32),
                pltpu.SemaphoreType.DMA,
            ],
            compiler_params=pltpu.CompilerParams(vmem_limit_bytes=held * BLOCK * width * 4 + 4 * 1024 * 1024),
            name=name,
        )(queries_across, order, *part, *(array for array, _ in pieces))

    part = attend("early", 0, [early, early_pair])
    last, *part = together(last, *part)
    last = join_pieces(last)
    return attend("last", 2, [last, swap(last, "col", 1)], part, ends=True)


def solution(mesh):
    placed = (
        P(("groups", "col"), "row", None),
        P(("groups", "row"), "col", None),
        P(("groups", "row"), "col", None),
        P("groups", None, None, None),
        P("groups", None, None),
    )
    return jax.shard_map(
        per_device,
        mesh=mesh,
        in_specs=placed,
        out_specs=P(("groups", "col"), "row", None),
        check_vma=False,
    )
```

```python
import functools
import math

import jax
import jax.numpy as jnp
from jax import lax
from jax.experimental import pallas as pl
from jax.experimental.pallas import tpu as pltpu
from jax.sharding import PartitionSpec as P

BLOCK = 128
CORES = 2

floor_score = -1e30


def join_kernel(transpose, *refs):
    out_ref = refs[-1]
    first = 0
    for ref in refs[:-1]:
        if not transpose:
            out_ref[first : first + ref.shape[0]] = ref[...]
        for n in range(ref.shape[0] if transpose else 0):
            out_ref[first + n, :BLOCK, :] = ref[n, :BLOCK, :]
            out_ref[first + n, BLOCK:, :] = ref[n, BLOCK:, :].T
        first += ref.shape[0]


def prepare_kernel(heads, per, places, q_ref, list_hbm, count_hbm, qt_ref, order_ref,
                   active_ref, list_ref, count_ref, sems):
    own_blocks, head_size = qt_ref.shape[:2]
    panels, slots = list_ref.shape[1:]
    end = order_ref.shape[2] - 2
    cols = lax.axis_size("col")
    col_index = lax.axis_index("col")
    row_index = lax.axis_index("row")
    first = row_index * own_blocks
    copies = (
        pltpu.make_async_copy(list_hbm.at[col_index, pl.ds(first, own_blocks)], list_ref, sems.at[0]),
        pltpu.make_async_copy(count_hbm.at[col_index, pl.ds(first, own_blocks)], count_ref, sems.at[1]),
    )
    for copy in copies:
        copy.start()
    for s in range(own_blocks):
        for h in range(heads):
            tile = q_ref[0, pl.ds(s * BLOCK, BLOCK), pl.ds(h * head_size, head_size)]
            qt_ref[s, :, pl.ds(h * BLOCK, BLOCK)] = tile.T
    for copy in copies:
        copy.wait()
    for s in range(own_blocks):
        diagonal = col_index * list_hbm.shape[1] + first + s
        for r in range(panels):
            for n in range(slots):
                active_ref[r * slots + n] = 0
            for n in reversed(range(slots)):
                active_ref[r * slots + list_ref[s, r, n]] = (n < count_ref[s, r]).astype(jnp.int32)
        for part, where in enumerate(places):
            total = jnp.int32(0)
            diagonal_slot = jnp.int32(-1)
            for n, (row_flip, col_flip) in enumerate(where):
                for k in range(per):
                    block = ((row_index ^ row_flip) * cols + (col_index ^ col_flip)) * per + k
                    order_ref[s, part, total] = n * per + k
                    on_diagonal = block == diagonal
                    diagonal_slot = jnp.where(on_diagonal, n * per + k, diagonal_slot)
                    total = total + jnp.where(on_diagonal, 0, active_ref[block])
            here = diagonal_slot >= 0
            order_ref[s, part, total] = diagonal_slot
            order_ref[s, part, end + 1] = jnp.where(here, total, -1)
            total = total + here.astype(jnp.int32)
            order_ref[s, part, total] = 0
            order_ref[s, part, end] = total


def partial_attention(s, part, kv_ref, order_ref, qt_ref, score_ref, acc_ref):
    head_size, width = qt_ref.shape[1:]
    end = order_ref.shape[2] - 2
    factor = math.log2(math.e) / head_size**0.5
    total = order_ref[s, part, end]
    diagonal = order_ref[s, part, end + 1]
    pairs = (total + 1) // 2
    key_at = lax.broadcasted_iota(jnp.int32, (BLOCK, width), 0)
    query_at = lax.broadcasted_iota(jnp.int32, (BLOCK, width), 1) % BLOCK

    def score(p, top):
        pair = [order_ref[s, part, 2 * p + n] for n in range(2)]
        keys = jnp.concatenate([kv_ref[slot, :BLOCK, :] for slot in pair])
        found = jnp.dot(keys, qt_ref[s], preferred_element_type=jnp.float32)
        for n in range(2):
            t = 2 * p + n
            reach = jnp.where(t == diagonal, 0, jnp.where(t < total, BLOCK, -BLOCK))
            one = jnp.where(query_at + reach >= key_at, found[n * BLOCK : (n + 1) * BLOCK], floor_score)
            score_ref[t] = one
            top = jnp.maximum(top, jnp.max(one.reshape(BLOCK // 8, 8, width), axis=0))
        return top

    top = lax.fori_loop(0, pairs, score, jnp.full((8, width), floor_score, jnp.float32))
    top = jnp.max(top, axis=0, keepdims=True) * factor
    acc_ref[...] = jnp.zeros_like(acc_ref)

    def mix(p, denom):
        pair = [order_ref[s, part, 2 * p + n] for n in range(2)]
        values = jnp.concatenate([kv_ref[slot, BLOCK:, :] for slot in pair], axis=1)
        weights = [jnp.exp2(score_ref[2 * p + n] * factor - top) for n in range(2)]
        rounded = jnp.concatenate([one.astype(jnp.bfloat16) for one in weights])
        acc_ref[...] += jnp.dot(values, rounded, preferred_element_type=jnp.float32)
        return denom + jnp.sum((weights[0] + weights[1]).reshape(BLOCK // 8, 8, width), axis=0)

    denom = lax.fori_loop(0, pairs, mix, jnp.zeros((8, width), jnp.float32))
    return top, jnp.sum(denom, axis=0, keepdims=True)


def attend_kernel(heads, part, merges, ends, qt_ref, order_hbm, kv_ref, *refs):
    score_ref, acc_ref, order_ref, sem = refs[-4:]
    outs = refs[-5:-4] if ends else refs[-6:-4]
    ins = refs[: -4 - len(outs)]
    head_size = qt_ref.shape[1]
    copy = pltpu.make_async_copy(order_hbm, order_ref, sem)
    copy.start()
    copy.wait()
    for s in range(qt_ref.shape[0]):
        top, denom = partial_attention(s, part, kv_ref, order_ref, qt_ref, score_ref, acc_ref)
        scale = other_scale = 1.0
        if merges:
            acc_in, stats_in = ins
            other_top, other_denom = stats_in[s, 0:1], stats_in[s, 1:2]
            overall = jnp.maximum(top, other_top)
            scale, other_scale = jnp.exp2(top - overall), jnp.exp2(other_top - overall)
            denom = scale * denom + other_scale * other_denom
            top = overall
        if ends:
            share = 1.0 / denom
            scale, other_scale = scale * share, other_scale * share
        acc = acc_ref[...] * scale
        if merges:
            acc = acc + acc_in[s] * other_scale
        if ends:
            rows = pl.ds(s * BLOCK, BLOCK)
            acc = acc.astype(outs[0].dtype)
            for h in range(heads):
                at = pl.ds(h * head_size, head_size)
                outs[0][0, rows, at] = acc[:, h * BLOCK : (h + 1) * BLOCK].T
        else:
            outs[0][s] = acc
            outs[1][s, 0:1] = top
            outs[1][s, 1:2] = denom


def swap(piece, axis, flip):
    array, places = piece
    came = lax.ppermute(array, axis, [(i, i ^ flip) for i in range(lax.axis_size(axis))])
    if axis == "row":
        return came, [(r ^ flip, c) for r, c in places]
    return came, [(r, c ^ flip) for r, c in places]


def join_pieces(pieces, transpose=True):
    vmem = pl.BlockSpec(memory_space=pltpu.VMEM)
    first = pieces[0][0]
    blocks = sum(array.shape[0] for array, _ in pieces)
    array = pl.pallas_call(
        functools.partial(join_kernel, transpose),
        out_shape=jax.ShapeDtypeStruct((blocks,) + first.shape[1:], first.dtype),
        in_specs=[vmem] * len(pieces),
        out_specs=vmem,
        compiler_params=pltpu.CompilerParams(vmem_limit_bytes=4 * 1024 * 1024),
        name="join",
    )(*(array for array, _ in pieces))
    return array, [place for _, places in pieces for place in places]


def together(pieces, *others):
    arrays = lax.optimization_barrier([array for array, _ in pieces] + list(others))
    held = [(array, places) for array, (_, places) in zip(arrays, pieces)]
    return (held, *arrays[len(held) :]) if others else held


def across(piece, cols):
    pieces = [piece]
    flip = CORES
    while flip < cols:
        pieces += [swap(one, "col", flip) for one in pieces]
        flip *= 2
    return pieces[1:]


def per_device(queries, keys, values, block_list, block_count):
    head_size = keys.shape[2]
    heads = queries.shape[2] // head_size
    own_blocks = queries.shape[1] // BLOCK
    per = keys.shape[1] // BLOCK
    rows = lax.axis_size("row")
    cols = lax.axis_size("col")
    panels, slots = block_list.shape[2:]
    blocks = panels * slots
    vmem = pl.BlockSpec(memory_space=pltpu.VMEM)
    smem = pl.BlockSpec(memory_space=pltpu.SMEM)
    anywhere = pl.BlockSpec(memory_space=pl.ANY)
    small = pltpu.CompilerParams(vmem_limit_bytes=4 * 1024 * 1024)

    shape = (per, BLOCK, head_size)
    packed = jnp.concatenate([keys.reshape(shape), values.reshape(shape)], axis=1)

    own = (packed, [(0, 0)])
    flip = rows // 2
    while flip > 2:
        came = swap(own, "row", flip)
        own = jnp.concatenate([own[0], came[0]]), own[1] + came[1]
        flip //= 2
    near, far, opposite = (swap(own, "row", flip) for flip in (1, 2, 3))
    own_across = across(own, cols)
    early_places = [place for _, where in (own, *own_across, near, far, opposite) for place in where]
    late_places = [(r, c ^ flip) for flip in range(CORES, cols, CORES) for r, c in near[1] + far[1] + opposite[1]]
    places = [where + [(r, c ^ 1) for r, c in where] for where in (early_places, late_places)]

    longest = max(len(where) for where in places) * per
    queries_across, order = pl.pallas_call(
        functools.partial(prepare_kernel, heads, per, places),
        out_shape=(
            jax.ShapeDtypeStruct((own_blocks, head_size, heads * BLOCK), queries.dtype),
            jax.ShapeDtypeStruct((own_blocks, len(places), longest + 3), jnp.int32),
        ),
        in_specs=[vmem, anywhere, anywhere],
        out_specs=(vmem, smem),
        scratch_shapes=[
            pltpu.SMEM((blocks,), jnp.int32),
            pltpu.SMEM((own_blocks, panels, slots), jnp.int32),
            pltpu.SMEM((own_blocks, panels), jnp.int32),
            pltpu.SemaphoreType.DMA((2,)),
        ],
        compiler_params=small,
        name="prepare",
    )(queries, block_list, block_count)
    (opposite,), queries_across, order = together([opposite], queries_across, order)
    others = [near, far, opposite]
    last = across(join_pieces(others, False), cols)
    halves = [join_pieces([own, *own_across]), join_pieces([near, far]), join_pieces([opposite])]
    early = join_pieces(halves + [swap(half, "col", 1) for half in halves], False)

    width = heads * BLOCK

    def attend(name, part, kv, earlier=(), ends=False):
        whole = jax.ShapeDtypeStruct(queries.shape, jnp.bfloat16)
        parts = (
            jax.ShapeDtypeStruct((own_blocks, head_size, width), jnp.float32),
            jax.ShapeDtypeStruct((own_blocks, 2, width), jnp.float32),
        )
        held = kv.shape[0] + kv.shape[0] % 2
        return pl.pallas_call(
            functools.partial(attend_kernel, heads, part, bool(earlier), ends),
            out_shape=whole if ends else parts,
            in_specs=[vmem, anywhere, vmem] + [vmem] * len(earlier),
            out_specs=vmem if ends else (vmem, vmem),
            scratch_shapes=[
                pltpu.VMEM((held, BLOCK, width), jnp.float32),
                pltpu.VMEM((head_size, width), jnp.float32),
                pltpu.SMEM(order.shape, jnp.int32),
                pltpu.SemaphoreType.DMA,
            ],
            compiler_params=pltpu.CompilerParams(vmem_limit_bytes=held * BLOCK * width * 4 + 4 * 1024 * 1024),
            name=name,
        )(queries_across, order, kv, *earlier)

    part = attend("early", 0, early[0])
    last, *part = together(last, *part)
    last = join_pieces(last)
    last = join_pieces([last, swap(last, "col", 1)], False)
    return attend("last", 1, last[0], part, ends=True)


def solution(mesh):
    placed = (
        P(("groups", "col"), "row", None),
        P(("groups", "row"), "col", None),
        P(("groups", "row"), "col", None),
        P("groups", None, None, None),
        P("groups", None, None),
    )
    return jax.shard_map(
        per_device,
        mesh=mesh,
        in_specs=placed,
        out_specs=P(("groups", "col"), "row", None),
        check_vma=False,
    )
```

```python
import functools
import math

import jax
import jax.numpy as jnp
from jax import lax
from jax.experimental import pallas as pl
from jax.experimental.pallas import tpu as pltpu
from jax.sharding import PartitionSpec as P

BLOCK = 128
CORES = 2

floor_score = -1e30
floor_top = -1e20


def join_kernel(transpose, *refs):
    out_ref = refs[-1]
    first = 0
    for ref in refs[:-1]:
        if not transpose:
            out_ref[first : first + ref.shape[0]] = ref[...]
        for n in range(ref.shape[0] if transpose else 0):
            out_ref[first + n, :BLOCK, :] = ref[n, :BLOCK, :]
            out_ref[first + n, BLOCK:, :] = ref[n, BLOCK:, :].T
        first += ref.shape[0]


def prepare_kernel(per, places, dense, list_hbm, count_hbm, order_ref, active_ref, list_ref, count_ref, sems):
    own_blocks = order_ref.shape[0]
    panels, slots = list_ref.shape[1:]
    cols = lax.axis_size("col")
    col_index = lax.axis_index("col")
    row_index = lax.axis_index("row")
    first = row_index * own_blocks
    copies = (
        pltpu.make_async_copy(list_hbm.at[col_index, pl.ds(first, own_blocks)], list_ref, sems.at[0]),
        pltpu.make_async_copy(count_hbm.at[col_index, pl.ds(first, own_blocks)], count_ref, sems.at[1]),
    )
    for copy in copies:
        copy.start()
    for copy in copies:
        copy.wait()
    for s in range(own_blocks):
        diagonal = col_index * list_hbm.shape[1] + first + s
        for r in range(panels):
            for n in range(slots):
                active_ref[r * slots + n] = 0
            for n in reversed(range(slots)):
                active_ref[r * slots + list_ref[s, r, n]] = (n < count_ref[s, r]).astype(jnp.int32)
        for part, where in enumerate(places):
            total = jnp.int32(0)
            diagonal_slot = jnp.int32(-1)
            for n, (row_flip, col_flip) in enumerate(where):
                for k in range(per):
                    slot = n * per + k
                    block = ((row_index ^ row_flip) * cols + (col_index ^ col_flip)) * per + k
                    on_diagonal = block == diagonal
                    if dense:
                        reach = jnp.where(on_diagonal, 0, jnp.where(active_ref[block] > 0, BLOCK, -BLOCK))
                        order_ref[s, part, slot : slot + 1, :] = jnp.full((1, order_ref.shape[3]), reach, jnp.int32)
                        continue
                    order_ref[s, part, total] = slot
                    diagonal_slot = jnp.where(on_diagonal, slot, diagonal_slot)
                    total = total + jnp.where(on_diagonal, 0, active_ref[block])
            if dense:
                continue
            end = order_ref.shape[2] - 2
            here = diagonal_slot >= 0
            order_ref[s, part, total] = diagonal_slot
            order_ref[s, part, end + 1] = jnp.where(here, total, -1)
            total = total + here.astype(jnp.int32)
            order_ref[s, part, total] = 0
            order_ref[s, part, end] = total


def blockwise(array, fold):
    return fold(array.reshape(array.shape[0] // 8, 8, array.shape[1]), axis=0)


def dense_attention(reach, kv_ref, queries, score_ref):
    head_size, width = queries.shape
    slots = kv_ref.shape[0]
    factor = math.log2(math.e) / head_size**0.5
    key_at = lax.broadcasted_iota(jnp.int32, (BLOCK, width), 0)
    query_at = lax.broadcasted_iota(jnp.int32, (BLOCK, width), 1) % BLOCK
    keys = jnp.concatenate([kv_ref[slot, :BLOCK, :] for slot in range(slots)])
    found = jnp.dot(keys, queries, preferred_element_type=jnp.float32)
    top = jnp.full((8, width), floor_top, jnp.float32)
    for slot in range(slots):
        seen = query_at + reach[slot : slot + 1, :] >= key_at
        one = jnp.where(seen, found[slot * BLOCK : (slot + 1) * BLOCK], floor_score)
        score_ref[slot] = one
        top = jnp.maximum(top, blockwise(one, jnp.max))
    top = jnp.max(top, axis=0, keepdims=True) * factor
    denom = jnp.zeros((8, width), jnp.float32)
    rounded = []
    for slot in range(slots):
        one = jnp.exp2(score_ref[slot] * factor - top)
        denom = denom + blockwise(one, jnp.sum)
        rounded.append(one.astype(jnp.bfloat16))
    values = jnp.concatenate([kv_ref[slot, BLOCK:, :] for slot in range(slots)], axis=1)
    acc = jnp.dot(values, jnp.concatenate(rounded), preferred_element_type=jnp.float32)
    return acc, top, jnp.sum(denom, axis=0, keepdims=True)


def listed_attention(s, part, order_ref, kv_ref, queries, score_ref, acc_ref):
    head_size, width = queries.shape
    end = order_ref.shape[2] - 2
    factor = math.log2(math.e) / head_size**0.5
    total = order_ref[s, part, end]
    diagonal = order_ref[s, part, end + 1]
    pairs = (total + 1) // 2
    key_at = lax.broadcasted_iota(jnp.int32, (BLOCK, width), 0)
    query_at = lax.broadcasted_iota(jnp.int32, (BLOCK, width), 1) % BLOCK

    def score(p, top):
        pair = [order_ref[s, part, 2 * p + n] for n in range(2)]
        keys = jnp.concatenate([kv_ref[slot, :BLOCK, :] for slot in pair])
        found = jnp.dot(keys, queries, preferred_element_type=jnp.float32)
        for n in range(2):
            t = 2 * p + n
            reach = jnp.where(t == diagonal, 0, jnp.where(t < total, BLOCK, -BLOCK))
            one = jnp.where(query_at + reach >= key_at, found[n * BLOCK : (n + 1) * BLOCK], floor_score)
            score_ref[t] = one
            top = jnp.maximum(top, blockwise(one, jnp.max))
        return top

    top = lax.fori_loop(0, pairs, score, jnp.full((8, width), floor_top, jnp.float32))
    top = jnp.max(top, axis=0, keepdims=True) * factor
    acc_ref[...] = jnp.zeros_like(acc_ref)

    def mix(p, denom):
        pair = [order_ref[s, part, 2 * p + n] for n in range(2)]
        values = jnp.concatenate([kv_ref[slot, BLOCK:, :] for slot in pair], axis=1)
        weights = [jnp.exp2(score_ref[2 * p + n] * factor - top) for n in range(2)]
        rounded = jnp.concatenate([one.astype(jnp.bfloat16) for one in weights])
        acc_ref[...] += jnp.dot(values, rounded, preferred_element_type=jnp.float32)
        return denom + blockwise(weights[0] + weights[1], jnp.sum)

    denom = lax.fori_loop(0, pairs, mix, jnp.zeros((8, width), jnp.float32))
    return acc_ref[...], top, jnp.sum(denom, axis=0, keepdims=True)


def get_order(dense, order_ref, scratch):
    if dense:
        return order_ref
    held, sem = scratch
    copy = pltpu.make_async_copy(order_ref, held, sem)
    copy.start()
    copy.wait()
    return held


def attention(dense, s, part, order_ref, kv_ref, queries, score_ref, acc_ref):
    if dense:
        return dense_attention(order_ref[s, part], kv_ref, queries, score_ref)
    return listed_attention(s, part, order_ref, kv_ref, queries, score_ref, acc_ref)


def early_kernel(heads, dense, q_ref, order_in, kv_ref, qt_ref, acc_out, stats_out, score_ref, acc_ref, *scratch):
    order_ref = get_order(dense, order_in, scratch)
    own_blocks, head_size = qt_ref.shape[:2]
    for s in range(own_blocks):
        for h in range(heads):
            tile = q_ref[0, pl.ds(s * BLOCK, BLOCK), pl.ds(h * head_size, head_size)]
            qt_ref[s, :, pl.ds(h * BLOCK, BLOCK)] = tile.T
        acc, top, denom = attention(dense, s, 0, order_ref, kv_ref, qt_ref[s], score_ref, acc_ref)
        acc_out[s] = acc
        stats_out[s, 0:1] = top
        stats_out[s, 1:2] = denom


def last_kernel(heads, dense, qt_ref, order_in, kv_ref, acc_in, stats_in, out_hbm,
                out_ref, out_sems, score_ref, acc_ref, *scratch):
    order_ref = get_order(dense, order_in, scratch)
    own_blocks, head_size = qt_ref.shape[:2]
    copies = []
    for s in range(own_blocks):
        acc, top, denom = attention(dense, s, 1, order_ref, kv_ref, qt_ref[s], score_ref, acc_ref)
        other_top, other_denom = stats_in[s, 0:1], stats_in[s, 1:2]
        overall = jnp.maximum(top, other_top)
        scale, other_scale = jnp.exp2(top - overall), jnp.exp2(other_top - overall)
        share = 1.0 / (scale * denom + other_scale * other_denom)
        scale, other_scale = scale * share, other_scale * share
        for h in range(heads):
            rows, at = pl.ds(s * BLOCK, BLOCK), pl.ds(h * head_size, head_size)
            cut = slice(h * BLOCK, (h + 1) * BLOCK)
            one = acc[:, cut] * scale[:, cut] + acc_in[s, :, cut] * other_scale[:, cut]
            out_ref[0, rows, at] = one.astype(out_ref.dtype).T
            copy = pltpu.make_async_copy(out_ref.at[0, rows, at], out_hbm.at[0, rows, at], out_sems.at[s, h])
            copy.start()
            copies.append(copy)
    for copy in copies:
        copy.wait()


def swap(piece, axis, flip):
    array, places = piece
    came = lax.ppermute(array, axis, [(i, i ^ flip) for i in range(lax.axis_size(axis))])
    if axis == "row":
        return came, [(r ^ flip, c) for r, c in places]
    return came, [(r, c ^ flip) for r, c in places]


def join_pieces(pieces, transpose=True):
    vmem = pl.BlockSpec(memory_space=pltpu.VMEM)
    first = pieces[0][0]
    blocks = sum(array.shape[0] for array, _ in pieces)
    array = pl.pallas_call(
        functools.partial(join_kernel, transpose),
        out_shape=jax.ShapeDtypeStruct((blocks,) + first.shape[1:], first.dtype),
        in_specs=[vmem] * len(pieces),
        out_specs=vmem,
        compiler_params=pltpu.CompilerParams(vmem_limit_bytes=4 * 1024 * 1024),
        name="join",
    )(*(array for array, _ in pieces))
    return array, [place for _, places in pieces for place in places]


def together(pieces, *others):
    arrays = lax.optimization_barrier([array for array, _ in pieces] + list(others))
    held = [(array, places) for array, (_, places) in zip(arrays, pieces)]
    return (held, *arrays[len(held) :]) if others else held


def across(piece, cols):
    pieces = [piece]
    flip = CORES
    while flip < cols:
        pieces += [swap(one, "col", flip) for one in pieces]
        flip *= 2
    return pieces[1:]


def per_device(queries, keys, values, block_list, block_count):
    head_size = keys.shape[2]
    heads = queries.shape[2] // head_size
    own_blocks = queries.shape[1] // BLOCK
    per = keys.shape[1] // BLOCK
    rows = lax.axis_size("row")
    cols = lax.axis_size("col")
    panels, slots = block_list.shape[2:]
    blocks = panels * slots
    vmem = pl.BlockSpec(memory_space=pltpu.VMEM)
    smem = pl.BlockSpec(memory_space=pltpu.SMEM)
    anywhere = pl.BlockSpec(memory_space=pl.ANY)
    small = pltpu.CompilerParams(vmem_limit_bytes=4 * 1024 * 1024)

    shape = (per, BLOCK, head_size)
    packed = jnp.concatenate([keys.reshape(shape), values.reshape(shape)], axis=1)

    own = (packed, [(0, 0)])
    flip = rows // 2
    while flip > 2:
        came = swap(own, "row", flip)
        own = jnp.concatenate([own[0], came[0]]), own[1] + came[1]
        flip //= 2
    near, far, opposite = (swap(own, "row", flip) for flip in (1, 2, 3))
    own_across = across(own, cols)
    early_places = [place for _, where in (own, *own_across, near, far, opposite) for place in where]
    late_places = [(r, c ^ flip) for flip in range(CORES, cols, CORES) for r, c in near[1] + far[1] + opposite[1]]
    places = [where + [(r, c ^ 1) for r, c in where] for where in (early_places, late_places)]

    longest = max(len(where) for where in places) * per
    dense = longest <= 16
    width = heads * BLOCK
    order_shape = (own_blocks, len(places), longest, width) if dense else (own_blocks, len(places), longest + 3)
    order = pl.pallas_call(
        functools.partial(prepare_kernel, per, places, dense),
        out_shape=jax.ShapeDtypeStruct(order_shape, jnp.int32),
        in_specs=[anywhere, anywhere],
        out_specs=vmem if dense else smem,
        scratch_shapes=[
            pltpu.SMEM((blocks,), jnp.int32),
            pltpu.SMEM((own_blocks, panels, slots), jnp.int32),
            pltpu.SMEM((own_blocks, panels), jnp.int32),
            pltpu.SemaphoreType.DMA((2,)),
        ],
        compiler_params=small,
        name="prepare",
    )(block_list, block_count)
    (opposite,), order = together([opposite], order)
    others = [near, far, opposite]
    last = across(join_pieces(others, False), cols)
    halves = [join_pieces([own, *own_across]), join_pieces([near, far]), join_pieces([opposite])]
    early = join_pieces(halves + [swap(half, "col", 1) for half in halves], False)

    def attend(kernel, name, out_shape, out_specs, scratch, *args):
        held = args[2].shape[0] + args[2].shape[0] % 2
        scratch = scratch + [
            pltpu.VMEM((held, BLOCK, width), jnp.float32),
            pltpu.VMEM((head_size, width), jnp.float32),
        ]
        if not dense:
            scratch += [pltpu.SMEM(order.shape, jnp.int32), pltpu.SemaphoreType.DMA]
        return pl.pallas_call(
            functools.partial(kernel, heads, dense),
            out_shape=out_shape,
            in_specs=[vmem, vmem if dense else anywhere] + [vmem] * (len(args) - 2),
            out_specs=out_specs,
            scratch_shapes=scratch,
            compiler_params=pltpu.CompilerParams(vmem_limit_bytes=2 * held * BLOCK * width * 4 + 8 * 1024 * 1024),
            name=name,
        )(*args)

    parts = (
        jax.ShapeDtypeStruct((own_blocks, head_size, width), queries.dtype),
        jax.ShapeDtypeStruct((own_blocks, head_size, width), jnp.float32),
        jax.ShapeDtypeStruct((own_blocks, 2, width), jnp.float32),
    )
    queries_across, *part = attend(early_kernel, "early", parts, (vmem, vmem, vmem), [], queries, order, early[0])
    last, *part = together(last, *part)
    last = join_pieces(last)
    last = join_pieces([last, swap(last, "col", 1)], False)
    whole = jax.ShapeDtypeStruct(queries.shape, jnp.bfloat16)
    out_scratch = [pltpu.VMEM(queries.shape, jnp.bfloat16), pltpu.SemaphoreType.DMA((own_blocks, heads))]
    return attend(last_kernel, "last", whole, anywhere, out_scratch, queries_across, order, last[0], *part)


def solution(mesh):
    placed = (
        P(("groups", "col"), "row", None),
        P(("groups", "row"), "col", None),
        P(("groups", "row"), "col", None),
        P("groups", None, None, None),
        P("groups", None, None),
    )
    return jax.shard_map(
        per_device,
        mesh=mesh,
        in_specs=placed,
        out_specs=P(("groups", "col"), "row", None),
        check_vma=False,
    )
```

```python
import functools
import math

import jax
import jax.numpy as jnp
from jax import lax
from jax.experimental import pallas as pl
from jax.experimental.pallas import tpu as pltpu
from jax.sharding import PartitionSpec as P

BLOCK = 128
CORES = 2

floor_score = -1e30
floor_top = -1e20


def join_kernel(transpose, *refs):
    out_ref = refs[-1]
    first = 0
    for ref in refs[:-1]:
        if not transpose:
            out_ref[first : first + ref.shape[0]] = ref[...]
        for n in range(ref.shape[0] if transpose else 0):
            out_ref[first + n, :BLOCK, :] = ref[n, :BLOCK, :]
            out_ref[first + n, BLOCK:, :] = ref[n, BLOCK:, :].T
        first += ref.shape[0]


def prepare_kernel(per, places, dense, list_hbm, count_hbm, order_ref, active_ref, list_ref, count_ref, sems):
    own_blocks = order_ref.shape[0]
    panels, slots = list_ref.shape[1:]
    cols = lax.axis_size("col")
    col_index = lax.axis_index("col")
    row_index = lax.axis_index("row")
    first = row_index * own_blocks
    copies = (
        pltpu.make_async_copy(list_hbm.at[col_index, pl.ds(first, own_blocks)], list_ref, sems.at[0]),
        pltpu.make_async_copy(count_hbm.at[col_index, pl.ds(first, own_blocks)], count_ref, sems.at[1]),
    )
    for copy in copies:
        copy.start()
    for copy in copies:
        copy.wait()
    for s in range(own_blocks):
        diagonal = col_index * list_hbm.shape[1] + first + s
        for r in range(panels):
            for n in range(slots):
                active_ref[r * slots + n] = 0
            for n in reversed(range(slots)):
                active_ref[r * slots + list_ref[s, r, n]] = (n < count_ref[s, r]).astype(jnp.int32)
        for part, where in enumerate(places):
            total = jnp.int32(0)
            diagonal_slot = jnp.int32(-1)
            for n, (row_flip, col_flip) in enumerate(where):
                for k in range(per):
                    slot = n * per + k
                    block = ((row_index ^ row_flip) * cols + (col_index ^ col_flip)) * per + k
                    on_diagonal = block == diagonal
                    if dense:
                        reach = jnp.where(on_diagonal, 0, jnp.where(active_ref[block] > 0, BLOCK, -BLOCK))
                        order_ref[s, part, slot : slot + 1, :] = jnp.full((1, order_ref.shape[3]), reach, jnp.int32)
                        continue
                    order_ref[s, part, total] = slot
                    diagonal_slot = jnp.where(on_diagonal, slot, diagonal_slot)
                    total = total + jnp.where(on_diagonal, 0, active_ref[block])
            if dense:
                continue
            end = order_ref.shape[2] - 2
            here = diagonal_slot >= 0
            order_ref[s, part, total] = diagonal_slot
            order_ref[s, part, end + 1] = jnp.where(here, total, -1)
            total = total + here.astype(jnp.int32)
            order_ref[s, part, total] = 0
            order_ref[s, part, end] = total


def blockwise(array, fold):
    return fold(array.reshape(array.shape[0] // 8, 8, array.shape[1]), axis=0)


def dense_attention(reach, kv_ref, queries, score_ref):
    head_size, width = queries.shape
    slots = kv_ref.shape[0]
    factor = math.log2(math.e) / head_size**0.5
    key_at = lax.broadcasted_iota(jnp.int32, (BLOCK, width), 0)
    query_at = lax.broadcasted_iota(jnp.int32, (BLOCK, width), 1) % BLOCK
    keys = jnp.concatenate([kv_ref[slot, :BLOCK, :] for slot in range(slots)])
    found = jnp.dot(keys, queries, preferred_element_type=jnp.float32)
    top = jnp.full((8, width), floor_top, jnp.float32)
    for slot in range(slots):
        seen = query_at + reach[slot : slot + 1, :] >= key_at
        one = jnp.where(seen, found[slot * BLOCK : (slot + 1) * BLOCK], floor_score)
        score_ref[slot] = one
        top = jnp.maximum(top, blockwise(one, jnp.max))
    top = jnp.max(top, axis=0, keepdims=True) * factor
    denom = jnp.zeros((8, width), jnp.float32)
    rounded = []
    for slot in range(slots):
        one = jnp.exp2(score_ref[slot] * factor - top)
        denom = denom + blockwise(one, jnp.sum)
        rounded.append(one.astype(jnp.bfloat16))
    values = jnp.concatenate([kv_ref[slot, BLOCK:, :] for slot in range(slots)], axis=1)
    acc = jnp.dot(values, jnp.concatenate(rounded), preferred_element_type=jnp.float32)
    return acc, top, jnp.sum(denom, axis=0, keepdims=True)


def listed_attention(s, part, order_ref, kv_ref, queries, score_ref, acc_ref):
    head_size, width = queries.shape
    end = order_ref.shape[2] - 2
    factor = math.log2(math.e) / head_size**0.5
    total = order_ref[s, part, end]
    diagonal = order_ref[s, part, end + 1]
    pairs = (total + 1) // 2
    key_at = lax.broadcasted_iota(jnp.int32, (BLOCK, width), 0)
    query_at = lax.broadcasted_iota(jnp.int32, (BLOCK, width), 1) % BLOCK

    def score(p, top):
        pair = [order_ref[s, part, 2 * p + n] for n in range(2)]
        keys = jnp.concatenate([kv_ref[slot, :BLOCK, :] for slot in pair])
        found = jnp.dot(keys, queries, preferred_element_type=jnp.float32)
        for n in range(2):
            t = 2 * p + n
            reach = jnp.where(t == diagonal, 0, jnp.where(t < total, BLOCK, -BLOCK))
            one = jnp.where(query_at + reach >= key_at, found[n * BLOCK : (n + 1) * BLOCK], floor_score)
            score_ref[t] = one
            top = jnp.maximum(top, blockwise(one, jnp.max))
        return top

    top = lax.fori_loop(0, pairs, score, jnp.full((8, width), floor_top, jnp.float32))
    top = jnp.max(top, axis=0, keepdims=True) * factor
    acc_ref[...] = jnp.zeros_like(acc_ref)

    def mix(p, denom):
        pair = [order_ref[s, part, 2 * p + n] for n in range(2)]
        values = jnp.concatenate([kv_ref[slot, BLOCK:, :] for slot in pair], axis=1)
        weights = [jnp.exp2(score_ref[2 * p + n] * factor - top) for n in range(2)]
        rounded = jnp.concatenate([one.astype(jnp.bfloat16) for one in weights])
        acc_ref[...] += jnp.dot(values, rounded, preferred_element_type=jnp.float32)
        return denom + blockwise(weights[0] + weights[1], jnp.sum)

    denom = lax.fori_loop(0, pairs, mix, jnp.zeros((8, width), jnp.float32))
    return acc_ref[...], top, jnp.sum(denom, axis=0, keepdims=True)


def get_order(dense, order_ref, scratch):
    if dense:
        return order_ref
    held, sem = scratch
    copy = pltpu.make_async_copy(order_ref, held, sem)
    copy.start()
    copy.wait()
    return held


def attention(dense, s, part, order_ref, kv_ref, queries, score_ref, acc_ref):
    if dense:
        return dense_attention(order_ref[s, part], kv_ref, queries, score_ref)
    return listed_attention(s, part, order_ref, kv_ref, queries, score_ref, acc_ref)


def early_kernel(heads, dense, q_ref, order_in, kv_ref, qt_ref, acc_out, stats_out, score_ref, acc_ref, *scratch):
    order_ref = get_order(dense, order_in, scratch)
    own_blocks, head_size = qt_ref.shape[:2]
    for s in range(own_blocks):
        for h in range(heads):
            tile = q_ref[0, pl.ds(s * BLOCK, BLOCK), pl.ds(h * head_size, head_size)]
            qt_ref[s, :, pl.ds(h * BLOCK, BLOCK)] = tile.T
        acc, top, denom = attention(dense, s, 0, order_ref, kv_ref, qt_ref[s], score_ref, acc_ref)
        acc_out[s] = acc
        stats_out[s, 0:1] = top
        stats_out[s, 1:2] = denom


def last_kernel(heads, dense, qt_ref, order_in, kv_ref, acc_in, stats_in, out_hbm,
                out_ref, out_sems, score_ref, acc_ref, *scratch):
    order_ref = get_order(dense, order_in, scratch)
    own_blocks, head_size = qt_ref.shape[:2]
    copies = []
    for s in range(own_blocks):
        acc, top, denom = attention(dense, s, 1, order_ref, kv_ref, qt_ref[s], score_ref, acc_ref)
        other_top, other_denom = stats_in[s, 0:1], stats_in[s, 1:2]
        overall = jnp.maximum(top, other_top)
        scale, other_scale = jnp.exp2(top - overall), jnp.exp2(other_top - overall)
        share = 1.0 / (scale * denom + other_scale * other_denom)
        scale, other_scale = scale * share, other_scale * share
        for h in range(heads):
            rows, at = pl.ds(s * BLOCK, BLOCK), pl.ds(h * head_size, head_size)
            cut = slice(h * BLOCK, (h + 1) * BLOCK)
            one = acc[:, cut] * scale[:, cut] + acc_in[s, :, cut] * other_scale[:, cut]
            out_ref[0, rows, at] = one.astype(out_ref.dtype).T
            copy = pltpu.make_async_copy(out_ref.at[0, rows, at], out_hbm.at[0, rows, at], out_sems.at[s, h])
            copy.start()
            copies.append(copy)
    for copy in copies:
        copy.wait()


def swapper(rows, cols, own_blocks, per):
    def last_query(row, col):
        return (col * rows + row + 1) * own_blocks - 1

    def swap(piece, axis, flip, users):
        array, places = piece
        row_flip, col_flip = (flip, 0) if axis == "row" else (0, flip)
        places = [(r ^ row_flip, c ^ col_flip) for r, c in places]
        perm = []
        for row in range(rows):
            for col in range(cols):
                limit = max(last_query(*user) for user in users(row, col))
                if any(((row ^ r) * cols + (col ^ c)) * per <= limit for r, c in places):
                    perm.append(((row ^ row_flip) * cols + (col ^ col_flip), row * cols + col))
        return lax.ppermute(array, ("row", "col"), perm), places

    return swap


def join_pieces(pieces, transpose=True):
    vmem = pl.BlockSpec(memory_space=pltpu.VMEM)
    first = pieces[0][0]
    blocks = sum(array.shape[0] for array, _ in pieces)
    array = pl.pallas_call(
        functools.partial(join_kernel, transpose),
        out_shape=jax.ShapeDtypeStruct((blocks,) + first.shape[1:], first.dtype),
        in_specs=[vmem] * len(pieces),
        out_specs=vmem,
        compiler_params=pltpu.CompilerParams(vmem_limit_bytes=4 * 1024 * 1024),
        name="join",
    )(*(array for array, _ in pieces))
    return array, [place for _, places in pieces for place in places]


def together(pieces, *others):
    arrays = lax.optimization_barrier([array for array, _ in pieces] + list(others))
    held = [(array, places) for array, (_, places) in zip(arrays, pieces)]
    return (held, *arrays[len(held) :]) if others else held


def per_device(queries, keys, values, block_list, block_count):
    head_size = keys.shape[2]
    heads = queries.shape[2] // head_size
    own_blocks = queries.shape[1] // BLOCK
    per = keys.shape[1] // BLOCK
    rows = lax.axis_size("row")
    cols = lax.axis_size("col")
    panels, slots = block_list.shape[2:]
    blocks = panels * slots
    vmem = pl.BlockSpec(memory_space=pltpu.VMEM)
    smem = pl.BlockSpec(memory_space=pltpu.SMEM)
    anywhere = pl.BlockSpec(memory_space=pl.ANY)
    small = pltpu.CompilerParams(vmem_limit_bytes=4 * 1024 * 1024)
    swap = swapper(rows, cols, own_blocks, per)

    def everyone(row, col):
        return [(r, c) for r in range(rows) for c in range(cols)]

    def same_row(row, col):
        return [(row, c) for c in range(cols)]

    def same_chip(row, col):
        return [(row, col), (row, col ^ 1)]

    def across(piece):
        return [swap(piece, "col", flip, same_chip) for flip in range(CORES, cols, CORES)]

    def pair(piece):
        return swap(piece, "col", 1, lambda row, col: [(row, col)])

    shape = (per, BLOCK, head_size)
    packed = jnp.concatenate([keys.reshape(shape), values.reshape(shape)], axis=1)

    own = (packed, [(0, 0)])
    flip = rows // 2
    while flip > 2:
        came = swap(own, "row", flip, everyone)
        own = jnp.concatenate([own[0], came[0]]), own[1] + came[1]
        flip //= 2
    near, far, opposite = (swap(own, "row", flip, same_row) for flip in (1, 2, 3))
    own_across = across(own)
    early_places = [place for _, where in (own, *own_across, near, far, opposite) for place in where]
    late_places = [(r, c ^ flip) for flip in range(CORES, cols, CORES) for r, c in near[1] + far[1] + opposite[1]]
    places = [where + [(r, c ^ 1) for r, c in where] for where in (early_places, late_places)]

    longest = max(len(where) for where in places) * per
    dense = longest <= 16
    width = heads * BLOCK
    order_shape = (own_blocks, len(places), longest, width) if dense else (own_blocks, len(places), longest + 3)
    order = pl.pallas_call(
        functools.partial(prepare_kernel, per, places, dense),
        out_shape=jax.ShapeDtypeStruct(order_shape, jnp.int32),
        in_specs=[anywhere, anywhere],
        out_specs=vmem if dense else smem,
        scratch_shapes=[
            pltpu.SMEM((blocks,), jnp.int32),
            pltpu.SMEM((own_blocks, panels, slots), jnp.int32),
            pltpu.SMEM((own_blocks, panels), jnp.int32),
            pltpu.SemaphoreType.DMA((2,)),
        ],
        compiler_params=small,
        name="prepare",
    )(block_list, block_count)
    (opposite,), order = together([opposite], order)
    others = [near, far, opposite]
    last = across(join_pieces(others, False))
    halves = [join_pieces([own, *own_across]), join_pieces([near, far]), join_pieces([opposite])]
    early = join_pieces(halves + [pair(half) for half in halves], False)

    def attend(kernel, name, out_shape, out_specs, scratch, *args):
        held = args[2].shape[0] + args[2].shape[0] % 2
        scratch = scratch + [
            pltpu.VMEM((held, BLOCK, width), jnp.float32),
            pltpu.VMEM((head_size, width), jnp.float32),
        ]
        if not dense:
            scratch += [pltpu.SMEM(order.shape, jnp.int32), pltpu.SemaphoreType.DMA]
        return pl.pallas_call(
            functools.partial(kernel, heads, dense),
            out_shape=out_shape,
            in_specs=[vmem, vmem if dense else anywhere] + [vmem] * (len(args) - 2),
            out_specs=out_specs,
            scratch_shapes=scratch,
            compiler_params=pltpu.CompilerParams(vmem_limit_bytes=2 * held * BLOCK * width * 4 + 8 * 1024 * 1024),
            name=name,
        )(*args)

    parts = (
        jax.ShapeDtypeStruct((own_blocks, head_size, width), queries.dtype),
        jax.ShapeDtypeStruct((own_blocks, head_size, width), jnp.float32),
        jax.ShapeDtypeStruct((own_blocks, 2, width), jnp.float32),
    )
    queries_across, *part = attend(early_kernel, "early", parts, (vmem, vmem, vmem), [], queries, order, early[0])
    last, *part = together(last, *part)
    last = join_pieces(last)
    last = join_pieces([last, pair(last)], False)
    whole = jax.ShapeDtypeStruct(queries.shape, jnp.bfloat16)
    out_scratch = [pltpu.VMEM(queries.shape, jnp.bfloat16), pltpu.SemaphoreType.DMA((own_blocks, heads))]
    return attend(last_kernel, "last", whole, anywhere, out_scratch, queries_across, order, last[0], *part)


def solution(mesh):
    placed = (
        P(("groups", "col"), "row", None),
        P(("groups", "row"), "col", None),
        P(("groups", "row"), "col", None),
        P("groups", None, None, None),
        P("groups", None, None),
    )
    return jax.shard_map(
        per_device,
        mesh=mesh,
        in_specs=placed,
        out_specs=P(("groups", "col"), "row", None),
        check_vma=False,
    )
```

```python
import functools
import math

import jax
import jax.numpy as jnp
from jax import lax
from jax.experimental import pallas as pl
from jax.experimental.pallas import tpu as pltpu
from jax.sharding import PartitionSpec as P

BLOCK = 128
CORES = 2

floor_score = -1e30
floor_top = -1e20


def join_kernel(transpose, *refs):
    out_ref = refs[-1]
    first = 0
    for ref in refs[:-1]:
        if not transpose:
            out_ref[first : first + ref.shape[0]] = ref[...]
        for n in range(ref.shape[0] if transpose else 0):
            out_ref[first + n, :BLOCK, :] = ref[n, :BLOCK, :]
            out_ref[first + n, BLOCK:, :] = ref[n, BLOCK:, :].T
        first += ref.shape[0]


def prepare_kernel(per, places, dense, list_hbm, count_hbm, order_ref, active_ref, list_ref, count_ref, sems):
    own_blocks = order_ref.shape[0]
    panels, slots = list_ref.shape[1:]
    cols = lax.axis_size("col")
    col_index = lax.axis_index("col")
    row_index = lax.axis_index("row")
    first = row_index * own_blocks
    copies = (
        pltpu.make_async_copy(list_hbm.at[col_index, pl.ds(first, own_blocks)], list_ref, sems.at[0]),
        pltpu.make_async_copy(count_hbm.at[col_index, pl.ds(first, own_blocks)], count_ref, sems.at[1]),
    )
    for copy in copies:
        copy.start()
    for copy in copies:
        copy.wait()
    for s in range(own_blocks):
        diagonal = col_index * list_hbm.shape[1] + first + s
        for r in range(panels):
            for n in range(slots):
                active_ref[r * slots + n] = 0
            for n in reversed(range(slots)):
                active_ref[r * slots + list_ref[s, r, n]] = (n < count_ref[s, r]).astype(jnp.int32)
        for part, where in enumerate(places):
            total = jnp.int32(0)
            diagonal_slot = jnp.int32(-1)
            for n, (row_flip, col_flip) in enumerate(where):
                for k in range(per):
                    slot = n * per + k
                    block = ((row_index ^ row_flip) * cols + (col_index ^ col_flip)) * per + k
                    on_diagonal = block == diagonal
                    if dense:
                        reach = jnp.where(on_diagonal, 0, jnp.where(active_ref[block] > 0, BLOCK, -BLOCK))
                        order_ref[s, part, slot : slot + 1, :] = jnp.full((1, order_ref.shape[3]), reach, jnp.int32)
                        continue
                    order_ref[s, part, total] = slot
                    diagonal_slot = jnp.where(on_diagonal, slot, diagonal_slot)
                    total = total + jnp.where(on_diagonal, 0, active_ref[block])
            if dense:
                continue
            end = order_ref.shape[2] - 2
            here = diagonal_slot >= 0
            order_ref[s, part, total] = diagonal_slot
            order_ref[s, part, end + 1] = jnp.where(here, total, -1)
            total = total + here.astype(jnp.int32)
            order_ref[s, part, total] = 0
            order_ref[s, part, end] = total


def blockwise(array, fold):
    return fold(array.reshape(array.shape[0] // 8, 8, array.shape[1]), axis=0)


def dense_attention(reach, kv_ref, queries, score_ref):
    head_size, width = queries.shape
    slots = kv_ref.shape[0]
    factor = math.log2(math.e) / head_size**0.5
    key_at = lax.broadcasted_iota(jnp.int32, (BLOCK, width), 0)
    query_at = lax.broadcasted_iota(jnp.int32, (BLOCK, width), 1) % BLOCK
    keys = jnp.concatenate([kv_ref[slot, :BLOCK, :] for slot in range(slots)])
    found = jnp.dot(keys, queries, preferred_element_type=jnp.float32)
    top = jnp.full((8, width), floor_top, jnp.float32)
    for slot in range(slots):
        seen = query_at + reach[slot : slot + 1, :] >= key_at
        one = jnp.where(seen, found[slot * BLOCK : (slot + 1) * BLOCK], floor_score)
        score_ref[slot] = one
        top = jnp.maximum(top, blockwise(one, jnp.max))
    top = jnp.max(top, axis=0, keepdims=True) * factor
    denom = jnp.zeros((8, width), jnp.float32)
    rounded = []
    for slot in range(slots):
        one = jnp.exp2(score_ref[slot] * factor - top)
        denom = denom + blockwise(one, jnp.sum)
        rounded.append(one.astype(jnp.bfloat16))
    values = jnp.concatenate([kv_ref[slot, BLOCK:, :] for slot in range(slots)], axis=1)
    acc = jnp.dot(values, jnp.concatenate(rounded), preferred_element_type=jnp.float32)
    return acc, top, jnp.sum(denom, axis=0, keepdims=True)


def listed_attention(s, part, order_ref, kv_ref, queries, score_ref, acc_ref):
    head_size, width = queries.shape
    end = order_ref.shape[2] - 2
    factor = math.log2(math.e) / head_size**0.5
    total = order_ref[s, part, end]
    diagonal = order_ref[s, part, end + 1]
    pairs = (total + 1) // 2
    key_at = lax.broadcasted_iota(jnp.int32, (BLOCK, width), 0)
    query_at = lax.broadcasted_iota(jnp.int32, (BLOCK, width), 1) % BLOCK

    def score(p, top):
        pair = [order_ref[s, part, 2 * p + n] for n in range(2)]
        keys = jnp.concatenate([kv_ref[slot, :BLOCK, :] for slot in pair])
        found = jnp.dot(keys, queries, preferred_element_type=jnp.float32)
        for n in range(2):
            t = 2 * p + n
            reach = jnp.where(t == diagonal, 0, jnp.where(t < total, BLOCK, -BLOCK))
            one = jnp.where(query_at + reach >= key_at, found[n * BLOCK : (n + 1) * BLOCK], floor_score)
            score_ref[t] = one
            top = jnp.maximum(top, blockwise(one, jnp.max))
        return top

    top = lax.fori_loop(0, pairs, score, jnp.full((8, width), floor_top, jnp.float32))
    top = jnp.max(top, axis=0, keepdims=True) * factor
    acc_ref[...] = jnp.zeros_like(acc_ref)

    def mix(p, denom):
        pair = [order_ref[s, part, 2 * p + n] for n in range(2)]
        values = jnp.concatenate([kv_ref[slot, BLOCK:, :] for slot in pair], axis=1)
        weights = [jnp.exp2(score_ref[2 * p + n] * factor - top) for n in range(2)]
        rounded = jnp.concatenate([one.astype(jnp.bfloat16) for one in weights])
        acc_ref[...] += jnp.dot(values, rounded, preferred_element_type=jnp.float32)
        return denom + blockwise(weights[0] + weights[1], jnp.sum)

    denom = lax.fori_loop(0, pairs, mix, jnp.zeros((8, width), jnp.float32))
    return acc_ref[...], top, jnp.sum(denom, axis=0, keepdims=True)


def get_order(dense, order_ref, scratch):
    if dense:
        return order_ref
    held, sem = scratch
    copy = pltpu.make_async_copy(order_ref, held, sem)
    copy.start()
    copy.wait()
    return held


def attention(dense, s, part, order_ref, kv_ref, queries, score_ref, acc_ref):
    if dense:
        return dense_attention(order_ref[s, part], kv_ref, queries, score_ref)
    return listed_attention(s, part, order_ref, kv_ref, queries, score_ref, acc_ref)


def early_kernel(heads, dense, q_ref, order_in, kv_ref, qt_ref, acc_out, stats_out, score_ref, acc_ref, *scratch):
    order_ref = get_order(dense, order_in, scratch)
    own_blocks, head_size = qt_ref.shape[:2]
    for s in range(own_blocks):
        for h in range(heads):
            tile = q_ref[0, pl.ds(s * BLOCK, BLOCK), pl.ds(h * head_size, head_size)]
            qt_ref[s, :, pl.ds(h * BLOCK, BLOCK)] = tile.T
        acc, top, denom = attention(dense, s, 0, order_ref, kv_ref, qt_ref[s], score_ref, acc_ref)
        acc_out[s] = acc
        stats_out[s, 0:1] = top
        stats_out[s, 1:2] = denom


def last_kernel(heads, dense, qt_ref, order_in, kv_ref, acc_in, stats_in, out_hbm,
                out_ref, out_sems, score_ref, acc_ref, *scratch):
    order_ref = get_order(dense, order_in, scratch)
    own_blocks, head_size = qt_ref.shape[:2]
    copies = []
    for s in range(own_blocks):
        acc, top, denom = attention(dense, s, 1, order_ref, kv_ref, qt_ref[s], score_ref, acc_ref)
        other_top, other_denom = stats_in[s, 0:1], stats_in[s, 1:2]
        overall = jnp.maximum(top, other_top)
        scale, other_scale = jnp.exp2(top - overall), jnp.exp2(other_top - overall)
        share = 1.0 / (scale * denom + other_scale * other_denom)
        scale, other_scale = scale * share, other_scale * share
        for h in range(heads):
            rows, at = pl.ds(s * BLOCK, BLOCK), pl.ds(h * head_size, head_size)
            cut = slice(h * BLOCK, (h + 1) * BLOCK)
            one = acc[:, cut] * scale[:, cut] + acc_in[s, :, cut] * other_scale[:, cut]
            out_ref[0, rows, at] = one.astype(out_ref.dtype).T
            copy = pltpu.make_async_copy(out_ref.at[0, rows, at], out_hbm.at[0, rows, at], out_sems.at[s, h])
            copy.start()
            copies.append(copy)
    for copy in copies:
        copy.wait()


def swap(piece, axis, flip):
    array, places = piece
    came = lax.ppermute(array, axis, [(i, i ^ flip) for i in range(lax.axis_size(axis))])
    if axis == "row":
        return came, [(r ^ flip, c) for r, c in places]
    return came, [(r, c ^ flip) for r, c in places]


def join_pieces(pieces, transpose=True):
    vmem = pl.BlockSpec(memory_space=pltpu.VMEM)
    first = pieces[0][0]
    blocks = sum(array.shape[0] for array, _ in pieces)
    array = pl.pallas_call(
        functools.partial(join_kernel, transpose),
        out_shape=jax.ShapeDtypeStruct((blocks,) + first.shape[1:], first.dtype),
        in_specs=[vmem] * len(pieces),
        out_specs=vmem,
        compiler_params=pltpu.CompilerParams(vmem_limit_bytes=4 * 1024 * 1024),
        name="join",
    )(*(array for array, _ in pieces))
    return array, [place for _, places in pieces for place in places]


def together(pieces, *others):
    arrays = lax.optimization_barrier([array for array, _ in pieces] + list(others))
    held = [(array, places) for array, (_, places) in zip(arrays, pieces)]
    return (held, *arrays[len(held) :]) if others else held


def across(piece, cols):
    pieces = [piece]
    flip = CORES
    while flip < cols:
        pieces += [swap(one, "col", flip) for one in pieces]
        flip *= 2
    return pieces[1:]


def per_device(queries, keys, values, block_list, block_count):
    head_size = keys.shape[2]
    heads = queries.shape[2] // head_size
    own_blocks = queries.shape[1] // BLOCK
    per = keys.shape[1] // BLOCK
    rows = lax.axis_size("row")
    cols = lax.axis_size("col")
    panels, slots = block_list.shape[2:]
    blocks = panels * slots
    vmem = pl.BlockSpec(memory_space=pltpu.VMEM)
    smem = pl.BlockSpec(memory_space=pltpu.SMEM)
    anywhere = pl.BlockSpec(memory_space=pl.ANY)
    small = pltpu.CompilerParams(vmem_limit_bytes=4 * 1024 * 1024)

    shape = (per, BLOCK, head_size)
    packed = jnp.concatenate([keys.reshape(shape), values.reshape(shape)], axis=1)

    own = (packed, [(0, 0)])
    flip = rows // 2
    while flip > 2:
        came = swap(own, "row", flip)
        own = jnp.concatenate([own[0], came[0]]), own[1] + came[1]
        flip //= 2
    near, far, opposite = (swap(own, "row", flip) for flip in (1, 2, 3))
    own_across = across(own, cols)
    near_across = [swap(piece, "row", 1) for piece in own_across]
    early_places = [place for _, where in (own, *own_across, near, *near_across, far, opposite) for place in where]
    late_places = [(r, c ^ flip) for flip in range(CORES, cols, CORES) for r, c in far[1] + opposite[1]]
    places = [where + [(r, c ^ 1) for r, c in where] for where in (early_places, late_places)]

    longest = max(len(where) for where in places) * per
    dense = longest <= 16
    width = heads * BLOCK
    order_shape = (own_blocks, len(places), longest, width) if dense else (own_blocks, len(places), longest + 3)
    order = pl.pallas_call(
        functools.partial(prepare_kernel, per, places, dense),
        out_shape=jax.ShapeDtypeStruct(order_shape, jnp.int32),
        in_specs=[anywhere, anywhere],
        out_specs=vmem if dense else smem,
        scratch_shapes=[
            pltpu.SMEM((blocks,), jnp.int32),
            pltpu.SMEM((own_blocks, panels, slots), jnp.int32),
            pltpu.SMEM((own_blocks, panels), jnp.int32),
            pltpu.SemaphoreType.DMA((2,)),
        ],
        compiler_params=small,
        name="prepare",
    )(block_list, block_count)
    (opposite,), order = together([opposite], order)
    last = across(join_pieces([far, opposite], False), cols)
    halves = [join_pieces([own, *own_across, near]), join_pieces([*near_across, far, opposite])]
    early = join_pieces(halves + [swap(half, "col", 1) for half in halves], False)

    def attend(kernel, name, out_shape, out_specs, scratch, *args):
        held = args[2].shape[0] + args[2].shape[0] % 2
        scratch = scratch + [
            pltpu.VMEM((held, BLOCK, width), jnp.float32),
            pltpu.VMEM((head_size, width), jnp.float32),
        ]
        if not dense:
            scratch += [pltpu.SMEM(order.shape, jnp.int32), pltpu.SemaphoreType.DMA]
        return pl.pallas_call(
            functools.partial(kernel, heads, dense),
            out_shape=out_shape,
            in_specs=[vmem, vmem if dense else anywhere] + [vmem] * (len(args) - 2),
            out_specs=out_specs,
            scratch_shapes=scratch,
            compiler_params=pltpu.CompilerParams(vmem_limit_bytes=2 * held * BLOCK * width * 4 + 8 * 1024 * 1024),
            name=name,
        )(*args)

    parts = (
        jax.ShapeDtypeStruct((own_blocks, head_size, width), queries.dtype),
        jax.ShapeDtypeStruct((own_blocks, head_size, width), jnp.float32),
        jax.ShapeDtypeStruct((own_blocks, 2, width), jnp.float32),
    )
    queries_across, *part = attend(early_kernel, "early", parts, (vmem, vmem, vmem), [], queries, order, early[0])
    last = join_pieces(last)
    last = join_pieces([last, swap(last, "col", 1)], False)
    whole = jax.ShapeDtypeStruct(queries.shape, jnp.bfloat16)
    out_scratch = [pltpu.VMEM(queries.shape, jnp.bfloat16), pltpu.SemaphoreType.DMA((own_blocks, heads))]
    return attend(last_kernel, "last", whole, anywhere, out_scratch, queries_across, order, last[0], *part)


def solution(mesh):
    placed = (
        P(("groups", "col"), "row", None),
        P(("groups", "row"), "col", None),
        P(("groups", "row"), "col", None),
        P("groups", None, None, None),
        P("groups", None, None),
    )
    return jax.shard_map(
        per_device,
        mesh=mesh,
        in_specs=placed,
        out_specs=P(("groups", "col"), "row", None),
        check_vma=False,
    )
```

```python
import functools
import math

import jax
import jax.numpy as jnp
from jax import lax
from jax.experimental import pallas as pl
from jax.experimental.pallas import tpu as pltpu
from jax.sharding import PartitionSpec as P

BLOCK = 128
CORES = 2

floor_score = -1e30
floor_top = -1e20


def join_kernel(transpose, *refs):
    out_ref = refs[-1]
    first = 0
    for ref in refs[:-1]:
        if not transpose:
            out_ref[first : first + ref.shape[0]] = ref[...]
        for n in range(ref.shape[0] if transpose else 0):
            out_ref[first + n, :BLOCK, :] = ref[n, :BLOCK, :]
            out_ref[first + n, BLOCK:, :] = ref[n, BLOCK:, :].T
        first += ref.shape[0]


def prepare_kernel(per, places, dense, list_hbm, count_hbm, order_ref, active_ref, list_ref, count_ref, sems):
    own_blocks = order_ref.shape[0]
    panels, slots = list_ref.shape[1:]
    cols = lax.axis_size("col")
    col_index = lax.axis_index("col")
    row_index = lax.axis_index("row")
    first = row_index * own_blocks
    copies = (
        pltpu.make_async_copy(list_hbm.at[col_index, pl.ds(first, own_blocks)], list_ref, sems.at[0]),
        pltpu.make_async_copy(count_hbm.at[col_index, pl.ds(first, own_blocks)], count_ref, sems.at[1]),
    )
    for copy in copies:
        copy.start()
    for copy in copies:
        copy.wait()
    for s in range(own_blocks):
        diagonal = col_index * list_hbm.shape[1] + first + s
        for r in range(panels):
            for n in range(slots):
                active_ref[r * slots + n] = 0
            for n in reversed(range(slots)):
                active_ref[r * slots + list_ref[s, r, n]] = (n < count_ref[s, r]).astype(jnp.int32)
        for part, where in enumerate(places):
            total = jnp.int32(0)
            diagonal_slot = jnp.int32(-1)
            for n, (row_flip, col_flip) in enumerate(where):
                for k in range(per):
                    slot = n * per + k
                    block = ((row_index ^ row_flip) * cols + (col_index ^ col_flip)) * per + k
                    on_diagonal = block == diagonal
                    if dense:
                        reach = jnp.where(on_diagonal, 0, jnp.where(active_ref[block] > 0, BLOCK, -BLOCK))
                        order_ref[s, part, slot : slot + 1, :] = jnp.full((1, order_ref.shape[3]), reach, jnp.int32)
                        continue
                    order_ref[s, part, total] = slot
                    diagonal_slot = jnp.where(on_diagonal, slot, diagonal_slot)
                    total = total + jnp.where(on_diagonal, 0, active_ref[block])
            if dense:
                continue
            end = order_ref.shape[2] - 2
            here = diagonal_slot >= 0
            order_ref[s, part, total] = diagonal_slot
            order_ref[s, part, end + 1] = jnp.where(here, total, -1)
            total = total + here.astype(jnp.int32)
            order_ref[s, part, total] = 0
            order_ref[s, part, end] = total


def blockwise(array, fold):
    return fold(array.reshape(array.shape[0] // 8, 8, array.shape[1]), axis=0)


def dense_attention(reach, kv_ref, queries, score_ref):
    head_size, width = queries.shape
    slots = kv_ref.shape[0]
    factor = math.log2(math.e) / head_size**0.5
    key_at = lax.broadcasted_iota(jnp.int32, (BLOCK, width), 0)
    query_at = lax.broadcasted_iota(jnp.int32, (BLOCK, width), 1) % BLOCK
    keys = jnp.concatenate([kv_ref[slot, :BLOCK, :] for slot in range(slots)])
    found = jnp.dot(keys, queries, preferred_element_type=jnp.float32)
    top = jnp.full((8, width), floor_top, jnp.float32)
    for slot in range(slots):
        seen = query_at + reach[slot : slot + 1, :] >= key_at
        one = jnp.where(seen, found[slot * BLOCK : (slot + 1) * BLOCK], floor_score)
        score_ref[slot] = one
        top = jnp.maximum(top, blockwise(one, jnp.max))
    top = jnp.max(top, axis=0, keepdims=True) * factor
    denom = jnp.zeros((8, width), jnp.float32)
    rounded = []
    for slot in range(slots):
        one = jnp.exp2(score_ref[slot] * factor - top)
        denom = denom + blockwise(one, jnp.sum)
        rounded.append(one.astype(jnp.bfloat16))
    values = jnp.concatenate([kv_ref[slot, BLOCK:, :] for slot in range(slots)], axis=1)
    acc = jnp.dot(values, jnp.concatenate(rounded), preferred_element_type=jnp.float32)
    return acc, top, jnp.sum(denom, axis=0, keepdims=True)


def listed_attention(s, part, order_ref, kv_ref, queries, score_ref, acc_ref):
    head_size, width = queries.shape
    end = order_ref.shape[2] - 2
    factor = math.log2(math.e) / head_size**0.5
    total = order_ref[s, part, end]
    diagonal = order_ref[s, part, end + 1]
    pairs = (total + 1) // 2
    key_at = lax.broadcasted_iota(jnp.int32, (BLOCK, width), 0)
    query_at = lax.broadcasted_iota(jnp.int32, (BLOCK, width), 1) % BLOCK

    def score(p, top):
        pair = [order_ref[s, part, 2 * p + n] for n in range(2)]
        keys = jnp.concatenate([kv_ref[slot, :BLOCK, :] for slot in pair])
        found = jnp.dot(keys, queries, preferred_element_type=jnp.float32)
        for n in range(2):
            t = 2 * p + n
            reach = jnp.where(t == diagonal, 0, jnp.where(t < total, BLOCK, -BLOCK))
            one = jnp.where(query_at + reach >= key_at, found[n * BLOCK : (n + 1) * BLOCK], floor_score)
            score_ref[t] = one
            top = jnp.maximum(top, blockwise(one, jnp.max))
        return top

    top = lax.fori_loop(0, pairs, score, jnp.full((8, width), floor_top, jnp.float32))
    top = jnp.max(top, axis=0, keepdims=True) * factor
    acc_ref[...] = jnp.zeros_like(acc_ref)

    def mix(p, denom):
        pair = [order_ref[s, part, 2 * p + n] for n in range(2)]
        values = jnp.concatenate([kv_ref[slot, BLOCK:, :] for slot in pair], axis=1)
        weights = [jnp.exp2(score_ref[2 * p + n] * factor - top) for n in range(2)]
        rounded = jnp.concatenate([one.astype(jnp.bfloat16) for one in weights])
        acc_ref[...] += jnp.dot(values, rounded, preferred_element_type=jnp.float32)
        return denom + blockwise(weights[0] + weights[1], jnp.sum)

    denom = lax.fori_loop(0, pairs, mix, jnp.zeros((8, width), jnp.float32))
    return acc_ref[...], top, jnp.sum(denom, axis=0, keepdims=True)


def get_order(dense, order_ref, scratch):
    if dense:
        return order_ref
    held, sem = scratch
    copy = pltpu.make_async_copy(order_ref, held, sem)
    copy.start()
    copy.wait()
    return held


def attention(dense, s, part, order_ref, kv_ref, queries, score_ref, acc_ref):
    if dense:
        return dense_attention(order_ref[s, part], kv_ref, queries, score_ref)
    return listed_attention(s, part, order_ref, kv_ref, queries, score_ref, acc_ref)


def turn_kernel(heads, q_ref, qt_ref):
    own_blocks, head_size = qt_ref.shape[:2]
    for s in range(own_blocks):
        for h in range(heads):
            tile = q_ref[0, pl.ds(s * BLOCK, BLOCK), pl.ds(h * head_size, head_size)]
            qt_ref[s, :, pl.ds(h * BLOCK, BLOCK)] = tile.T


def early_kernel(heads, dense, qt_ref, order_in, kv_ref, acc_out, stats_out, score_ref, acc_ref, *scratch):
    order_ref = get_order(dense, order_in, scratch)
    for s in range(qt_ref.shape[0]):
        acc, top, denom = attention(dense, s, 0, order_ref, kv_ref, qt_ref[s], score_ref, acc_ref)
        acc_out[s] = acc
        stats_out[s, 0:1] = top
        stats_out[s, 1:2] = denom


def last_kernel(per, places, heads, dense, qt_ref, order_in, kv_ref, acc_in, stats_in, out_hbm,
                out_ref, out_sems, score_ref, acc_ref, *scratch):
    order_ref = get_order(dense, order_in, scratch)
    own_blocks, head_size, width = qt_ref.shape
    rows, cols = lax.axis_size("row"), lax.axis_size("col")
    row_index, col_index = lax.axis_index("row"), lax.axis_index("col")
    sources = [(row_index ^ row_flip) * cols + (col_index ^ col_flip) for row_flip, col_flip in places]
    earliest = functools.reduce(jnp.minimum, sources) * per

    for s in range(own_blocks):
        useful = earliest <= (col_index * rows + row_index) * own_blocks + s

        def finish(acc, scale):
            copies = []
            for h in range(heads):
                at = pl.ds(h * head_size, head_size)
                cut = slice(h * BLOCK, (h + 1) * BLOCK)
                one = acc_in[s, :, cut] * scale[:, cut]
                if acc is not None:
                    one = one + acc[:, cut]
                out_ref[0, pl.ds(s * BLOCK, BLOCK), at] = one.astype(out_ref.dtype).T
                place = (0, pl.ds(s * BLOCK, BLOCK), at)
                copies.append(pltpu.make_async_copy(out_ref.at[place], out_hbm.at[place], out_sems.at[s, h]))
                copies[-1].start()
            for copy in copies:
                copy.wait()

        @pl.when(useful)
        def _():
            acc, top, denom = attention(dense, s, 1, order_ref, kv_ref, qt_ref[s], score_ref, acc_ref)
            other_top, other_denom = stats_in[s, 0:1], stats_in[s, 1:2]
            overall = jnp.maximum(top, other_top)
            scale, other_scale = jnp.exp2(top - overall), jnp.exp2(other_top - overall)
            share = 1.0 / (scale * denom + other_scale * other_denom)
            finish(acc * (scale * share), other_scale * share)

        @pl.when(jnp.logical_not(useful))
        def _():
            finish(None, 1.0 / stats_in[s, 1:2])


def swap(piece, axis, flip):
    array, places = piece
    came = lax.ppermute(array, axis, [(i, i ^ flip) for i in range(lax.axis_size(axis))])
    if axis == "row":
        return came, [(r ^ flip, c) for r, c in places]
    return came, [(r, c ^ flip) for r, c in places]


def join_pieces(pieces, transpose=True):
    vmem = pl.BlockSpec(memory_space=pltpu.VMEM)
    first = pieces[0][0]
    blocks = sum(array.shape[0] for array, _ in pieces)
    array = pl.pallas_call(
        functools.partial(join_kernel, transpose),
        out_shape=jax.ShapeDtypeStruct((blocks,) + first.shape[1:], first.dtype),
        in_specs=[vmem] * len(pieces),
        out_specs=vmem,
        compiler_params=pltpu.CompilerParams(vmem_limit_bytes=4 * 1024 * 1024),
        name="join",
    )(*(array for array, _ in pieces))
    return array, [place for _, places in pieces for place in places]


def together(pieces, *others):
    arrays = lax.optimization_barrier([array for array, _ in pieces] + list(others))
    held = [(array, places) for array, (_, places) in zip(arrays, pieces)]
    return (held, *arrays[len(held) :]) if others else held


def across(piece, cols):
    pieces = [piece]
    flip = CORES
    while flip < cols:
        pieces += [swap(one, "col", flip) for one in pieces]
        flip *= 2
    return pieces[1:]


def per_device(queries, keys, values, block_list, block_count):
    head_size = keys.shape[2]
    heads = queries.shape[2] // head_size
    own_blocks = queries.shape[1] // BLOCK
    per = keys.shape[1] // BLOCK
    rows = lax.axis_size("row")
    cols = lax.axis_size("col")
    panels, slots = block_list.shape[2:]
    blocks = panels * slots
    vmem = pl.BlockSpec(memory_space=pltpu.VMEM)
    smem = pl.BlockSpec(memory_space=pltpu.SMEM)
    anywhere = pl.BlockSpec(memory_space=pl.ANY)
    small = pltpu.CompilerParams(vmem_limit_bytes=4 * 1024 * 1024)

    shape = (per, BLOCK, head_size)
    packed = jnp.concatenate([keys.reshape(shape), values.reshape(shape)], axis=1)

    own = (packed, [(0, 0)])
    flip = rows // 2
    while flip > 2:
        came = swap(own, "row", flip)
        own = jnp.concatenate([own[0], came[0]]), own[1] + came[1]
        flip //= 2
    near, far, opposite = (swap(own, "row", flip) for flip in (1, 2, 3))
    own_across = across(own, cols)
    near_across = [swap(piece, "row", 1) for piece in own_across]
    early_places = [place for _, where in (own, *own_across, near, *near_across, far, opposite) for place in where]
    late_places = [(r, c ^ flip) for flip in range(CORES, cols, CORES) for r, c in far[1] + opposite[1]]
    places = [where + [(r, c ^ 1) for r, c in where] for where in (early_places, late_places)]

    longest = max(len(where) for where in places) * per
    dense = longest <= 16
    width = heads * BLOCK
    order_shape = (own_blocks, len(places), longest, width) if dense else (own_blocks, len(places), longest + 3)
    order = pl.pallas_call(
        functools.partial(prepare_kernel, per, places, dense),
        out_shape=jax.ShapeDtypeStruct(order_shape, jnp.int32),
        in_specs=[anywhere, anywhere],
        out_specs=vmem if dense else smem,
        scratch_shapes=[
            pltpu.SMEM((blocks,), jnp.int32),
            pltpu.SMEM((own_blocks, panels, slots), jnp.int32),
            pltpu.SMEM((own_blocks, panels), jnp.int32),
            pltpu.SemaphoreType.DMA((2,)),
        ],
        compiler_params=small,
        name="prepare",
    )(block_list, block_count)
    (opposite,), order = together([opposite], order)
    last = across(join_pieces([far, opposite], False), cols)
    halves = [join_pieces([own, *own_across, near]), join_pieces([*near_across, far, opposite])]
    early = join_pieces(halves + [swap(half, "col", 1) for half in halves], False)

    def attend(kernel, name, out_shape, out_specs, scratch, *args):
        held = args[2].shape[0] + args[2].shape[0] % 2
        scratch = scratch + [
            pltpu.VMEM((held, BLOCK, width), jnp.float32),
            pltpu.VMEM((head_size, width), jnp.float32),
        ]
        if not dense:
            scratch += [pltpu.SMEM(order.shape, jnp.int32), pltpu.SemaphoreType.DMA]
        return pl.pallas_call(
            functools.partial(kernel, heads, dense),
            out_shape=out_shape,
            in_specs=[vmem, vmem if dense else anywhere] + [vmem] * (len(args) - 2),
            out_specs=out_specs,
            scratch_shapes=scratch,
            compiler_params=pltpu.CompilerParams(vmem_limit_bytes=2 * held * BLOCK * width * 4 + 8 * 1024 * 1024),
            name=name,
        )(*args)

    queries_across = pl.pallas_call(
        functools.partial(turn_kernel, heads),
        out_shape=jax.ShapeDtypeStruct((own_blocks, head_size, width), queries.dtype),
        in_specs=[vmem],
        out_specs=vmem,
        compiler_params=small,
        name="turn",
    )(queries)
    last, queries_across = together(last, queries_across)
    parts = (
        jax.ShapeDtypeStruct((own_blocks, head_size, width), jnp.float32),
        jax.ShapeDtypeStruct((own_blocks, 2, width), jnp.float32),
    )
    part = attend(early_kernel, "early", parts, (vmem, vmem), [], queries_across, order, early[0])
    last = join_pieces(last)
    last = join_pieces([last, swap(last, "col", 1)], False)
    whole = jax.ShapeDtypeStruct(queries.shape, jnp.bfloat16)
    out_scratch = [pltpu.VMEM(queries.shape, jnp.bfloat16), pltpu.SemaphoreType.DMA((own_blocks, heads))]
    end = functools.partial(last_kernel, per, places[1])
    return attend(end, "last", whole, anywhere, out_scratch, queries_across, order, last[0], *part)


def solution(mesh):
    placed = (
        P(("groups", "col"), "row", None),
        P(("groups", "row"), "col", None),
        P(("groups", "row"), "col", None),
        P("groups", None, None, None),
        P("groups", None, None),
    )
    return jax.shard_map(
        per_device,
        mesh=mesh,
        in_specs=placed,
        out_specs=P(("groups", "col"), "row", None),
        check_vma=False,
    )
```

```python
import functools
import math

import jax
import jax.numpy as jnp
from jax import lax
from jax.experimental import pallas as pl
from jax.experimental.pallas import tpu as pltpu
from jax.sharding import PartitionSpec as P

BLOCK = 128
CORES = 2

floor_score = -1e30
floor_top = -1e20


def join_kernel(transpose, *refs):
    out_ref = refs[-1]
    first = 0
    for ref in refs[:-1]:
        if not transpose:
            out_ref[first : first + ref.shape[0]] = ref[...]
        for n in range(ref.shape[0] if transpose else 0):
            out_ref[first + n, :BLOCK, :] = ref[n, :BLOCK, :]
            out_ref[first + n, BLOCK:, :] = ref[n, BLOCK:, :].T
        first += ref.shape[0]


def prepare_kernel(per, places, dense, list_hbm, count_hbm, order_ref, active_ref, list_ref, count_ref, sems):
    own_blocks = order_ref.shape[0]
    panels, slots = list_ref.shape[1:]
    cols = lax.axis_size("col")
    col_index = lax.axis_index("col")
    row_index = lax.axis_index("row")
    first = row_index * own_blocks
    copies = (
        pltpu.make_async_copy(list_hbm.at[col_index, pl.ds(first, own_blocks)], list_ref, sems.at[0]),
        pltpu.make_async_copy(count_hbm.at[col_index, pl.ds(first, own_blocks)], count_ref, sems.at[1]),
    )
    for copy in copies:
        copy.start()
    for copy in copies:
        copy.wait()
    for s in range(own_blocks):
        diagonal = col_index * list_hbm.shape[1] + first + s
        for r in range(panels):
            for n in range(slots):
                active_ref[r * slots + n] = 0
            for n in reversed(range(slots)):
                active_ref[r * slots + list_ref[s, r, n]] = (n < count_ref[s, r]).astype(jnp.int32)
        for part, where in enumerate(places):
            total = jnp.int32(0)
            diagonal_slot = jnp.int32(-1)
            for n, (row_flip, col_flip) in enumerate(where):
                for k in range(per):
                    slot = n * per + k
                    block = ((row_index ^ row_flip) * cols + (col_index ^ col_flip)) * per + k
                    on_diagonal = block == diagonal
                    if dense:
                        reach = jnp.where(on_diagonal, 0, jnp.where(active_ref[block] > 0, BLOCK, -BLOCK))
                        order_ref[s, part, slot : slot + 1, :] = jnp.full((1, order_ref.shape[3]), reach, jnp.int32)
                        continue
                    order_ref[s, part, total] = slot
                    diagonal_slot = jnp.where(on_diagonal, slot, diagonal_slot)
                    total = total + jnp.where(on_diagonal, 0, active_ref[block])
            if dense:
                continue
            end = order_ref.shape[2] - 2
            here = diagonal_slot >= 0
            order_ref[s, part, total] = diagonal_slot
            order_ref[s, part, end + 1] = jnp.where(here, total, -1)
            total = total + here.astype(jnp.int32)
            order_ref[s, part, total] = 0
            order_ref[s, part, end] = total


def blockwise(array, fold):
    return fold(array.reshape(array.shape[0] // 8, 8, array.shape[1]), axis=0)


def dense_attention(reach, kv_ref, queries, score_ref):
    head_size, width = queries.shape
    slots = kv_ref.shape[0]
    factor = math.log2(math.e) / head_size**0.5
    key_at = lax.broadcasted_iota(jnp.int32, (BLOCK, width), 0)
    query_at = lax.broadcasted_iota(jnp.int32, (BLOCK, width), 1) % BLOCK
    keys = jnp.concatenate([kv_ref[slot, :BLOCK, :] for slot in range(slots)])
    found = jnp.dot(keys, queries, preferred_element_type=jnp.float32)
    top = jnp.full((8, width), floor_top, jnp.float32)
    for slot in range(slots):
        seen = query_at + reach[slot : slot + 1, :] >= key_at
        one = jnp.where(seen, found[slot * BLOCK : (slot + 1) * BLOCK], floor_score)
        score_ref[slot] = one
        top = jnp.maximum(top, blockwise(one, jnp.max))
    top = jnp.max(top, axis=0, keepdims=True) * factor
    denom = jnp.zeros((8, width), jnp.float32)
    rounded = []
    for slot in range(slots):
        one = jnp.exp2(score_ref[slot] * factor - top)
        denom = denom + blockwise(one, jnp.sum)
        rounded.append(one.astype(jnp.bfloat16))
    values = jnp.concatenate([kv_ref[slot, BLOCK:, :] for slot in range(slots)], axis=1)
    acc = jnp.dot(values, jnp.concatenate(rounded), preferred_element_type=jnp.float32)
    return acc, top, jnp.sum(denom, axis=0, keepdims=True)


def listed_attention(s, part, order_ref, kv_ref, queries, score_ref, acc_ref):
    head_size, width = queries.shape
    end = order_ref.shape[2] - 2
    factor = math.log2(math.e) / head_size**0.5
    total = order_ref[s, part, end]
    diagonal = order_ref[s, part, end + 1]
    pairs = (total + 1) // 2
    key_at = lax.broadcasted_iota(jnp.int32, (BLOCK, width), 0)
    query_at = lax.broadcasted_iota(jnp.int32, (BLOCK, width), 1) % BLOCK

    def score(p, top):
        pair = [order_ref[s, part, 2 * p + n] for n in range(2)]
        keys = jnp.concatenate([kv_ref[slot, :BLOCK, :] for slot in pair])
        found = jnp.dot(keys, queries, preferred_element_type=jnp.float32)
        for n in range(2):
            t = 2 * p + n
            reach = jnp.where(t == diagonal, 0, jnp.where(t < total, BLOCK, -BLOCK))
            one = jnp.where(query_at + reach >= key_at, found[n * BLOCK : (n + 1) * BLOCK], floor_score)
            score_ref[t] = one
            top = jnp.maximum(top, blockwise(one, jnp.max))
        return top

    top = lax.fori_loop(0, pairs, score, jnp.full((8, width), floor_top, jnp.float32))
    top = jnp.max(top, axis=0, keepdims=True) * factor
    acc_ref[...] = jnp.zeros_like(acc_ref)

    def mix(p, denom):
        pair = [order_ref[s, part, 2 * p + n] for n in range(2)]
        values = jnp.concatenate([kv_ref[slot, BLOCK:, :] for slot in pair], axis=1)
        weights = [jnp.exp2(score_ref[2 * p + n] * factor - top) for n in range(2)]
        rounded = jnp.concatenate([one.astype(jnp.bfloat16) for one in weights])
        acc_ref[...] += jnp.dot(values, rounded, preferred_element_type=jnp.float32)
        return denom + blockwise(weights[0] + weights[1], jnp.sum)

    denom = lax.fori_loop(0, pairs, mix, jnp.zeros((8, width), jnp.float32))
    return acc_ref[...], top, jnp.sum(denom, axis=0, keepdims=True)


def get_order(dense, order_ref, scratch):
    if dense:
        return order_ref
    held, sem = scratch
    copy = pltpu.make_async_copy(order_ref, held, sem)
    copy.start()
    copy.wait()
    return held


def attention(dense, s, part, order_ref, kv_ref, queries, score_ref, acc_ref):
    if dense:
        return dense_attention(order_ref[s, part], kv_ref, queries, score_ref)
    return listed_attention(s, part, order_ref, kv_ref, queries, score_ref, acc_ref)


def turn_kernel(heads, q_ref, qt_ref):
    own_blocks, head_size = qt_ref.shape[:2]
    for s in range(own_blocks):
        for h in range(heads):
            tile = q_ref[0, pl.ds(s * BLOCK, BLOCK), pl.ds(h * head_size, head_size)]
            qt_ref[s, :, pl.ds(h * BLOCK, BLOCK)] = tile.T


def early_kernel(heads, dense, qt_ref, order_in, kv_ref, acc_out, stats_out, score_ref, acc_ref, *scratch):
    order_ref = get_order(dense, order_in, scratch)
    for s in range(qt_ref.shape[0]):
        acc, top, denom = attention(dense, s, 0, order_ref, kv_ref, qt_ref[s], score_ref, acc_ref)
        acc_out[s] = acc
        stats_out[s, 0:1] = top
        stats_out[s, 1:2] = denom


def last_kernel(per, places, heads, dense, qt_ref, order_in, kv_ref, acc_in, stats_in, out_hbm,
                out_ref, out_sems, score_ref, acc_ref, *scratch):
    order_ref = get_order(dense, order_in, scratch)
    own_blocks, head_size, width = qt_ref.shape
    rows, cols = lax.axis_size("row"), lax.axis_size("col")
    row_index, col_index = lax.axis_index("row"), lax.axis_index("col")
    sources = [(row_index ^ row_flip) * cols + (col_index ^ col_flip) for row_flip, col_flip in places]
    earliest = functools.reduce(jnp.minimum, sources) * per

    for s in range(own_blocks):
        useful = earliest <= (col_index * rows + row_index) * own_blocks + s

        def finish(acc, scale):
            copies = []
            for h in range(heads):
                at = pl.ds(h * head_size, head_size)
                cut = slice(h * BLOCK, (h + 1) * BLOCK)
                one = acc_in[s, :, cut] * scale[:, cut]
                if acc is not None:
                    one = one + acc[:, cut]
                out_ref[0, pl.ds(s * BLOCK, BLOCK), at] = one.astype(out_ref.dtype).T
                place = (0, pl.ds(s * BLOCK, BLOCK), at)
                copies.append(pltpu.make_async_copy(out_ref.at[place], out_hbm.at[place], out_sems.at[s, h]))
                copies[-1].start()
            for copy in copies:
                copy.wait()

        @pl.when(useful)
        def _():
            acc, top, denom = attention(dense, s, 1, order_ref, kv_ref, qt_ref[s], score_ref, acc_ref)
            other_top, other_denom = stats_in[s, 0:1], stats_in[s, 1:2]
            overall = jnp.maximum(top, other_top)
            scale, other_scale = jnp.exp2(top - overall), jnp.exp2(other_top - overall)
            share = 1.0 / (scale * denom + other_scale * other_denom)
            finish(acc * (scale * share), other_scale * share)

        @pl.when(jnp.logical_not(useful))
        def _():
            finish(None, 1.0 / stats_in[s, 1:2])


def swap(piece, axis, flip):
    array, places = piece
    came = lax.ppermute(array, axis, [(i, i ^ flip) for i in range(lax.axis_size(axis))])
    if axis == "row":
        return came, [(r ^ flip, c) for r, c in places]
    return came, [(r, c ^ flip) for r, c in places]


def join_pieces(pieces, transpose=True):
    vmem = pl.BlockSpec(memory_space=pltpu.VMEM)
    first = pieces[0][0]
    blocks = sum(array.shape[0] for array, _ in pieces)
    array = pl.pallas_call(
        functools.partial(join_kernel, transpose),
        out_shape=jax.ShapeDtypeStruct((blocks,) + first.shape[1:], first.dtype),
        in_specs=[vmem] * len(pieces),
        out_specs=vmem,
        compiler_params=pltpu.CompilerParams(vmem_limit_bytes=4 * 1024 * 1024),
        name="join",
    )(*(array for array, _ in pieces))
    return array, [place for _, places in pieces for place in places]


def together(pieces, *others):
    arrays = lax.optimization_barrier([array for array, _ in pieces] + list(others))
    held = [(array, places) for array, (_, places) in zip(arrays, pieces)]
    return (held, *arrays[len(held) :]) if others else held


def across(piece, cols):
    pieces = [piece]
    flip = CORES
    while flip < cols:
        pieces += [swap(one, "col", flip) for one in pieces]
        flip *= 2
    return pieces[1:]


def per_device(queries, keys, values, block_list, block_count):
    head_size = keys.shape[2]
    heads = queries.shape[2] // head_size
    own_blocks = queries.shape[1] // BLOCK
    per = keys.shape[1] // BLOCK
    rows = lax.axis_size("row")
    cols = lax.axis_size("col")
    panels, slots = block_list.shape[2:]
    blocks = panels * slots
    vmem = pl.BlockSpec(memory_space=pltpu.VMEM)
    smem = pl.BlockSpec(memory_space=pltpu.SMEM)
    anywhere = pl.BlockSpec(memory_space=pl.ANY)
    small = pltpu.CompilerParams(vmem_limit_bytes=4 * 1024 * 1024)

    shape = (per, BLOCK, head_size)
    packed = jnp.concatenate([keys.reshape(shape), values.reshape(shape)], axis=1)

    own = (packed, [(0, 0)])
    flip = rows // 2
    while flip > 2:
        came = swap(own, "row", flip)
        own = jnp.concatenate([own[0], came[0]]), own[1] + came[1]
        flip //= 2
    near, far, opposite = (swap(own, "row", flip) for flip in (1, 2, 3))
    own_across = across(own, cols)
    near_across = [swap(piece, "row", 1) for piece in own_across]
    early_places = [place for _, where in (own, *own_across, near, *near_across, far, opposite) for place in where]
    late_places = [(r, c ^ flip) for flip in range(CORES, cols, CORES) for r, c in far[1] + opposite[1]]
    places = [where + [(r, c ^ 1) for r, c in where] for where in (early_places, late_places)]

    longest = max(len(where) for where in places) * per
    dense = longest <= 16
    width = heads * BLOCK
    order_shape = (own_blocks, len(places), longest, width) if dense else (own_blocks, len(places), longest + 3)
    order = pl.pallas_call(
        functools.partial(prepare_kernel, per, places, dense),
        out_shape=jax.ShapeDtypeStruct(order_shape, jnp.int32),
        in_specs=[anywhere, anywhere],
        out_specs=vmem if dense else smem,
        scratch_shapes=[
            pltpu.SMEM((blocks,), jnp.int32),
            pltpu.SMEM((own_blocks, panels, slots), jnp.int32),
            pltpu.SMEM((own_blocks, panels), jnp.int32),
            pltpu.SemaphoreType.DMA((2,)),
        ],
        compiler_params=small,
        name="prepare",
    )(block_list, block_count)
    (far,), order = together([far], order)
    last = across(far, cols) + across(opposite, cols)
    halves = [join_pieces([own, *own_across, near]), join_pieces([*near_across, far, opposite])]
    early = join_pieces(halves + [swap(half, "col", 1) for half in halves], False)

    def attend(kernel, name, out_shape, out_specs, scratch, *args):
        held = args[2].shape[0] + args[2].shape[0] % 2
        scratch = scratch + [
            pltpu.VMEM((held, BLOCK, width), jnp.float32),
            pltpu.VMEM((head_size, width), jnp.float32),
        ]
        if not dense:
            scratch += [pltpu.SMEM(order.shape, jnp.int32), pltpu.SemaphoreType.DMA]
        return pl.pallas_call(
            functools.partial(kernel, heads, dense),
            out_shape=out_shape,
            in_specs=[vmem, vmem if dense else anywhere] + [vmem] * (len(args) - 2),
            out_specs=out_specs,
            scratch_shapes=scratch,
            compiler_params=pltpu.CompilerParams(vmem_limit_bytes=2 * held * BLOCK * width * 4 + 8 * 1024 * 1024),
            name=name,
        )(*args)

    queries_across = pl.pallas_call(
        functools.partial(turn_kernel, heads),
        out_shape=jax.ShapeDtypeStruct((own_blocks, head_size, width), queries.dtype),
        in_specs=[vmem],
        out_specs=vmem,
        compiler_params=small,
        name="turn",
    )(queries)
    last, queries_across = together(last, queries_across)
    parts = (
        jax.ShapeDtypeStruct((own_blocks, head_size, width), jnp.float32),
        jax.ShapeDtypeStruct((own_blocks, 2, width), jnp.float32),
    )
    part = attend(early_kernel, "early", parts, (vmem, vmem), [], queries_across, order, early[0])
    last = join_pieces(last)
    last = join_pieces([last, swap(last, "col", 1)], False)
    whole = jax.ShapeDtypeStruct(queries.shape, jnp.bfloat16)
    out_scratch = [pltpu.VMEM(queries.shape, jnp.bfloat16), pltpu.SemaphoreType.DMA((own_blocks, heads))]
    end = functools.partial(last_kernel, per, places[1])
    return attend(end, "last", whole, anywhere, out_scratch, queries_across, order, last[0], *part)


def solution(mesh):
    placed = (
        P(("groups", "col"), "row", None),
        P(("groups", "row"), "col", None),
        P(("groups", "row"), "col", None),
        P("groups", None, None, None),
        P("groups", None, None),
    )
    return jax.shard_map(
        per_device,
        mesh=mesh,
        in_specs=placed,
        out_specs=P(("groups", "col"), "row", None),
        check_vma=False,
    )
```

```python
import functools
import math

import jax
import jax.numpy as jnp
from jax import lax
from jax.experimental import pallas as pl
from jax.experimental.pallas import tpu as pltpu
from jax.sharding import PartitionSpec as P

BLOCK = 128
CORES = 2

floor_score = -1e30
floor_top = -1e20


def join_kernel(transpose, *refs):
    out_ref = refs[-1]
    first = 0
    for ref in refs[:-1]:
        if not transpose:
            out_ref[first : first + ref.shape[0]] = ref[...]
        for n in range(ref.shape[0] if transpose else 0):
            out_ref[first + n, :BLOCK, :] = ref[n, :BLOCK, :]
            out_ref[first + n, BLOCK:, :] = ref[n, BLOCK:, :].T
        first += ref.shape[0]


def prepare_kernel(per, places, dense, list_hbm, count_hbm, order_ref, active_ref, list_ref, count_ref, sems):
    own_blocks = order_ref.shape[0]
    panels, slots = list_ref.shape[1:]
    cols = lax.axis_size("col")
    col_index = lax.axis_index("col")
    row_index = lax.axis_index("row")
    first = row_index * own_blocks
    copies = (
        pltpu.make_async_copy(list_hbm.at[col_index, pl.ds(first, own_blocks)], list_ref, sems.at[0]),
        pltpu.make_async_copy(count_hbm.at[col_index, pl.ds(first, own_blocks)], count_ref, sems.at[1]),
    )
    for copy in copies:
        copy.start()
    for copy in copies:
        copy.wait()
    for s in range(own_blocks):
        diagonal = col_index * list_hbm.shape[1] + first + s
        for r in range(panels):
            for n in range(slots):
                active_ref[r * slots + n] = 0
            for n in reversed(range(slots)):
                active_ref[r * slots + list_ref[s, r, n]] = (n < count_ref[s, r]).astype(jnp.int32)
        for part, where in enumerate(places):
            total = jnp.int32(0)
            diagonal_slot = jnp.int32(-1)
            for n, (row_flip, col_flip) in enumerate(where):
                for k in range(per):
                    slot = n * per + k
                    block = ((row_index ^ row_flip) * cols + (col_index ^ col_flip)) * per + k
                    on_diagonal = block == diagonal
                    if dense:
                        reach = jnp.where(on_diagonal, 0, jnp.where(active_ref[block] > 0, BLOCK, -BLOCK))
                        order_ref[s, part, slot : slot + 1, :] = jnp.full((1, order_ref.shape[3]), reach, jnp.int32)
                        continue
                    order_ref[s, part, total] = slot
                    diagonal_slot = jnp.where(on_diagonal, slot, diagonal_slot)
                    total = total + jnp.where(on_diagonal, 0, active_ref[block])
            if dense:
                continue
            end = order_ref.shape[2] - 2
            here = diagonal_slot >= 0
            order_ref[s, part, total] = diagonal_slot
            order_ref[s, part, end + 1] = jnp.where(here, total, -1)
            total = total + here.astype(jnp.int32)
            order_ref[s, part, total] = 0
            order_ref[s, part, end] = total


def blockwise(array, fold):
    return fold(array.reshape(array.shape[0] // 8, 8, array.shape[1]), axis=0)


def dense_attention(reach, kv_ref, queries, score_ref):
    head_size, width = queries.shape
    slots = kv_ref.shape[0]
    factor = math.log2(math.e) / head_size**0.5
    key_at = lax.broadcasted_iota(jnp.int32, (BLOCK, width), 0)
    query_at = lax.broadcasted_iota(jnp.int32, (BLOCK, width), 1) % BLOCK
    keys = jnp.concatenate([kv_ref[slot, :BLOCK, :] for slot in range(slots)])
    found = jnp.dot(keys, queries, preferred_element_type=jnp.float32)
    top = jnp.full((8, width), floor_top, jnp.float32)
    for slot in range(slots):
        seen = query_at + reach[slot : slot + 1, :] >= key_at
        one = jnp.where(seen, found[slot * BLOCK : (slot + 1) * BLOCK], floor_score)
        score_ref[slot] = one
        top = jnp.maximum(top, blockwise(one, jnp.max))
    top = jnp.max(top, axis=0, keepdims=True) * factor
    denom = jnp.zeros((8, width), jnp.float32)
    rounded = []
    for slot in range(slots):
        one = jnp.exp2(score_ref[slot] * factor - top)
        denom = denom + blockwise(one, jnp.sum)
        rounded.append(one.astype(jnp.bfloat16))
    values = jnp.concatenate([kv_ref[slot, BLOCK:, :] for slot in range(slots)], axis=1)
    acc = jnp.dot(values, jnp.concatenate(rounded), preferred_element_type=jnp.float32)
    return acc, top, jnp.sum(denom, axis=0, keepdims=True)


def listed_attention(s, part, order_ref, kv_ref, queries, score_ref, acc_ref):
    head_size, width = queries.shape
    end = order_ref.shape[2] - 2
    factor = math.log2(math.e) / head_size**0.5
    total = order_ref[s, part, end]
    diagonal = order_ref[s, part, end + 1]
    pairs = (total + 1) // 2
    key_at = lax.broadcasted_iota(jnp.int32, (BLOCK, width), 0)
    query_at = lax.broadcasted_iota(jnp.int32, (BLOCK, width), 1) % BLOCK

    def score(p, top):
        pair = [order_ref[s, part, 2 * p + n] for n in range(2)]
        keys = jnp.concatenate([kv_ref[slot, :BLOCK, :] for slot in pair])
        found = jnp.dot(keys, queries, preferred_element_type=jnp.float32)
        for n in range(2):
            t = 2 * p + n
            reach = jnp.where(t == diagonal, 0, jnp.where(t < total, BLOCK, -BLOCK))
            one = jnp.where(query_at + reach >= key_at, found[n * BLOCK : (n + 1) * BLOCK], floor_score)
            score_ref[t] = one
            top = jnp.maximum(top, blockwise(one, jnp.max))
        return top

    top = lax.fori_loop(0, pairs, score, jnp.full((8, width), floor_top, jnp.float32))
    top = jnp.max(top, axis=0, keepdims=True) * factor
    acc_ref[...] = jnp.zeros_like(acc_ref)

    def mix(p, denom):
        pair = [order_ref[s, part, 2 * p + n] for n in range(2)]
        values = jnp.concatenate([kv_ref[slot, BLOCK:, :] for slot in pair], axis=1)
        weights = [jnp.exp2(score_ref[2 * p + n] * factor - top) for n in range(2)]
        rounded = jnp.concatenate([one.astype(jnp.bfloat16) for one in weights])
        acc_ref[...] += jnp.dot(values, rounded, preferred_element_type=jnp.float32)
        return denom + blockwise(weights[0] + weights[1], jnp.sum)

    denom = lax.fori_loop(0, pairs, mix, jnp.zeros((8, width), jnp.float32))
    return acc_ref[...], top, jnp.sum(denom, axis=0, keepdims=True)


def get_order(dense, order_ref, scratch):
    if dense:
        return order_ref
    held, sem = scratch
    copy = pltpu.make_async_copy(order_ref, held, sem)
    copy.start()
    copy.wait()
    return held


def attention(dense, s, part, order_ref, kv_ref, queries, score_ref, acc_ref):
    if dense:
        return dense_attention(order_ref[s, part], kv_ref, queries, score_ref)
    return listed_attention(s, part, order_ref, kv_ref, queries, score_ref, acc_ref)


def turn_kernel(heads, q_ref, qt_ref):
    own_blocks, head_size = qt_ref.shape[:2]
    for s in range(own_blocks):
        for h in range(heads):
            tile = q_ref[0, pl.ds(s * BLOCK, BLOCK), pl.ds(h * head_size, head_size)]
            qt_ref[s, :, pl.ds(h * BLOCK, BLOCK)] = tile.T


def early_kernel(heads, dense, qt_ref, order_in, kv_ref, acc_out, stats_out, score_ref, acc_ref, *scratch):
    order_ref = get_order(dense, order_in, scratch)
    for s in range(qt_ref.shape[0]):
        acc, top, denom = attention(dense, s, 0, order_ref, kv_ref, qt_ref[s], score_ref, acc_ref)
        acc_out[s] = acc
        stats_out[s, 0:1] = top
        stats_out[s, 1:2] = denom


def last_kernel(per, places, heads, dense, qt_ref, order_in, kv_ref, acc_in, stats_in, out_hbm,
                out_ref, out_sems, score_ref, acc_ref, *scratch):
    order_ref = get_order(dense, order_in, scratch)
    own_blocks, head_size, width = qt_ref.shape
    rows, cols = lax.axis_size("row"), lax.axis_size("col")
    row_index, col_index = lax.axis_index("row"), lax.axis_index("col")
    sources = [(row_index ^ row_flip) * cols + (col_index ^ col_flip) for row_flip, col_flip in places]
    earliest = functools.reduce(jnp.minimum, sources) * per

    for s in range(own_blocks):
        useful = earliest <= (col_index * rows + row_index) * own_blocks + s

        def finish(acc, scale):
            copies = []
            for h in range(heads):
                at = pl.ds(h * head_size, head_size)
                cut = slice(h * BLOCK, (h + 1) * BLOCK)
                one = acc_in[s, :, cut] * scale[:, cut]
                if acc is not None:
                    one = one + acc[:, cut]
                out_ref[0, pl.ds(s * BLOCK, BLOCK), at] = one.astype(out_ref.dtype).T
                place = (0, pl.ds(s * BLOCK, BLOCK), at)
                copies.append(pltpu.make_async_copy(out_ref.at[place], out_hbm.at[place], out_sems.at[s, h]))
                copies[-1].start()
            for copy in copies:
                copy.wait()

        @pl.when(useful)
        def _():
            acc, top, denom = attention(dense, s, 1, order_ref, kv_ref, qt_ref[s], score_ref, acc_ref)
            other_top, other_denom = stats_in[s, 0:1], stats_in[s, 1:2]
            overall = jnp.maximum(top, other_top)
            scale, other_scale = jnp.exp2(top - overall), jnp.exp2(other_top - overall)
            share = 1.0 / (scale * denom + other_scale * other_denom)
            finish(acc * (scale * share), other_scale * share)

        @pl.when(jnp.logical_not(useful))
        def _():
            finish(None, 1.0 / stats_in[s, 1:2])


def swap(piece, axis, flip):
    array, places = piece
    came = lax.ppermute(array, axis, [(i, i ^ flip) for i in range(lax.axis_size(axis))])
    if axis == "row":
        return came, [(r ^ flip, c) for r, c in places]
    return came, [(r, c ^ flip) for r, c in places]


def join_pieces(pieces, transpose=True):
    vmem = pl.BlockSpec(memory_space=pltpu.VMEM)
    first = pieces[0][0]
    blocks = sum(array.shape[0] for array, _ in pieces)
    array = pl.pallas_call(
        functools.partial(join_kernel, transpose),
        out_shape=jax.ShapeDtypeStruct((blocks,) + first.shape[1:], first.dtype),
        in_specs=[vmem] * len(pieces),
        out_specs=vmem,
        compiler_params=pltpu.CompilerParams(vmem_limit_bytes=4 * 1024 * 1024),
        name="join",
    )(*(array for array, _ in pieces))
    return array, [place for _, places in pieces for place in places]


def together(pieces, *others):
    arrays = lax.optimization_barrier([array for array, _ in pieces] + list(others))
    held = [(array, places) for array, (_, places) in zip(arrays, pieces)]
    return (held, *arrays[len(held) :]) if others else held


def across(piece, cols):
    pieces = [piece]
    flip = CORES
    while flip < cols:
        pieces += [swap(one, "col", flip) for one in pieces]
        flip *= 2
    return pieces[1:]


def per_device(queries, keys, values, block_list, block_count):
    head_size = keys.shape[2]
    heads = queries.shape[2] // head_size
    own_blocks = queries.shape[1] // BLOCK
    per = keys.shape[1] // BLOCK
    rows = lax.axis_size("row")
    cols = lax.axis_size("col")
    panels, slots = block_list.shape[2:]
    blocks = panels * slots
    vmem = pl.BlockSpec(memory_space=pltpu.VMEM)
    smem = pl.BlockSpec(memory_space=pltpu.SMEM)
    anywhere = pl.BlockSpec(memory_space=pl.ANY)
    small = pltpu.CompilerParams(vmem_limit_bytes=4 * 1024 * 1024)

    shape = (per, BLOCK, head_size)
    packed = jnp.concatenate([keys.reshape(shape), values.reshape(shape)], axis=1)

    own = (packed, [(0, 0)])
    flip = rows // 2
    while flip > 2:
        came = swap(own, "row", flip)
        own = jnp.concatenate([own[0], came[0]]), own[1] + came[1]
        flip //= 2
    near, far, opposite = (swap(own, "row", flip) for flip in (1, 2, 3))
    own_across = across(own, cols)
    near_across = [swap(piece, "row", 1) for piece in own_across]
    early_places = [place for _, where in (own, *own_across, near, *near_across, far, opposite) for place in where]
    late_places = [(r, c ^ flip) for flip in range(CORES, cols, CORES) for r, c in far[1] + opposite[1]]
    places = [where + [(r, c ^ 1) for r, c in where] for where in (early_places, late_places)]

    longest = max(len(where) for where in places) * per
    dense = longest <= 16
    width = heads * BLOCK
    order_shape = (own_blocks, len(places), longest, width) if dense else (own_blocks, len(places), longest + 3)
    order = pl.pallas_call(
        functools.partial(prepare_kernel, per, places, dense),
        out_shape=jax.ShapeDtypeStruct(order_shape, jnp.int32),
        in_specs=[anywhere, anywhere],
        out_specs=vmem if dense else smem,
        scratch_shapes=[
            pltpu.SMEM((blocks,), jnp.int32),
            pltpu.SMEM((own_blocks, panels, slots), jnp.int32),
            pltpu.SMEM((own_blocks, panels), jnp.int32),
            pltpu.SemaphoreType.DMA((2,)),
        ],
        compiler_params=small,
        name="prepare",
    )(block_list, block_count)
    (far,), order = together([far], order)
    last = across(far, cols) + across(opposite, cols)
    halves = [join_pieces([own, *own_across]), join_pieces([near, *near_across]), join_pieces([far, opposite])]
    early = join_pieces(halves + [swap(half, "col", 1) for half in halves], False)

    def attend(kernel, name, out_shape, out_specs, scratch, *args):
        held = args[2].shape[0] + args[2].shape[0] % 2
        scratch = scratch + [
            pltpu.VMEM((held, BLOCK, width), jnp.float32),
            pltpu.VMEM((head_size, width), jnp.float32),
        ]
        if not dense:
            scratch += [pltpu.SMEM(order.shape, jnp.int32), pltpu.SemaphoreType.DMA]
        return pl.pallas_call(
            functools.partial(kernel, heads, dense),
            out_shape=out_shape,
            in_specs=[vmem, vmem if dense else anywhere] + [vmem] * (len(args) - 2),
            out_specs=out_specs,
            scratch_shapes=scratch,
            compiler_params=pltpu.CompilerParams(vmem_limit_bytes=2 * held * BLOCK * width * 4 + 8 * 1024 * 1024),
            name=name,
        )(*args)

    queries_across = pl.pallas_call(
        functools.partial(turn_kernel, heads),
        out_shape=jax.ShapeDtypeStruct((own_blocks, head_size, width), queries.dtype),
        in_specs=[vmem],
        out_specs=vmem,
        compiler_params=small,
        name="turn",
    )(queries)
    last, queries_across = together(last, queries_across)
    parts = (
        jax.ShapeDtypeStruct((own_blocks, head_size, width), jnp.float32),
        jax.ShapeDtypeStruct((own_blocks, 2, width), jnp.float32),
    )
    part = attend(early_kernel, "early", parts, (vmem, vmem), [], queries_across, order, early[0])
    last = join_pieces(last)
    last_pair, *part = together([swap(last, "col", 1)], *part)
    last = join_pieces([last, *last_pair], False)
    whole = jax.ShapeDtypeStruct(queries.shape, jnp.bfloat16)
    out_scratch = [pltpu.VMEM(queries.shape, jnp.bfloat16), pltpu.SemaphoreType.DMA((own_blocks, heads))]
    end = functools.partial(last_kernel, per, places[1])
    return attend(end, "last", whole, anywhere, out_scratch, queries_across, order, last[0], *part)


def solution(mesh):
    placed = (
        P(("groups", "col"), "row", None),
        P(("groups", "row"), "col", None),
        P(("groups", "row"), "col", None),
        P("groups", None, None, None),
        P("groups", None, None),
    )
    return jax.shard_map(
        per_device,
        mesh=mesh,
        in_specs=placed,
        out_specs=P(("groups", "col"), "row", None),
        check_vma=False,
    )
```

```python
import functools
import math

import jax
import jax.numpy as jnp
from jax import lax
from jax.experimental import pallas as pl
from jax.experimental.pallas import tpu as pltpu
from jax.sharding import PartitionSpec as P

BLOCK = 128
CORES = 2

floor_score = -1e30
floor_top = -1e20


def join_kernel(transpose, *refs):
    out_ref = refs[-1]
    first = 0
    for ref in refs[:-1]:
        if not transpose:
            out_ref[first : first + ref.shape[0]] = ref[...]
        for n in range(ref.shape[0] if transpose else 0):
            out_ref[first + n, :BLOCK, :] = ref[n, :BLOCK, :]
            out_ref[first + n, BLOCK:, :] = ref[n, BLOCK:, :].T
        first += ref.shape[0]


def prepare_kernel(per, places, dense, list_hbm, count_hbm, order_ref, active_ref, list_ref, count_ref, sems):
    own_blocks = order_ref.shape[0]
    panels, slots = list_ref.shape[1:]
    cols = lax.axis_size("col")
    col_index = lax.axis_index("col")
    row_index = lax.axis_index("row")
    first = row_index * own_blocks
    copies = (
        pltpu.make_async_copy(list_hbm.at[col_index, pl.ds(first, own_blocks)], list_ref, sems.at[0]),
        pltpu.make_async_copy(count_hbm.at[col_index, pl.ds(first, own_blocks)], count_ref, sems.at[1]),
    )
    for copy in copies:
        copy.start()
    for copy in copies:
        copy.wait()
    for s in range(own_blocks):
        diagonal = col_index * list_hbm.shape[1] + first + s
        for r in range(panels):
            for n in range(slots):
                active_ref[r * slots + n] = 0
            for n in reversed(range(slots)):
                active_ref[r * slots + list_ref[s, r, n]] = (n < count_ref[s, r]).astype(jnp.int32)
        for part, where in enumerate(places):
            total = jnp.int32(0)
            diagonal_slot = jnp.int32(-1)
            for n, (row_flip, col_flip) in enumerate(where):
                for k in range(per):
                    slot = n * per + k
                    block = ((row_index ^ row_flip) * cols + (col_index ^ col_flip)) * per + k
                    on_diagonal = block == diagonal
                    if dense:
                        reach = jnp.where(on_diagonal, 0, jnp.where(active_ref[block] > 0, BLOCK, -BLOCK))
                        order_ref[s, part, slot : slot + 1, :] = jnp.full((1, order_ref.shape[3]), reach, jnp.int32)
                        continue
                    order_ref[s, part, total] = slot
                    diagonal_slot = jnp.where(on_diagonal, slot, diagonal_slot)
                    total = total + jnp.where(on_diagonal, 0, active_ref[block])
            if dense:
                continue
            end = order_ref.shape[2] - 2
            here = diagonal_slot >= 0
            order_ref[s, part, total] = diagonal_slot
            order_ref[s, part, end + 1] = jnp.where(here, total, -1)
            total = total + here.astype(jnp.int32)
            order_ref[s, part, total] = 0
            order_ref[s, part, end] = total


def blockwise(array, fold):
    return fold(array.reshape(array.shape[0] // 8, 8, array.shape[1]), axis=0)


def dense_attention(reach, kv_ref, queries, score_ref):
    head_size, width = queries.shape
    slots = kv_ref.shape[0]
    factor = math.log2(math.e) / head_size**0.5
    key_at = lax.broadcasted_iota(jnp.int32, (BLOCK, width), 0)
    query_at = lax.broadcasted_iota(jnp.int32, (BLOCK, width), 1) % BLOCK
    keys = jnp.concatenate([kv_ref[slot, :BLOCK, :] for slot in range(slots)])
    found = jnp.dot(keys, queries, preferred_element_type=jnp.float32)
    top = jnp.full((8, width), floor_top, jnp.float32)
    for slot in range(slots):
        seen = query_at + reach[slot : slot + 1, :] >= key_at
        one = jnp.where(seen, found[slot * BLOCK : (slot + 1) * BLOCK], floor_score)
        score_ref[slot] = one
        top = jnp.maximum(top, blockwise(one, jnp.max))
    top = jnp.max(top, axis=0, keepdims=True) * factor
    denom = jnp.zeros((8, width), jnp.float32)
    rounded = []
    for slot in range(slots):
        one = jnp.exp2(score_ref[slot] * factor - top)
        denom = denom + blockwise(one, jnp.sum)
        rounded.append(one.astype(jnp.bfloat16))
    values = jnp.concatenate([kv_ref[slot, BLOCK:, :] for slot in range(slots)], axis=1)
    acc = jnp.dot(values, jnp.concatenate(rounded), preferred_element_type=jnp.float32)
    return acc, top, jnp.sum(denom, axis=0, keepdims=True)


def listed_attention(s, part, order_ref, kv_ref, queries, score_ref, acc_ref):
    head_size, width = queries.shape
    end = order_ref.shape[2] - 2
    factor = math.log2(math.e) / head_size**0.5
    total = order_ref[s, part, end]
    diagonal = order_ref[s, part, end + 1]
    pairs = (total + 1) // 2
    key_at = lax.broadcasted_iota(jnp.int32, (BLOCK, width), 0)
    query_at = lax.broadcasted_iota(jnp.int32, (BLOCK, width), 1) % BLOCK

    def score(p, top):
        pair = [order_ref[s, part, 2 * p + n] for n in range(2)]
        keys = jnp.concatenate([kv_ref[slot, :BLOCK, :] for slot in pair])
        found = jnp.dot(keys, queries, preferred_element_type=jnp.float32)
        for n in range(2):
            t = 2 * p + n
            reach = jnp.where(t == diagonal, 0, jnp.where(t < total, BLOCK, -BLOCK))
            one = jnp.where(query_at + reach >= key_at, found[n * BLOCK : (n + 1) * BLOCK], floor_score)
            score_ref[t] = one
            top = jnp.maximum(top, blockwise(one, jnp.max))
        return top

    top = lax.fori_loop(0, pairs, score, jnp.full((8, width), floor_top, jnp.float32))
    top = jnp.max(top, axis=0, keepdims=True) * factor
    acc_ref[...] = jnp.zeros_like(acc_ref)

    def mix(p, denom):
        pair = [order_ref[s, part, 2 * p + n] for n in range(2)]
        values = jnp.concatenate([kv_ref[slot, BLOCK:, :] for slot in pair], axis=1)
        weights = [jnp.exp2(score_ref[2 * p + n] * factor - top) for n in range(2)]
        rounded = jnp.concatenate([one.astype(jnp.bfloat16) for one in weights])
        acc_ref[...] += jnp.dot(values, rounded, preferred_element_type=jnp.float32)
        return denom + blockwise(weights[0] + weights[1], jnp.sum)

    denom = lax.fori_loop(0, pairs, mix, jnp.zeros((8, width), jnp.float32))
    return acc_ref[...], top, jnp.sum(denom, axis=0, keepdims=True)


def get_order(dense, order_ref, scratch):
    if dense:
        return order_ref
    held, sem = scratch
    copy = pltpu.make_async_copy(order_ref, held, sem)
    copy.start()
    copy.wait()
    return held


def attention(dense, s, part, order_ref, kv_ref, queries, score_ref, acc_ref):
    if dense:
        return dense_attention(order_ref[s, part], kv_ref, queries, score_ref)
    return listed_attention(s, part, order_ref, kv_ref, queries, score_ref, acc_ref)


def turn_kernel(heads, q_ref, qt_ref):
    own_blocks, head_size = qt_ref.shape[:2]
    for s in range(own_blocks):
        for h in range(heads):
            tile = q_ref[0, pl.ds(s * BLOCK, BLOCK), pl.ds(h * head_size, head_size)]
            qt_ref[s, :, pl.ds(h * BLOCK, BLOCK)] = tile.T


def early_kernel(heads, dense, qt_ref, order_in, kv_ref, acc_out, stats_out, score_ref, acc_ref, *scratch):
    order_ref = get_order(dense, order_in, scratch)
    for s in range(qt_ref.shape[0]):
        acc, top, denom = attention(dense, s, 0, order_ref, kv_ref, qt_ref[s], score_ref, acc_ref)
        acc_out[s] = acc
        stats_out[s, 0:1] = top
        stats_out[s, 1:2] = denom


def last_kernel(per, places, heads, dense, qt_ref, order_in, kv_ref, acc_in, stats_in, out_hbm,
                out_ref, out_sems, score_ref, acc_ref, *scratch):
    order_ref = get_order(dense, order_in, scratch)
    own_blocks, head_size, width = qt_ref.shape
    rows, cols = lax.axis_size("row"), lax.axis_size("col")
    row_index, col_index = lax.axis_index("row"), lax.axis_index("col")
    sources = [(row_index ^ row_flip) * cols + (col_index ^ col_flip) for row_flip, col_flip in places]
    earliest = functools.reduce(jnp.minimum, sources) * per

    for s in range(own_blocks):
        useful = earliest <= (col_index * rows + row_index) * own_blocks + s

        def finish(acc, scale):
            copies = []
            for h in range(heads):
                at = pl.ds(h * head_size, head_size)
                cut = slice(h * BLOCK, (h + 1) * BLOCK)
                one = acc_in[s, :, cut] * scale[:, cut]
                if acc is not None:
                    one = one + acc[:, cut]
                out_ref[0, pl.ds(s * BLOCK, BLOCK), at] = one.astype(out_ref.dtype).T
                place = (0, pl.ds(s * BLOCK, BLOCK), at)
                copies.append(pltpu.make_async_copy(out_ref.at[place], out_hbm.at[place], out_sems.at[s, h]))
                copies[-1].start()
            for copy in copies:
                copy.wait()

        @pl.when(useful)
        def _():
            acc, top, denom = attention(dense, s, 1, order_ref, kv_ref, qt_ref[s], score_ref, acc_ref)
            other_top, other_denom = stats_in[s, 0:1], stats_in[s, 1:2]
            overall = jnp.maximum(top, other_top)
            scale, other_scale = jnp.exp2(top - overall), jnp.exp2(other_top - overall)
            share = 1.0 / (scale * denom + other_scale * other_denom)
            finish(acc * (scale * share), other_scale * share)

        @pl.when(jnp.logical_not(useful))
        def _():
            finish(None, 1.0 / stats_in[s, 1:2])


def swap(piece, axis, flip):
    array, places = piece
    came = lax.ppermute(array, axis, [(i, i ^ flip) for i in range(lax.axis_size(axis))])
    if axis == "row":
        return came, [(r ^ flip, c) for r, c in places]
    return came, [(r, c ^ flip) for r, c in places]


def join_pieces(pieces, transpose=True):
    vmem = pl.BlockSpec(memory_space=pltpu.VMEM)
    first = pieces[0][0]
    blocks = sum(array.shape[0] for array, _ in pieces)
    array = pl.pallas_call(
        functools.partial(join_kernel, transpose),
        out_shape=jax.ShapeDtypeStruct((blocks,) + first.shape[1:], first.dtype),
        in_specs=[vmem] * len(pieces),
        out_specs=vmem,
        compiler_params=pltpu.CompilerParams(vmem_limit_bytes=4 * 1024 * 1024),
        name="join",
    )(*(array for array, _ in pieces))
    return array, [place for _, places in pieces for place in places]


def together(pieces, *others):
    arrays = lax.optimization_barrier([array for array, _ in pieces] + list(others))
    held = [(array, places) for array, (_, places) in zip(arrays, pieces)]
    return (held, *arrays[len(held) :]) if others else held


def across(piece, cols):
    pieces = [piece]
    flip = CORES
    while flip < cols:
        pieces += [swap(one, "col", flip) for one in pieces]
        flip *= 2
    return pieces[1:]


def per_device(queries, keys, values, block_list, block_count):
    head_size = keys.shape[2]
    heads = queries.shape[2] // head_size
    own_blocks = queries.shape[1] // BLOCK
    per = keys.shape[1] // BLOCK
    rows = lax.axis_size("row")
    cols = lax.axis_size("col")
    panels, slots = block_list.shape[2:]
    blocks = panels * slots
    vmem = pl.BlockSpec(memory_space=pltpu.VMEM)
    smem = pl.BlockSpec(memory_space=pltpu.SMEM)
    anywhere = pl.BlockSpec(memory_space=pl.ANY)
    small = pltpu.CompilerParams(vmem_limit_bytes=4 * 1024 * 1024)

    shape = (per, BLOCK, head_size)
    packed = jnp.concatenate([keys.reshape(shape), values.reshape(shape)], axis=1)

    own = (packed, [(0, 0)])
    flip = rows // 2
    while flip > 2:
        came = swap(own, "row", flip)
        own = jnp.concatenate([own[0], came[0]]), own[1] + came[1]
        flip //= 2
    near, far, opposite = (swap(own, "row", flip) for flip in (1, 2, 3))
    own_across = across(own, cols)
    near_across = [swap(piece, "row", 1) for piece in own_across]
    early_places = [place for _, where in (own, *own_across, near, *near_across, far, opposite) for place in where]
    late_places = [(r, c ^ flip) for flip in range(CORES, cols, CORES) for r, c in far[1] + opposite[1]]
    places = [where + [(r, c ^ 1) for r, c in where] for where in (early_places, late_places)]

    longest = max(len(where) for where in places) * per
    dense = longest <= 16
    width = heads * BLOCK
    order_shape = (own_blocks, len(places), longest, width) if dense else (own_blocks, len(places), longest + 3)
    order = pl.pallas_call(
        functools.partial(prepare_kernel, per, places, dense),
        out_shape=jax.ShapeDtypeStruct(order_shape, jnp.int32),
        in_specs=[anywhere, anywhere],
        out_specs=vmem if dense else smem,
        scratch_shapes=[
            pltpu.SMEM((blocks,), jnp.int32),
            pltpu.SMEM((own_blocks, panels, slots), jnp.int32),
            pltpu.SMEM((own_blocks, panels), jnp.int32),
            pltpu.SemaphoreType.DMA((2,)),
        ],
        compiler_params=small,
        name="prepare",
    )(block_list, block_count)
    (far,), order = together([far], order)
    far_across, queries = together(across(far, cols), queries)
    last = far_across + across(opposite, cols)
    halves = [join_pieces([own, *own_across]), join_pieces([near, *near_across]), join_pieces([far, opposite])]
    early = join_pieces(halves + [swap(half, "col", 1) for half in halves], False)

    def attend(kernel, name, out_shape, out_specs, scratch, *args):
        held = args[2].shape[0] + args[2].shape[0] % 2
        scratch = scratch + [
            pltpu.VMEM((held, BLOCK, width), jnp.float32),
            pltpu.VMEM((head_size, width), jnp.float32),
        ]
        if not dense:
            scratch += [pltpu.SMEM(order.shape, jnp.int32), pltpu.SemaphoreType.DMA]
        return pl.pallas_call(
            functools.partial(kernel, heads, dense),
            out_shape=out_shape,
            in_specs=[vmem, vmem if dense else anywhere] + [vmem] * (len(args) - 2),
            out_specs=out_specs,
            scratch_shapes=scratch,
            compiler_params=pltpu.CompilerParams(vmem_limit_bytes=2 * held * BLOCK * width * 4 + 8 * 1024 * 1024),
            name=name,
        )(*args)

    queries_across = pl.pallas_call(
        functools.partial(turn_kernel, heads),
        out_shape=jax.ShapeDtypeStruct((own_blocks, head_size, width), queries.dtype),
        in_specs=[vmem],
        out_specs=vmem,
        compiler_params=small,
        name="turn",
    )(queries)
    last, queries_across = together(last, queries_across)
    parts = (
        jax.ShapeDtypeStruct((own_blocks, head_size, width), jnp.float32),
        jax.ShapeDtypeStruct((own_blocks, 2, width), jnp.float32),
    )
    part = attend(early_kernel, "early", parts, (vmem, vmem), [], queries_across, order, early[0])
    last = join_pieces(last)
    last_pair, *part = together([swap(last, "col", 1)], *part)
    last = join_pieces([last, *last_pair], False)
    whole = jax.ShapeDtypeStruct(queries.shape, jnp.bfloat16)
    out_scratch = [pltpu.VMEM(queries.shape, jnp.bfloat16), pltpu.SemaphoreType.DMA((own_blocks, heads))]
    end = functools.partial(last_kernel, per, places[1])
    return attend(end, "last", whole, anywhere, out_scratch, queries_across, order, last[0], *part)


def solution(mesh):
    placed = (
        P(("groups", "col"), "row", None),
        P(("groups", "row"), "col", None),
        P(("groups", "row"), "col", None),
        P("groups", None, None, None),
        P("groups", None, None),
    )
    return jax.shard_map(
        per_device,
        mesh=mesh,
        in_specs=placed,
        out_specs=P(("groups", "col"), "row", None),
        check_vma=False,
    )
```

```python
import functools
import math

import jax
import jax.numpy as jnp
from jax import lax
from jax.experimental import pallas as pl
from jax.experimental.pallas import tpu as pltpu
from jax.sharding import PartitionSpec as P

BLOCK = 128
CORES = 2

floor_score = -1e30
floor_top = -1e20


def join_kernel(transpose, *refs):
    out_ref = refs[-1]
    first = 0
    for ref in refs[:-1]:
        if not transpose:
            out_ref[first : first + ref.shape[0]] = ref[...]
        for n in range(ref.shape[0] if transpose else 0):
            out_ref[first + n, :BLOCK, :] = ref[n, :BLOCK, :]
            out_ref[first + n, BLOCK:, :] = ref[n, BLOCK:, :].T
        first += ref.shape[0]


def prepare_kernel(per, places, dense, list_hbm, count_hbm, order_ref, active_ref, list_ref, count_ref, sems):
    own_blocks = order_ref.shape[0]
    panels, slots = list_ref.shape[1:]
    cols = lax.axis_size("col")
    col_index = lax.axis_index("col")
    row_index = lax.axis_index("row")
    first = row_index * own_blocks
    copies = (
        pltpu.make_async_copy(list_hbm.at[col_index, pl.ds(first, own_blocks)], list_ref, sems.at[0]),
        pltpu.make_async_copy(count_hbm.at[col_index, pl.ds(first, own_blocks)], count_ref, sems.at[1]),
    )
    for copy in copies:
        copy.start()
    for copy in copies:
        copy.wait()
    for s in range(own_blocks):
        diagonal = col_index * list_hbm.shape[1] + first + s
        for r in range(panels):
            for n in range(slots):
                active_ref[r * slots + n] = 0
            for n in reversed(range(slots)):
                active_ref[r * slots + list_ref[s, r, n]] = (n < count_ref[s, r]).astype(jnp.int32)
        for part, where in enumerate(places):
            total = jnp.int32(0)
            diagonal_slot = jnp.int32(-1)
            for n, (row_flip, col_flip) in enumerate(where):
                for k in range(per):
                    slot = n * per + k
                    block = ((row_index ^ row_flip) * cols + (col_index ^ col_flip)) * per + k
                    on_diagonal = block == diagonal
                    if dense:
                        reach = jnp.where(on_diagonal, 0, jnp.where(active_ref[block] > 0, BLOCK, -BLOCK))
                        order_ref[s, part, slot : slot + 1, :] = jnp.full((1, order_ref.shape[3]), reach, jnp.int32)
                        continue
                    order_ref[s, part, total] = slot
                    diagonal_slot = jnp.where(on_diagonal, slot, diagonal_slot)
                    total = total + jnp.where(on_diagonal, 0, active_ref[block])
            if dense:
                continue
            end = order_ref.shape[2] - 2
            here = diagonal_slot >= 0
            order_ref[s, part, total] = diagonal_slot
            order_ref[s, part, end + 1] = jnp.where(here, total, -1)
            total = total + here.astype(jnp.int32)
            order_ref[s, part, total] = 0
            order_ref[s, part, end] = total


def blockwise(array, fold):
    return fold(array.reshape(array.shape[0] // 8, 8, array.shape[1]), axis=0)


def dense_attention(reach, kv_ref, queries, score_ref):
    head_size, width = queries.shape
    slots = kv_ref.shape[0]
    factor = math.log2(math.e) / head_size**0.5
    key_at = lax.broadcasted_iota(jnp.int32, (BLOCK, width), 0)
    query_at = lax.broadcasted_iota(jnp.int32, (BLOCK, width), 1) % BLOCK
    keys = jnp.concatenate([kv_ref[slot, :BLOCK, :] for slot in range(slots)])
    found = jnp.dot(keys, queries, preferred_element_type=jnp.float32)
    top = jnp.full((8, width), floor_top, jnp.float32)
    for slot in range(slots):
        seen = query_at + reach[slot : slot + 1, :] >= key_at
        one = jnp.where(seen, found[slot * BLOCK : (slot + 1) * BLOCK], floor_score)
        score_ref[slot] = one
        top = jnp.maximum(top, blockwise(one, jnp.max))
    top = jnp.max(top, axis=0, keepdims=True) * factor
    denom = jnp.zeros((8, width), jnp.float32)
    rounded = []
    for slot in range(slots):
        one = jnp.exp2(score_ref[slot] * factor - top)
        denom = denom + blockwise(one, jnp.sum)
        rounded.append(one.astype(jnp.bfloat16))
    values = jnp.concatenate([kv_ref[slot, BLOCK:, :] for slot in range(slots)], axis=1)
    acc = jnp.dot(values, jnp.concatenate(rounded), preferred_element_type=jnp.float32)
    return acc, top, jnp.sum(denom, axis=0, keepdims=True)


def listed_attention(s, part, order_ref, kv_ref, queries, score_ref, acc_ref):
    head_size, width = queries.shape
    end = order_ref.shape[2] - 2
    factor = math.log2(math.e) / head_size**0.5
    total = order_ref[s, part, end]
    diagonal = order_ref[s, part, end + 1]
    pairs = (total + 1) // 2
    key_at = lax.broadcasted_iota(jnp.int32, (BLOCK, width), 0)
    query_at = lax.broadcasted_iota(jnp.int32, (BLOCK, width), 1) % BLOCK

    def score(p, top):
        pair = [order_ref[s, part, 2 * p + n] for n in range(2)]
        keys = jnp.concatenate([kv_ref[slot, :BLOCK, :] for slot in pair])
        found = jnp.dot(keys, queries, preferred_element_type=jnp.float32)
        for n in range(2):
            t = 2 * p + n
            reach = jnp.where(t == diagonal, 0, jnp.where(t < total, BLOCK, -BLOCK))
            one = jnp.where(query_at + reach >= key_at, found[n * BLOCK : (n + 1) * BLOCK], floor_score)
            score_ref[t] = one
            top = jnp.maximum(top, blockwise(one, jnp.max))
        return top

    top = lax.fori_loop(0, pairs, score, jnp.full((8, width), floor_top, jnp.float32))
    top = jnp.max(top, axis=0, keepdims=True) * factor
    acc_ref[...] = jnp.zeros_like(acc_ref)

    def mix(p, denom):
        pair = [order_ref[s, part, 2 * p + n] for n in range(2)]
        values = jnp.concatenate([kv_ref[slot, BLOCK:, :] for slot in pair], axis=1)
        weights = [jnp.exp2(score_ref[2 * p + n] * factor - top) for n in range(2)]
        rounded = jnp.concatenate([one.astype(jnp.bfloat16) for one in weights])
        acc_ref[...] += jnp.dot(values, rounded, preferred_element_type=jnp.float32)
        return denom + blockwise(weights[0] + weights[1], jnp.sum)

    denom = lax.fori_loop(0, pairs, mix, jnp.zeros((8, width), jnp.float32))
    return acc_ref[...], top, jnp.sum(denom, axis=0, keepdims=True)


def get_order(dense, order_ref, scratch):
    if dense:
        return order_ref
    held, sem = scratch
    copy = pltpu.make_async_copy(order_ref, held, sem)
    copy.start()
    copy.wait()
    return held


def attention(dense, s, part, order_ref, kv_ref, queries, score_ref, acc_ref):
    if dense:
        return dense_attention(order_ref[s, part], kv_ref, queries, score_ref)
    return listed_attention(s, part, order_ref, kv_ref, queries, score_ref, acc_ref)


def turn_kernel(heads, q_ref, qt_ref):
    own_blocks, head_size = qt_ref.shape[:2]
    for s in range(own_blocks):
        for h in range(heads):
            tile = q_ref[0, pl.ds(s * BLOCK, BLOCK), pl.ds(h * head_size, head_size)]
            qt_ref[s, :, pl.ds(h * BLOCK, BLOCK)] = tile.T


def early_kernel(heads, dense, qt_ref, order_in, kv_ref, acc_out, stats_out, score_ref, acc_ref, *scratch):
    order_ref = get_order(dense, order_in, scratch)
    for s in range(qt_ref.shape[0]):
        acc, top, denom = attention(dense, s, 0, order_ref, kv_ref, qt_ref[s], score_ref, acc_ref)
        acc_out[s] = acc
        stats_out[s, 0:1] = top
        stats_out[s, 1:2] = denom


def last_kernel(per, places, heads, dense, qt_ref, order_in, kv_ref, acc_in, stats_in, out_hbm,
                out_ref, out_sems, score_ref, acc_ref, *scratch):
    order_ref = get_order(dense, order_in, scratch)
    own_blocks, head_size, width = qt_ref.shape
    rows, cols = lax.axis_size("row"), lax.axis_size("col")
    row_index, col_index = lax.axis_index("row"), lax.axis_index("col")
    sources = [(row_index ^ row_flip) * cols + (col_index ^ col_flip) for row_flip, col_flip in places]
    earliest = functools.reduce(jnp.minimum, sources) * per

    for s in range(own_blocks):
        useful = earliest <= (col_index * rows + row_index) * own_blocks + s

        def finish(acc, scale):
            copies = []
            for h in range(heads):
                at = pl.ds(h * head_size, head_size)
                cut = slice(h * BLOCK, (h + 1) * BLOCK)
                one = acc_in[s, :, cut] * scale[:, cut]
                if acc is not None:
                    one = one + acc[:, cut]
                out_ref[0, pl.ds(s * BLOCK, BLOCK), at] = one.astype(out_ref.dtype).T
                place = (0, pl.ds(s * BLOCK, BLOCK), at)
                copies.append(pltpu.make_async_copy(out_ref.at[place], out_hbm.at[place], out_sems.at[s, h]))
                copies[-1].start()
            for copy in copies:
                copy.wait()

        @pl.when(useful)
        def _():
            acc, top, denom = attention(dense, s, 1, order_ref, kv_ref, qt_ref[s], score_ref, acc_ref)
            other_top, other_denom = stats_in[s, 0:1], stats_in[s, 1:2]
            overall = jnp.maximum(top, other_top)
            scale, other_scale = jnp.exp2(top - overall), jnp.exp2(other_top - overall)
            share = 1.0 / (scale * denom + other_scale * other_denom)
            finish(acc * (scale * share), other_scale * share)

        @pl.when(jnp.logical_not(useful))
        def _():
            finish(None, 1.0 / stats_in[s, 1:2])


def swap(piece, axis, flip):
    array, places = piece
    came = lax.ppermute(array, axis, [(i, i ^ flip) for i in range(lax.axis_size(axis))])
    if axis == "row":
        return came, [(r ^ flip, c) for r, c in places]
    return came, [(r, c ^ flip) for r, c in places]


def join_pieces(pieces, transpose=True):
    vmem = pl.BlockSpec(memory_space=pltpu.VMEM)
    first = pieces[0][0]
    blocks = sum(array.shape[0] for array, _ in pieces)
    array = pl.pallas_call(
        functools.partial(join_kernel, transpose),
        out_shape=jax.ShapeDtypeStruct((blocks,) + first.shape[1:], first.dtype),
        in_specs=[vmem] * len(pieces),
        out_specs=vmem,
        compiler_params=pltpu.CompilerParams(vmem_limit_bytes=4 * 1024 * 1024),
        name="join",
    )(*(array for array, _ in pieces))
    return array, [place for _, places in pieces for place in places]


def together(pieces, *others):
    arrays = lax.optimization_barrier([array for array, _ in pieces] + list(others))
    held = [(array, places) for array, (_, places) in zip(arrays, pieces)]
    return (held, *arrays[len(held) :]) if others else held


def across(piece, cols):
    pieces = [piece]
    flip = CORES
    while flip < cols:
        pieces += [swap(one, "col", flip) for one in pieces]
        flip *= 2
    return pieces[1:]


def per_device(queries, keys, values, block_list, block_count):
    head_size = keys.shape[2]
    heads = queries.shape[2] // head_size
    own_blocks = queries.shape[1] // BLOCK
    per = keys.shape[1] // BLOCK
    rows = lax.axis_size("row")
    cols = lax.axis_size("col")
    panels, slots = block_list.shape[2:]
    blocks = panels * slots
    vmem = pl.BlockSpec(memory_space=pltpu.VMEM)
    smem = pl.BlockSpec(memory_space=pltpu.SMEM)
    anywhere = pl.BlockSpec(memory_space=pl.ANY)
    small = pltpu.CompilerParams(vmem_limit_bytes=4 * 1024 * 1024)

    shape = (per, BLOCK, head_size)
    packed = jnp.concatenate([keys.reshape(shape), values.reshape(shape)], axis=1)

    own = (packed, [(0, 0)])
    flip = rows // 2
    while flip > 2:
        came = swap(own, "row", flip)
        own = jnp.concatenate([own[0], came[0]]), own[1] + came[1]
        flip //= 2
    near, far, opposite = (swap(own, "row", flip) for flip in (1, 2, 3))
    own_across = across(own, cols)
    near_across = [swap(piece, "row", 1) for piece in own_across]
    early_places = [place for _, where in (own, *own_across, near, *near_across, far, opposite) for place in where]
    late_places = [(r, c ^ flip) for flip in range(CORES, cols, CORES) for r, c in far[1] + opposite[1]]
    places = [where + [(r, c ^ 1) for r, c in where] for where in (early_places, late_places)]

    longest = max(len(where) for where in places) * per
    dense = longest <= 16
    width = heads * BLOCK
    order_shape = (own_blocks, len(places), longest, width) if dense else (own_blocks, len(places), longest + 3)
    order = pl.pallas_call(
        functools.partial(prepare_kernel, per, places, dense),
        out_shape=jax.ShapeDtypeStruct(order_shape, jnp.int32),
        in_specs=[anywhere, anywhere],
        out_specs=vmem if dense else smem,
        scratch_shapes=[
            pltpu.SMEM((blocks,), jnp.int32),
            pltpu.SMEM((own_blocks, panels, slots), jnp.int32),
            pltpu.SMEM((own_blocks, panels), jnp.int32),
            pltpu.SemaphoreType.DMA((2,)),
        ],
        compiler_params=small,
        name="prepare",
    )(block_list, block_count)
    (far,), order = together([far], order)
    last = across(far, cols) + across(opposite, cols)
    last, queries = together(last, queries)
    halves = [join_pieces([own, *own_across]), join_pieces([near, *near_across]), join_pieces([far, opposite])]
    early = join_pieces(halves + [swap(half, "col", 1) for half in halves], False)

    def attend(kernel, name, out_shape, out_specs, scratch, *args):
        held = args[2].shape[0] + args[2].shape[0] % 2
        scratch = scratch + [
            pltpu.VMEM((held, BLOCK, width), jnp.float32),
            pltpu.VMEM((head_size, width), jnp.float32),
        ]
        if not dense:
            scratch += [pltpu.SMEM(order.shape, jnp.int32), pltpu.SemaphoreType.DMA]
        return pl.pallas_call(
            functools.partial(kernel, heads, dense),
            out_shape=out_shape,
            in_specs=[vmem, vmem if dense else anywhere] + [vmem] * (len(args) - 2),
            out_specs=out_specs,
            scratch_shapes=scratch,
            compiler_params=pltpu.CompilerParams(vmem_limit_bytes=2 * held * BLOCK * width * 4 + 8 * 1024 * 1024),
            name=name,
        )(*args)

    queries_across = pl.pallas_call(
        functools.partial(turn_kernel, heads),
        out_shape=jax.ShapeDtypeStruct((own_blocks, head_size, width), queries.dtype),
        in_specs=[vmem],
        out_specs=vmem,
        compiler_params=small,
        name="turn",
    )(queries)
    parts = (
        jax.ShapeDtypeStruct((own_blocks, head_size, width), jnp.float32),
        jax.ShapeDtypeStruct((own_blocks, 2, width), jnp.float32),
    )
    part = attend(early_kernel, "early", parts, (vmem, vmem), [], queries_across, order, early[0])
    last = join_pieces(last)
    last_pair, *part = together([swap(last, "col", 1)], *part)
    last = join_pieces([last, *last_pair], False)
    whole = jax.ShapeDtypeStruct(queries.shape, jnp.bfloat16)
    out_scratch = [pltpu.VMEM(queries.shape, jnp.bfloat16), pltpu.SemaphoreType.DMA((own_blocks, heads))]
    end = functools.partial(last_kernel, per, places[1])
    return attend(end, "last", whole, anywhere, out_scratch, queries_across, order, last[0], *part)


def solution(mesh):
    placed = (
        P(("groups", "col"), "row", None),
        P(("groups", "row"), "col", None),
        P(("groups", "row"), "col", None),
        P("groups", None, None, None),
        P("groups", None, None),
    )
    return jax.shard_map(
        per_device,
        mesh=mesh,
        in_specs=placed,
        out_specs=P(("groups", "col"), "row", None),
        check_vma=False,
    )
```

```python
import functools
import math

import jax
import jax.numpy as jnp
from jax import lax
from jax.experimental import pallas as pl
from jax.experimental.pallas import tpu as pltpu
from jax.sharding import PartitionSpec as P

BLOCK = 128
CORES = 2

floor_score = -1e30
floor_top = -1e20


def join_kernel(transpose, *refs):
    out_ref = refs[-1]
    first = 0
    for ref in refs[:-1]:
        if not transpose:
            out_ref[first : first + ref.shape[0]] = ref[...]
        for n in range(ref.shape[0] if transpose else 0):
            out_ref[first + n, :BLOCK, :] = ref[n, :BLOCK, :]
            out_ref[first + n, BLOCK:, :] = ref[n, BLOCK:, :].T
        first += ref.shape[0]


def prepare_kernel(per, places, dense, list_hbm, count_hbm, order_ref, active_ref, list_ref, count_ref, sems):
    own_blocks = order_ref.shape[0]
    panels, slots = list_ref.shape[1:]
    cols = lax.axis_size("col")
    col_index = lax.axis_index("col")
    row_index = lax.axis_index("row")
    first = row_index * own_blocks
    copies = (
        pltpu.make_async_copy(list_hbm.at[col_index, pl.ds(first, own_blocks)], list_ref, sems.at[0]),
        pltpu.make_async_copy(count_hbm.at[col_index, pl.ds(first, own_blocks)], count_ref, sems.at[1]),
    )
    for copy in copies:
        copy.start()
    for copy in copies:
        copy.wait()
    for s in range(own_blocks):
        diagonal = col_index * list_hbm.shape[1] + first + s
        for r in range(panels):
            for n in range(slots):
                active_ref[r * slots + n] = 0
            for n in reversed(range(slots)):
                active_ref[r * slots + list_ref[s, r, n]] = (n < count_ref[s, r]).astype(jnp.int32)
        for part, where in enumerate(places):
            total = jnp.int32(0)
            diagonal_slot = jnp.int32(-1)
            for n, (row_flip, col_flip) in enumerate(where):
                for k in range(per):
                    slot = n * per + k
                    block = ((row_index ^ row_flip) * cols + (col_index ^ col_flip)) * per + k
                    on_diagonal = block == diagonal
                    if dense:
                        reach = jnp.where(on_diagonal, 0, jnp.where(active_ref[block] > 0, BLOCK, -BLOCK))
                        order_ref[s, part, slot : slot + 1, :] = jnp.full((1, order_ref.shape[3]), reach, jnp.int32)
                        continue
                    order_ref[s, part, total] = slot
                    diagonal_slot = jnp.where(on_diagonal, slot, diagonal_slot)
                    total = total + jnp.where(on_diagonal, 0, active_ref[block])
            if dense:
                continue
            end = order_ref.shape[2] - 2
            here = diagonal_slot >= 0
            order_ref[s, part, total] = diagonal_slot
            order_ref[s, part, end + 1] = jnp.where(here, total, -1)
            total = total + here.astype(jnp.int32)
            order_ref[s, part, total] = 0
            order_ref[s, part, end] = total


def blockwise(array, fold):
    return fold(array.reshape(array.shape[0] // 8, 8, array.shape[1]), axis=0)


def dense_attention(reach, kv_ref, queries, score_ref):
    head_size, width = queries.shape
    slots = kv_ref.shape[0]
    factor = math.log2(math.e) / head_size**0.5
    key_at = lax.broadcasted_iota(jnp.int32, (BLOCK, width), 0)
    query_at = lax.broadcasted_iota(jnp.int32, (BLOCK, width), 1) % BLOCK
    keys = jnp.concatenate([kv_ref[slot, :BLOCK, :] for slot in range(slots)])
    found = jnp.dot(keys, queries, preferred_element_type=jnp.float32)
    top = jnp.full((8, width), floor_top, jnp.float32)
    for slot in range(slots):
        seen = query_at + reach[slot : slot + 1, :] >= key_at
        one = jnp.where(seen, found[slot * BLOCK : (slot + 1) * BLOCK], floor_score)
        score_ref[slot] = one
        top = jnp.maximum(top, blockwise(one, jnp.max))
    top = jnp.max(top, axis=0, keepdims=True) * factor
    denom = jnp.zeros((8, width), jnp.float32)
    rounded = []
    for slot in range(slots):
        one = jnp.exp2(score_ref[slot] * factor - top)
        denom = denom + blockwise(one, jnp.sum)
        rounded.append(one.astype(jnp.bfloat16))
    values = jnp.concatenate([kv_ref[slot, BLOCK:, :] for slot in range(slots)], axis=1)
    acc = jnp.dot(values, jnp.concatenate(rounded), preferred_element_type=jnp.float32)
    return acc, top, jnp.sum(denom, axis=0, keepdims=True)


def listed_attention(s, part, order_ref, kv_ref, queries, score_ref, acc_ref):
    head_size, width = queries.shape
    end = order_ref.shape[2] - 2
    factor = math.log2(math.e) / head_size**0.5
    total = order_ref[s, part, end]
    diagonal = order_ref[s, part, end + 1]
    pairs = (total + 1) // 2
    key_at = lax.broadcasted_iota(jnp.int32, (BLOCK, width), 0)
    query_at = lax.broadcasted_iota(jnp.int32, (BLOCK, width), 1) % BLOCK

    def score(p, top):
        pair = [order_ref[s, part, 2 * p + n] for n in range(2)]
        keys = jnp.concatenate([kv_ref[slot, :BLOCK, :] for slot in pair])
        found = jnp.dot(keys, queries, preferred_element_type=jnp.float32)
        for n in range(2):
            t = 2 * p + n
            reach = jnp.where(t == diagonal, 0, jnp.where(t < total, BLOCK, -BLOCK))
            one = jnp.where(query_at + reach >= key_at, found[n * BLOCK : (n + 1) * BLOCK], floor_score)
            score_ref[t] = one
            top = jnp.maximum(top, blockwise(one, jnp.max))
        return top

    top = lax.fori_loop(0, pairs, score, jnp.full((8, width), floor_top, jnp.float32))
    top = jnp.max(top, axis=0, keepdims=True) * factor
    acc_ref[...] = jnp.zeros_like(acc_ref)

    def mix(p, denom):
        pair = [order_ref[s, part, 2 * p + n] for n in range(2)]
        values = jnp.concatenate([kv_ref[slot, BLOCK:, :] for slot in pair], axis=1)
        weights = [jnp.exp2(score_ref[2 * p + n] * factor - top) for n in range(2)]
        rounded = jnp.concatenate([one.astype(jnp.bfloat16) for one in weights])
        acc_ref[...] += jnp.dot(values, rounded, preferred_element_type=jnp.float32)
        return denom + blockwise(weights[0] + weights[1], jnp.sum)

    denom = lax.fori_loop(0, pairs, mix, jnp.zeros((8, width), jnp.float32))
    return acc_ref[...], top, jnp.sum(denom, axis=0, keepdims=True)


def get_order(dense, order_ref, scratch):
    if dense:
        return order_ref
    held, sem = scratch
    copy = pltpu.make_async_copy(order_ref, held, sem)
    copy.start()
    copy.wait()
    return held


def attention(dense, s, part, order_ref, kv_ref, queries, score_ref, acc_ref):
    if dense:
        return dense_attention(order_ref[s, part], kv_ref, queries, score_ref)
    return listed_attention(s, part, order_ref, kv_ref, queries, score_ref, acc_ref)


def turn_kernel(heads, q_ref, qt_ref):
    own_blocks, head_size = qt_ref.shape[:2]
    for s in range(own_blocks):
        for h in range(heads):
            tile = q_ref[0, pl.ds(s * BLOCK, BLOCK), pl.ds(h * head_size, head_size)]
            qt_ref[s, :, pl.ds(h * BLOCK, BLOCK)] = tile.T


def early_kernel(heads, dense, qt_ref, order_in, kv_ref, acc_out, stats_out, score_ref, acc_ref, *scratch):
    order_ref = get_order(dense, order_in, scratch)
    for s in range(qt_ref.shape[0]):
        acc, top, denom = attention(dense, s, 0, order_ref, kv_ref, qt_ref[s], score_ref, acc_ref)
        acc_out[s] = acc
        stats_out[s, 0:1] = top
        stats_out[s, 1:2] = denom


def last_kernel(per, places, heads, dense, qt_ref, order_in, kv_ref, acc_in, stats_in, out_hbm,
                out_ref, out_sems, score_ref, acc_ref, *scratch):
    order_ref = get_order(dense, order_in, scratch)
    own_blocks, head_size, width = qt_ref.shape
    rows, cols = lax.axis_size("row"), lax.axis_size("col")
    row_index, col_index = lax.axis_index("row"), lax.axis_index("col")
    sources = [(row_index ^ row_flip) * cols + (col_index ^ col_flip) for row_flip, col_flip in places]
    earliest = functools.reduce(jnp.minimum, sources) * per

    for s in range(own_blocks):
        useful = earliest <= (col_index * rows + row_index) * own_blocks + s

        def finish(acc, scale):
            copies = []
            for h in range(heads):
                at = pl.ds(h * head_size, head_size)
                cut = slice(h * BLOCK, (h + 1) * BLOCK)
                one = acc_in[s, :, cut] * scale[:, cut]
                if acc is not None:
                    one = one + acc[:, cut]
                out_ref[0, pl.ds(s * BLOCK, BLOCK), at] = one.astype(out_ref.dtype).T
                place = (0, pl.ds(s * BLOCK, BLOCK), at)
                copies.append(pltpu.make_async_copy(out_ref.at[place], out_hbm.at[place], out_sems.at[s, h]))
                copies[-1].start()
            for copy in copies:
                copy.wait()

        @pl.when(useful)
        def _():
            acc, top, denom = attention(dense, s, 1, order_ref, kv_ref, qt_ref[s], score_ref, acc_ref)
            other_top, other_denom = stats_in[s, 0:1], stats_in[s, 1:2]
            overall = jnp.maximum(top, other_top)
            scale, other_scale = jnp.exp2(top - overall), jnp.exp2(other_top - overall)
            share = 1.0 / (scale * denom + other_scale * other_denom)
            finish(acc * (scale * share), other_scale * share)

        @pl.when(jnp.logical_not(useful))
        def _():
            finish(None, 1.0 / stats_in[s, 1:2])


def swap(piece, axis, flip):
    array, places = piece
    came = lax.ppermute(array, axis, [(i, i ^ flip) for i in range(lax.axis_size(axis))])
    if axis == "row":
        return came, [(r ^ flip, c) for r, c in places]
    return came, [(r, c ^ flip) for r, c in places]


def join_pieces(pieces, transpose=True):
    vmem = pl.BlockSpec(memory_space=pltpu.VMEM)
    first = pieces[0][0]
    blocks = sum(array.shape[0] for array, _ in pieces)
    array = pl.pallas_call(
        functools.partial(join_kernel, transpose),
        out_shape=jax.ShapeDtypeStruct((blocks,) + first.shape[1:], first.dtype),
        in_specs=[vmem] * len(pieces),
        out_specs=vmem,
        compiler_params=pltpu.CompilerParams(vmem_limit_bytes=4 * 1024 * 1024),
        name="join",
    )(*(array for array, _ in pieces))
    return array, [place for _, places in pieces for place in places]


def together(pieces, *others):
    arrays = lax.optimization_barrier([array for array, _ in pieces] + list(others))
    held = [(array, places) for array, (_, places) in zip(arrays, pieces)]
    return (held, *arrays[len(held) :]) if others else held


def across(piece, cols):
    pieces = [piece]
    flip = CORES
    while flip < cols:
        pieces += [swap(one, "col", flip) for one in pieces]
        flip *= 2
    return pieces[1:]


def per_device(queries, keys, values, block_list, block_count):
    head_size = keys.shape[2]
    heads = queries.shape[2] // head_size
    own_blocks = queries.shape[1] // BLOCK
    per = keys.shape[1] // BLOCK
    rows = lax.axis_size("row")
    cols = lax.axis_size("col")
    panels, slots = block_list.shape[2:]
    blocks = panels * slots
    vmem = pl.BlockSpec(memory_space=pltpu.VMEM)
    smem = pl.BlockSpec(memory_space=pltpu.SMEM)
    anywhere = pl.BlockSpec(memory_space=pl.ANY)
    small = pltpu.CompilerParams(vmem_limit_bytes=4 * 1024 * 1024)

    shape = (per, BLOCK, head_size)
    packed = jnp.concatenate([keys.reshape(shape), values.reshape(shape)], axis=1)

    own = (packed, [(0, 0)])
    flip = rows // 2
    while flip > 2:
        came = swap(own, "row", flip)
        own = jnp.concatenate([own[0], came[0]]), own[1] + came[1]
        flip //= 2
    near, far, opposite = (swap(own, "row", flip) for flip in (1, 2, 3))
    own_across = across(own, cols)
    near_across = [swap(piece, "row", 1) for piece in own_across]
    early_places = [place for _, where in (own, *own_across, near, *near_across, far, opposite) for place in where]
    late_places = [(r, c ^ flip) for flip in range(CORES, cols, CORES) for r, c in far[1] + opposite[1]]
    places = [where + [(r, c ^ 1) for r, c in where] for where in (early_places, late_places)]

    longest = max(len(where) for where in places) * per
    dense = longest <= 16
    width = heads * BLOCK
    order_shape = (own_blocks, len(places), longest, width) if dense else (own_blocks, len(places), longest + 3)
    order = pl.pallas_call(
        functools.partial(prepare_kernel, per, places, dense),
        out_shape=jax.ShapeDtypeStruct(order_shape, jnp.int32),
        in_specs=[anywhere, anywhere],
        out_specs=vmem if dense else smem,
        scratch_shapes=[
            pltpu.SMEM((blocks,), jnp.int32),
            pltpu.SMEM((own_blocks, panels, slots), jnp.int32),
            pltpu.SMEM((own_blocks, panels), jnp.int32),
            pltpu.SemaphoreType.DMA((2,)),
        ],
        compiler_params=small,
        name="prepare",
    )(block_list, block_count)
    far_across, queries, order = together(across(far, cols), queries, order)
    last = far_across + across(opposite, cols)
    halves = [join_pieces([own, *own_across]), join_pieces([near, *near_across]), join_pieces([far, opposite])]
    early = join_pieces(halves + [swap(half, "col", 1) for half in halves], False)

    def attend(kernel, name, out_shape, out_specs, scratch, *args):
        held = args[2].shape[0] + args[2].shape[0] % 2
        scratch = scratch + [
            pltpu.VMEM((held, BLOCK, width), jnp.float32),
            pltpu.VMEM((head_size, width), jnp.float32),
        ]
        if not dense:
            scratch += [pltpu.SMEM(order.shape, jnp.int32), pltpu.SemaphoreType.DMA]
        return pl.pallas_call(
            functools.partial(kernel, heads, dense),
            out_shape=out_shape,
            in_specs=[vmem, vmem if dense else anywhere] + [vmem] * (len(args) - 2),
            out_specs=out_specs,
            scratch_shapes=scratch,
            compiler_params=pltpu.CompilerParams(vmem_limit_bytes=2 * held * BLOCK * width * 4 + 8 * 1024 * 1024),
            name=name,
        )(*args)

    queries_across = pl.pallas_call(
        functools.partial(turn_kernel, heads),
        out_shape=jax.ShapeDtypeStruct((own_blocks, head_size, width), queries.dtype),
        in_specs=[vmem],
        out_specs=vmem,
        compiler_params=small,
        name="turn",
    )(queries)
    last, queries_across = together(last, queries_across)
    parts = (
        jax.ShapeDtypeStruct((own_blocks, head_size, width), jnp.float32),
        jax.ShapeDtypeStruct((own_blocks, 2, width), jnp.float32),
    )
    part = attend(early_kernel, "early", parts, (vmem, vmem), [], queries_across, order, early[0])
    last = join_pieces(last)
    last_pair, *part = together([swap(last, "col", 1)], *part)
    last = join_pieces([last, *last_pair], False)
    whole = jax.ShapeDtypeStruct(queries.shape, jnp.bfloat16)
    out_scratch = [pltpu.VMEM(queries.shape, jnp.bfloat16), pltpu.SemaphoreType.DMA((own_blocks, heads))]
    end = functools.partial(last_kernel, per, places[1])
    return attend(end, "last", whole, anywhere, out_scratch, queries_across, order, last[0], *part)


def solution(mesh):
    placed = (
        P(("groups", "col"), "row", None),
        P(("groups", "row"), "col", None),
        P(("groups", "row"), "col", None),
        P("groups", None, None, None),
        P("groups", None, None),
    )
    return jax.shard_map(
        per_device,
        mesh=mesh,
        in_specs=placed,
        out_specs=P(("groups", "col"), "row", None),
        check_vma=False,
    )
```

```python
import functools
import math

import jax
import jax.numpy as jnp
from jax import lax
from jax.experimental import pallas as pl
from jax.experimental.pallas import tpu as pltpu
from jax.sharding import PartitionSpec as P

BLOCK = 128
CORES = 2

floor_score = -1e30
floor_top = -1e20


def join_kernel(transpose, *refs):
    out_ref = refs[-1]
    first = 0
    for ref in refs[:-1]:
        if not transpose:
            out_ref[first : first + ref.shape[0]] = ref[...]
        for n in range(ref.shape[0] if transpose else 0):
            out_ref[first + n, :BLOCK, :] = ref[n, :BLOCK, :]
            out_ref[first + n, BLOCK:, :] = ref[n, BLOCK:, :].T
        first += ref.shape[0]


def prepare_kernel(per, places, dense, list_hbm, count_hbm, order_ref, active_ref, list_ref, count_ref, sems):
    own_blocks = order_ref.shape[0]
    panels, slots = list_ref.shape[1:]
    cols = lax.axis_size("col")
    col_index = lax.axis_index("col")
    row_index = lax.axis_index("row")
    first = row_index * own_blocks
    copies = (
        pltpu.make_async_copy(list_hbm.at[col_index, pl.ds(first, own_blocks)], list_ref, sems.at[0]),
        pltpu.make_async_copy(count_hbm.at[col_index, pl.ds(first, own_blocks)], count_ref, sems.at[1]),
    )
    for copy in copies:
        copy.start()
    for copy in copies:
        copy.wait()
    for s in range(own_blocks):
        diagonal = col_index * list_hbm.shape[1] + first + s
        for r in range(panels):
            for n in range(slots):
                active_ref[r * slots + n] = 0
            for n in reversed(range(slots)):
                active_ref[r * slots + list_ref[s, r, n]] = (n < count_ref[s, r]).astype(jnp.int32)
        for part, where in enumerate(places):
            total = jnp.int32(0)
            diagonal_slot = jnp.int32(-1)
            for n, (row_flip, col_flip) in enumerate(where):
                for k in range(per):
                    slot = n * per + k
                    block = ((row_index ^ row_flip) * cols + (col_index ^ col_flip)) * per + k
                    on_diagonal = block == diagonal
                    if dense:
                        reach = jnp.where(on_diagonal, 0, jnp.where(active_ref[block] > 0, BLOCK, -BLOCK))
                        order_ref[s, part, slot : slot + 1, :] = jnp.full((1, order_ref.shape[3]), reach, jnp.int32)
                        continue
                    order_ref[s, part, total] = slot
                    diagonal_slot = jnp.where(on_diagonal, slot, diagonal_slot)
                    total = total + jnp.where(on_diagonal, 0, active_ref[block])
            if dense:
                continue
            end = order_ref.shape[2] - 2
            here = diagonal_slot >= 0
            order_ref[s, part, total] = diagonal_slot
            order_ref[s, part, end + 1] = jnp.where(here, total, -1)
            total = total + here.astype(jnp.int32)
            order_ref[s, part, total] = 0
            order_ref[s, part, end] = total


def blockwise(array, fold):
    return fold(array.reshape(array.shape[0] // 8, 8, array.shape[1]), axis=0)


def dense_attention(reach, kv_ref, queries, score_ref):
    head_size, width = queries.shape
    slots = kv_ref.shape[0]
    factor = math.log2(math.e) / head_size**0.5
    key_at = lax.broadcasted_iota(jnp.int32, (BLOCK, width), 0)
    query_at = lax.broadcasted_iota(jnp.int32, (BLOCK, width), 1) % BLOCK
    keys = jnp.concatenate([kv_ref[slot, :BLOCK, :] for slot in range(slots)])
    found = jnp.dot(keys, queries, preferred_element_type=jnp.float32)
    top = jnp.full((8, width), floor_top, jnp.float32)
    for slot in range(slots):
        seen = query_at + reach[slot : slot + 1, :] >= key_at
        one = jnp.where(seen, found[slot * BLOCK : (slot + 1) * BLOCK], floor_score)
        score_ref[slot] = one
        top = jnp.maximum(top, blockwise(one, jnp.max))
    top = jnp.max(top, axis=0, keepdims=True) * factor
    denom = jnp.zeros((8, width), jnp.float32)
    rounded = []
    for slot in range(slots):
        one = jnp.exp2(score_ref[slot] * factor - top)
        denom = denom + blockwise(one, jnp.sum)
        rounded.append(one.astype(jnp.bfloat16))
    values = jnp.concatenate([kv_ref[slot, BLOCK:, :] for slot in range(slots)], axis=1)
    acc = jnp.dot(values, jnp.concatenate(rounded), preferred_element_type=jnp.float32)
    return acc, top, jnp.sum(denom, axis=0, keepdims=True)


def listed_attention(s, part, order_ref, kv_ref, queries, score_ref, acc_ref):
    head_size, width = queries.shape
    end = order_ref.shape[2] - 2
    factor = math.log2(math.e) / head_size**0.5
    total = order_ref[s, part, end]
    diagonal = order_ref[s, part, end + 1]
    pairs = (total + 1) // 2
    key_at = lax.broadcasted_iota(jnp.int32, (BLOCK, width), 0)
    query_at = lax.broadcasted_iota(jnp.int32, (BLOCK, width), 1) % BLOCK

    def score(p, top):
        pair = [order_ref[s, part, 2 * p + n] for n in range(2)]
        keys = jnp.concatenate([kv_ref[slot, :BLOCK, :] for slot in pair])
        found = jnp.dot(keys, queries, preferred_element_type=jnp.float32)
        for n in range(2):
            t = 2 * p + n
            reach = jnp.where(t == diagonal, 0, jnp.where(t < total, BLOCK, -BLOCK))
            one = jnp.where(query_at + reach >= key_at, found[n * BLOCK : (n + 1) * BLOCK], floor_score)
            score_ref[t] = one
            top = jnp.maximum(top, blockwise(one, jnp.max))
        return top

    top = lax.fori_loop(0, pairs, score, jnp.full((8, width), floor_top, jnp.float32))
    top = jnp.max(top, axis=0, keepdims=True) * factor
    acc_ref[...] = jnp.zeros_like(acc_ref)

    def mix(p, denom):
        pair = [order_ref[s, part, 2 * p + n] for n in range(2)]
        values = jnp.concatenate([kv_ref[slot, BLOCK:, :] for slot in pair], axis=1)
        weights = [jnp.exp2(score_ref[2 * p + n] * factor - top) for n in range(2)]
        rounded = jnp.concatenate([one.astype(jnp.bfloat16) for one in weights])
        acc_ref[...] += jnp.dot(values, rounded, preferred_element_type=jnp.float32)
        return denom + blockwise(weights[0] + weights[1], jnp.sum)

    denom = lax.fori_loop(0, pairs, mix, jnp.zeros((8, width), jnp.float32))
    return acc_ref[...], top, jnp.sum(denom, axis=0, keepdims=True)


def get_order(dense, order_ref, scratch):
    if dense:
        return order_ref
    held, sem = scratch
    copy = pltpu.make_async_copy(order_ref, held, sem)
    copy.start()
    copy.wait()
    return held


def attention(dense, s, part, order_ref, kv_ref, queries, score_ref, acc_ref):
    if dense:
        return dense_attention(order_ref[s, part], kv_ref, queries, score_ref)
    return listed_attention(s, part, order_ref, kv_ref, queries, score_ref, acc_ref)


def turn_kernel(heads, q_ref, qt_ref):
    own_blocks, head_size = qt_ref.shape[:2]
    for s in range(own_blocks):
        for h in range(heads):
            tile = q_ref[0, pl.ds(s * BLOCK, BLOCK), pl.ds(h * head_size, head_size)]
            qt_ref[s, :, pl.ds(h * BLOCK, BLOCK)] = tile.T


def early_kernel(heads, dense, qt_ref, order_in, kv_ref, acc_out, stats_out, score_ref, acc_ref, *scratch):
    order_ref = get_order(dense, order_in, scratch)
    for s in range(qt_ref.shape[0]):
        acc, top, denom = attention(dense, s, 0, order_ref, kv_ref, qt_ref[s], score_ref, acc_ref)
        acc_out[s] = acc
        stats_out[s, 0:1] = top
        stats_out[s, 1:2] = denom


def last_kernel(per, places, heads, dense, qt_ref, order_in, kv_ref, acc_in, stats_in, out_hbm,
                out_ref, out_sems, score_ref, acc_ref, *scratch):
    order_ref = get_order(dense, order_in, scratch)
    own_blocks, head_size, width = qt_ref.shape
    rows, cols = lax.axis_size("row"), lax.axis_size("col")
    row_index, col_index = lax.axis_index("row"), lax.axis_index("col")
    sources = [(row_index ^ row_flip) * cols + (col_index ^ col_flip) for row_flip, col_flip in places]
    earliest = functools.reduce(jnp.minimum, sources) * per

    for s in range(own_blocks):
        useful = earliest <= (col_index * rows + row_index) * own_blocks + s

        def finish(acc, scale):
            copies = []
            for h in range(heads):
                at = pl.ds(h * head_size, head_size)
                cut = slice(h * BLOCK, (h + 1) * BLOCK)
                one = acc_in[s, :, cut] * scale[:, cut]
                if acc is not None:
                    one = one + acc[:, cut]
                out_ref[0, pl.ds(s * BLOCK, BLOCK), at] = one.astype(out_ref.dtype).T
                place = (0, pl.ds(s * BLOCK, BLOCK), at)
                copies.append(pltpu.make_async_copy(out_ref.at[place], out_hbm.at[place], out_sems.at[s, h]))
                copies[-1].start()
            for copy in copies:
                copy.wait()

        @pl.when(useful)
        def _():
            acc, top, denom = attention(dense, s, 1, order_ref, kv_ref, qt_ref[s], score_ref, acc_ref)
            other_top, other_denom = stats_in[s, 0:1], stats_in[s, 1:2]
            overall = jnp.maximum(top, other_top)
            scale, other_scale = jnp.exp2(top - overall), jnp.exp2(other_top - overall)
            share = 1.0 / (scale * denom + other_scale * other_denom)
            finish(acc * (scale * share), other_scale * share)

        @pl.when(jnp.logical_not(useful))
        def _():
            finish(None, 1.0 / stats_in[s, 1:2])


def swap(piece, axis, flip):
    array, places = piece
    came = lax.ppermute(array, axis, [(i, i ^ flip) for i in range(lax.axis_size(axis))])
    if axis == "row":
        return came, [(r ^ flip, c) for r, c in places]
    return came, [(r, c ^ flip) for r, c in places]


def join_pieces(pieces, transpose=True):
    vmem = pl.BlockSpec(memory_space=pltpu.VMEM)
    first = pieces[0][0]
    blocks = sum(array.shape[0] for array, _ in pieces)
    array = pl.pallas_call(
        functools.partial(join_kernel, transpose),
        out_shape=jax.ShapeDtypeStruct((blocks,) + first.shape[1:], first.dtype),
        in_specs=[vmem] * len(pieces),
        out_specs=vmem,
        compiler_params=pltpu.CompilerParams(vmem_limit_bytes=4 * 1024 * 1024),
        name="join",
    )(*(array for array, _ in pieces))
    return array, [place for _, places in pieces for place in places]


def together(pieces, *others):
    arrays = lax.optimization_barrier([array for array, _ in pieces] + list(others))
    held = [(array, places) for array, (_, places) in zip(arrays, pieces)]
    return (held, *arrays[len(held) :]) if others else held


def across(piece, cols):
    pieces = [piece]
    flip = CORES
    while flip < cols:
        pieces += [swap(one, "col", flip) for one in pieces]
        flip *= 2
    return pieces[1:]


def per_device(queries, keys, values, block_list, block_count):
    head_size = keys.shape[2]
    heads = queries.shape[2] // head_size
    own_blocks = queries.shape[1] // BLOCK
    per = keys.shape[1] // BLOCK
    rows = lax.axis_size("row")
    cols = lax.axis_size("col")
    panels, slots = block_list.shape[2:]
    blocks = panels * slots
    vmem = pl.BlockSpec(memory_space=pltpu.VMEM)
    smem = pl.BlockSpec(memory_space=pltpu.SMEM)
    anywhere = pl.BlockSpec(memory_space=pl.ANY)
    small = pltpu.CompilerParams(vmem_limit_bytes=4 * 1024 * 1024)

    shape = (per, BLOCK, head_size)
    packed = jnp.concatenate([keys.reshape(shape), values.reshape(shape)], axis=1)

    own = (packed, [(0, 0)])
    flip = rows // 2
    while flip > 2:
        came = swap(own, "row", flip)
        own = jnp.concatenate([own[0], came[0]]), own[1] + came[1]
        flip //= 2
    near, far = (swap(own, "row", flip) for flip in (1, 2))
    own_across = across(own, cols)
    near, far, *own_across = together([near, far, *own_across])
    opposite = swap(far, "row", 1)
    near_across = [swap(piece, "row", 1) for piece in own_across]
    early_places = [place for _, where in (own, *own_across, near, *near_across, far, opposite) for place in where]
    late_places = [(r, c ^ flip) for flip in range(CORES, cols, CORES) for r, c in far[1] + opposite[1]]
    places = [where + [(r, c ^ 1) for r, c in where] for where in (early_places, late_places)]

    longest = max(len(where) for where in places) * per
    dense = longest <= 16
    width = heads * BLOCK
    order_shape = (own_blocks, len(places), longest, width) if dense else (own_blocks, len(places), longest + 3)
    order = pl.pallas_call(
        functools.partial(prepare_kernel, per, places, dense),
        out_shape=jax.ShapeDtypeStruct(order_shape, jnp.int32),
        in_specs=[anywhere, anywhere],
        out_specs=vmem if dense else smem,
        scratch_shapes=[
            pltpu.SMEM((blocks,), jnp.int32),
            pltpu.SMEM((own_blocks, panels, slots), jnp.int32),
            pltpu.SMEM((own_blocks, panels), jnp.int32),
            pltpu.SemaphoreType.DMA((2,)),
        ],
        compiler_params=small,
        name="prepare",
    )(block_list, block_count)
    far_across, queries, order = together(across(far, cols), queries, order)
    last = far_across + across(opposite, cols)
    halves = [join_pieces([own, *own_across]), join_pieces([near, *near_across]), join_pieces([far, opposite])]
    early = join_pieces(halves + [swap(half, "col", 1) for half in halves], False)

    def attend(kernel, name, out_shape, out_specs, scratch, *args):
        held = args[2].shape[0] + args[2].shape[0] % 2
        scratch = scratch + [
            pltpu.VMEM((held, BLOCK, width), jnp.float32),
            pltpu.VMEM((head_size, width), jnp.float32),
        ]
        if not dense:
            scratch += [pltpu.SMEM(order.shape, jnp.int32), pltpu.SemaphoreType.DMA]
        return pl.pallas_call(
            functools.partial(kernel, heads, dense),
            out_shape=out_shape,
            in_specs=[vmem, vmem if dense else anywhere] + [vmem] * (len(args) - 2),
            out_specs=out_specs,
            scratch_shapes=scratch,
            compiler_params=pltpu.CompilerParams(vmem_limit_bytes=2 * held * BLOCK * width * 4 + 8 * 1024 * 1024),
            name=name,
        )(*args)

    queries_across = pl.pallas_call(
        functools.partial(turn_kernel, heads),
        out_shape=jax.ShapeDtypeStruct((own_blocks, head_size, width), queries.dtype),
        in_specs=[vmem],
        out_specs=vmem,
        compiler_params=small,
        name="turn",
    )(queries)
    last, queries_across = together(last, queries_across)
    parts = (
        jax.ShapeDtypeStruct((own_blocks, head_size, width), jnp.float32),
        jax.ShapeDtypeStruct((own_blocks, 2, width), jnp.float32),
    )
    part = attend(early_kernel, "early", parts, (vmem, vmem), [], queries_across, order, early[0])
    last = join_pieces(last)
    last_pair, *part = together([swap(last, "col", 1)], *part)
    last = join_pieces([last, *last_pair], False)
    whole = jax.ShapeDtypeStruct(queries.shape, jnp.bfloat16)
    out_scratch = [pltpu.VMEM(queries.shape, jnp.bfloat16), pltpu.SemaphoreType.DMA((own_blocks, heads))]
    end = functools.partial(last_kernel, per, places[1])
    return attend(end, "last", whole, anywhere, out_scratch, queries_across, order, last[0], *part)


def solution(mesh):
    placed = (
        P(("groups", "col"), "row", None),
        P(("groups", "row"), "col", None),
        P(("groups", "row"), "col", None),
        P("groups", None, None, None),
        P("groups", None, None),
    )
    return jax.shard_map(
        per_device,
        mesh=mesh,
        in_specs=placed,
        out_specs=P(("groups", "col"), "row", None),
        check_vma=False,
    )
```

```python
import functools
import math

import jax
import jax.numpy as jnp
from jax import lax
from jax.experimental import pallas as pl
from jax.experimental.pallas import tpu as pltpu
from jax.sharding import PartitionSpec as P

BLOCK = 128
CORES = 2

floor_score = -1e30
floor_top = -1e20


def join_kernel(transpose, *refs):
    out_ref = refs[-1]
    first = 0
    for ref in refs[:-1]:
        if not transpose:
            out_ref[first : first + ref.shape[0]] = ref[...]
        for n in range(ref.shape[0] if transpose else 0):
            out_ref[first + n, :BLOCK, :] = ref[n, :BLOCK, :]
            out_ref[first + n, BLOCK:, :] = ref[n, BLOCK:, :].T
        first += ref.shape[0]


def prepare_kernel(per, places, dense, list_hbm, count_hbm, order_ref, active_ref, list_ref, count_ref, sems):
    own_blocks = order_ref.shape[0]
    panels, slots = list_ref.shape[1:]
    cols = lax.axis_size("col")
    col_index = lax.axis_index("col")
    row_index = lax.axis_index("row")
    first = row_index * own_blocks
    copies = (
        pltpu.make_async_copy(list_hbm.at[col_index, pl.ds(first, own_blocks)], list_ref, sems.at[0]),
        pltpu.make_async_copy(count_hbm.at[col_index, pl.ds(first, own_blocks)], count_ref, sems.at[1]),
    )
    for copy in copies:
        copy.start()
    for copy in copies:
        copy.wait()
    for s in range(own_blocks):
        diagonal = col_index * list_hbm.shape[1] + first + s
        for r in range(panels):
            for n in range(slots):
                active_ref[r * slots + n] = 0
            for n in reversed(range(slots)):
                active_ref[r * slots + list_ref[s, r, n]] = (n < count_ref[s, r]).astype(jnp.int32)
        for part, where in enumerate(places):
            total = jnp.int32(0)
            diagonal_slot = jnp.int32(-1)
            for n, (row_flip, col_flip) in enumerate(where):
                for k in range(per):
                    slot = n * per + k
                    block = ((row_index ^ row_flip) * cols + (col_index ^ col_flip)) * per + k
                    on_diagonal = block == diagonal
                    if dense:
                        reach = jnp.where(on_diagonal, 0, jnp.where(active_ref[block] > 0, BLOCK, -BLOCK))
                        order_ref[s, part, slot : slot + 1, :] = jnp.full((1, order_ref.shape[3]), reach, jnp.int32)
                        continue
                    order_ref[s, part, total] = slot
                    diagonal_slot = jnp.where(on_diagonal, slot, diagonal_slot)
                    total = total + jnp.where(on_diagonal, 0, active_ref[block])
            if dense:
                continue
            end = order_ref.shape[2] - 2
            here = diagonal_slot >= 0
            order_ref[s, part, total] = diagonal_slot
            order_ref[s, part, end + 1] = jnp.where(here, total, -1)
            total = total + here.astype(jnp.int32)
            order_ref[s, part, total] = 0
            order_ref[s, part, end] = total


def blockwise(array, fold):
    return fold(array.reshape(array.shape[0] // 8, 8, array.shape[1]), axis=0)


def dense_attention(reach, kv_ref, queries, score_ref):
    head_size, width = queries.shape
    slots = kv_ref.shape[0]
    factor = math.log2(math.e) / head_size**0.5
    key_at = lax.broadcasted_iota(jnp.int32, (BLOCK, width), 0)
    query_at = lax.broadcasted_iota(jnp.int32, (BLOCK, width), 1) % BLOCK
    keys = jnp.concatenate([kv_ref[slot, :BLOCK, :] for slot in range(slots)])
    found = jnp.dot(keys, queries, preferred_element_type=jnp.float32)
    top = jnp.full((8, width), floor_top, jnp.float32)
    for slot in range(slots):
        seen = query_at + reach[slot : slot + 1, :] >= key_at
        one = jnp.where(seen, found[slot * BLOCK : (slot + 1) * BLOCK], floor_score)
        score_ref[slot] = one
        top = jnp.maximum(top, blockwise(one, jnp.max))
    top = jnp.max(top, axis=0, keepdims=True) * factor
    denom = jnp.zeros((8, width), jnp.float32)
    rounded = []
    for slot in range(slots):
        one = jnp.exp2(score_ref[slot] * factor - top)
        denom = denom + blockwise(one, jnp.sum)
        rounded.append(one.astype(jnp.bfloat16))
    values = jnp.concatenate([kv_ref[slot, BLOCK:, :] for slot in range(slots)], axis=1)
    acc = jnp.dot(values, jnp.concatenate(rounded), preferred_element_type=jnp.float32)
    return acc, top, jnp.sum(denom, axis=0, keepdims=True)


def listed_attention(s, part, order_ref, kv_ref, queries, score_ref, acc_ref):
    head_size, width = queries.shape
    end = order_ref.shape[2] - 2
    factor = math.log2(math.e) / head_size**0.5
    total = order_ref[s, part, end]
    diagonal = order_ref[s, part, end + 1]
    pairs = (total + 1) // 2
    key_at = lax.broadcasted_iota(jnp.int32, (BLOCK, width), 0)
    query_at = lax.broadcasted_iota(jnp.int32, (BLOCK, width), 1) % BLOCK

    def score(p, top):
        pair = [order_ref[s, part, 2 * p + n] for n in range(2)]
        keys = jnp.concatenate([kv_ref[slot, :BLOCK, :] for slot in pair])
        found = jnp.dot(keys, queries, preferred_element_type=jnp.float32)
        for n in range(2):
            t = 2 * p + n
            reach = jnp.where(t == diagonal, 0, jnp.where(t < total, BLOCK, -BLOCK))
            one = jnp.where(query_at + reach >= key_at, found[n * BLOCK : (n + 1) * BLOCK], floor_score)
            score_ref[t] = one
            top = jnp.maximum(top, blockwise(one, jnp.max))
        return top

    top = lax.fori_loop(0, pairs, score, jnp.full((8, width), floor_top, jnp.float32))
    top = jnp.max(top, axis=0, keepdims=True) * factor
    acc_ref[...] = jnp.zeros_like(acc_ref)

    def mix(p, denom):
        pair = [order_ref[s, part, 2 * p + n] for n in range(2)]
        values = jnp.concatenate([kv_ref[slot, BLOCK:, :] for slot in pair], axis=1)
        weights = [jnp.exp2(score_ref[2 * p + n] * factor - top) for n in range(2)]
        rounded = jnp.concatenate([one.astype(jnp.bfloat16) for one in weights])
        acc_ref[...] += jnp.dot(values, rounded, preferred_element_type=jnp.float32)
        return denom + blockwise(weights[0] + weights[1], jnp.sum)

    denom = lax.fori_loop(0, pairs, mix, jnp.zeros((8, width), jnp.float32))
    return acc_ref[...], top, jnp.sum(denom, axis=0, keepdims=True)


def get_order(dense, order_ref, scratch):
    if dense:
        return order_ref
    held, sem = scratch
    copy = pltpu.make_async_copy(order_ref, held, sem)
    copy.start()
    copy.wait()
    return held


def attention(dense, s, part, order_ref, kv_ref, queries, score_ref, acc_ref):
    if dense:
        return dense_attention(order_ref[s, part], kv_ref, queries, score_ref)
    return listed_attention(s, part, order_ref, kv_ref, queries, score_ref, acc_ref)


def turn_kernel(heads, q_ref, qt_ref):
    own_blocks, head_size = qt_ref.shape[:2]
    for s in range(own_blocks):
        for h in range(heads):
            tile = q_ref[0, pl.ds(s * BLOCK, BLOCK), pl.ds(h * head_size, head_size)]
            qt_ref[s, :, pl.ds(h * BLOCK, BLOCK)] = tile.T


def early_kernel(heads, dense, qt_ref, order_in, kv_ref, acc_out, stats_out, score_ref, acc_ref, *scratch):
    order_ref = get_order(dense, order_in, scratch)
    for s in range(qt_ref.shape[0]):
        acc, top, denom = attention(dense, s, 0, order_ref, kv_ref, qt_ref[s], score_ref, acc_ref)
        acc_out[s] = acc
        stats_out[s, 0:1] = top
        stats_out[s, 1:2] = denom


def last_kernel(per, places, heads, dense, qt_ref, order_in, kv_ref, acc_in, stats_in, out_hbm,
                out_ref, out_sems, score_ref, acc_ref, *scratch):
    order_ref = get_order(dense, order_in, scratch)
    own_blocks, head_size, width = qt_ref.shape
    rows, cols = lax.axis_size("row"), lax.axis_size("col")
    row_index, col_index = lax.axis_index("row"), lax.axis_index("col")
    sources = [(row_index ^ row_flip) * cols + (col_index ^ col_flip) for row_flip, col_flip in places]
    earliest = functools.reduce(jnp.minimum, sources) * per

    for s in range(own_blocks):
        useful = earliest <= (col_index * rows + row_index) * own_blocks + s

        def finish(acc, scale):
            copies = []
            for h in range(heads):
                at = pl.ds(h * head_size, head_size)
                cut = slice(h * BLOCK, (h + 1) * BLOCK)
                one = acc_in[s, :, cut] * scale[:, cut]
                if acc is not None:
                    one = one + acc[:, cut]
                out_ref[0, pl.ds(s * BLOCK, BLOCK), at] = one.astype(out_ref.dtype).T
                place = (0, pl.ds(s * BLOCK, BLOCK), at)
                copies.append(pltpu.make_async_copy(out_ref.at[place], out_hbm.at[place], out_sems.at[s, h]))
                copies[-1].start()
            for copy in copies:
                copy.wait()

        @pl.when(useful)
        def _():
            acc, top, denom = attention(dense, s, 1, order_ref, kv_ref, qt_ref[s], score_ref, acc_ref)
            other_top, other_denom = stats_in[s, 0:1], stats_in[s, 1:2]
            overall = jnp.maximum(top, other_top)
            scale, other_scale = jnp.exp2(top - overall), jnp.exp2(other_top - overall)
            share = 1.0 / (scale * denom + other_scale * other_denom)
            finish(acc * (scale * share), other_scale * share)

        @pl.when(jnp.logical_not(useful))
        def _():
            finish(None, 1.0 / stats_in[s, 1:2])


def swap(piece, axis, flip):
    array, places = piece
    came = lax.ppermute(array, axis, [(i, i ^ flip) for i in range(lax.axis_size(axis))])
    if axis == "row":
        return came, [(r ^ flip, c) for r, c in places]
    return came, [(r, c ^ flip) for r, c in places]


def join_pieces(pieces, transpose=True):
    vmem = pl.BlockSpec(memory_space=pltpu.VMEM)
    first = pieces[0][0]
    blocks = sum(array.shape[0] for array, _ in pieces)
    array = pl.pallas_call(
        functools.partial(join_kernel, transpose),
        out_shape=jax.ShapeDtypeStruct((blocks,) + first.shape[1:], first.dtype),
        in_specs=[vmem] * len(pieces),
        out_specs=vmem,
        compiler_params=pltpu.CompilerParams(vmem_limit_bytes=4 * 1024 * 1024),
        name="join",
    )(*(array for array, _ in pieces))
    return array, [place for _, places in pieces for place in places]


def together(pieces, *others):
    arrays = lax.optimization_barrier([array for array, _ in pieces] + list(others))
    held = [(array, places) for array, (_, places) in zip(arrays, pieces)]
    return (held, *arrays[len(held) :]) if others else held


def across(piece, cols):
    pieces = [piece]
    flip = CORES
    while flip < cols:
        pieces += [swap(one, "col", flip) for one in pieces]
        flip *= 2
    return pieces[1:]


def per_device(queries, keys, values, block_list, block_count):
    head_size = keys.shape[2]
    heads = queries.shape[2] // head_size
    own_blocks = queries.shape[1] // BLOCK
    per = keys.shape[1] // BLOCK
    rows = lax.axis_size("row")
    cols = lax.axis_size("col")
    panels, slots = block_list.shape[2:]
    blocks = panels * slots
    vmem = pl.BlockSpec(memory_space=pltpu.VMEM)
    smem = pl.BlockSpec(memory_space=pltpu.SMEM)
    anywhere = pl.BlockSpec(memory_space=pl.ANY)
    small = pltpu.CompilerParams(vmem_limit_bytes=4 * 1024 * 1024)

    shape = (per, BLOCK, head_size)
    packed = jnp.concatenate([keys.reshape(shape), values.reshape(shape)], axis=1)

    own = (packed, [(0, 0)])
    flip = rows // 2
    while flip > 2:
        came = swap(own, "row", flip)
        own = jnp.concatenate([own[0], came[0]]), own[1] + came[1]
        flip //= 2
    near, far, opposite = (swap(own, "row", flip) for flip in (1, 2, 3))
    own_across = across(own, cols)
    near_across = [swap(piece, "row", 1) for piece in own_across]
    early_places = [place for _, where in (own, near, *own_across, *near_across, far, opposite) for place in where]
    late_places = [(r, c ^ flip) for flip in range(CORES, cols, CORES) for r, c in far[1] + opposite[1]]
    places = [where + [(r, c ^ 1) for r, c in where] for where in (early_places, late_places)]

    longest = max(len(where) for where in places) * per
    dense = longest <= 16
    width = heads * BLOCK
    order_shape = (own_blocks, len(places), longest, width) if dense else (own_blocks, len(places), longest + 3)
    order = pl.pallas_call(
        functools.partial(prepare_kernel, per, places, dense),
        out_shape=jax.ShapeDtypeStruct(order_shape, jnp.int32),
        in_specs=[anywhere, anywhere],
        out_specs=vmem if dense else smem,
        scratch_shapes=[
            pltpu.SMEM((blocks,), jnp.int32),
            pltpu.SMEM((own_blocks, panels, slots), jnp.int32),
            pltpu.SMEM((own_blocks, panels), jnp.int32),
            pltpu.SemaphoreType.DMA((2,)),
        ],
        compiler_params=small,
        name="prepare",
    )(block_list, block_count)
    (far, near), order = together([far, near], order)
    far_across = across(far, cols)
    seconds = together(far_across + near_across)
    far_across, near_across = seconds[: len(far_across)], seconds[len(far_across) :]
    last = far_across + across(opposite, cols)
    last, queries = together(last, queries)
    halves = [join_pieces([own, near]), join_pieces([*own_across, *near_across]), join_pieces([far, opposite])]
    early = join_pieces(halves + [swap(half, "col", 1) for half in halves], False)

    def attend(kernel, name, out_shape, out_specs, scratch, *args):
        held = args[2].shape[0] + args[2].shape[0] % 2
        scratch = scratch + [
            pltpu.VMEM((held, BLOCK, width), jnp.float32),
            pltpu.VMEM((head_size, width), jnp.float32),
        ]
        if not dense:
            scratch += [pltpu.SMEM(order.shape, jnp.int32), pltpu.SemaphoreType.DMA]
        return pl.pallas_call(
            functools.partial(kernel, heads, dense),
            out_shape=out_shape,
            in_specs=[vmem, vmem if dense else anywhere] + [vmem] * (len(args) - 2),
            out_specs=out_specs,
            scratch_shapes=scratch,
            compiler_params=pltpu.CompilerParams(vmem_limit_bytes=2 * held * BLOCK * width * 4 + 8 * 1024 * 1024),
            name=name,
        )(*args)

    queries_across = pl.pallas_call(
        functools.partial(turn_kernel, heads),
        out_shape=jax.ShapeDtypeStruct((own_blocks, head_size, width), queries.dtype),
        in_specs=[vmem],
        out_specs=vmem,
        compiler_params=small,
        name="turn",
    )(queries)
    parts = (
        jax.ShapeDtypeStruct((own_blocks, head_size, width), jnp.float32),
        jax.ShapeDtypeStruct((own_blocks, 2, width), jnp.float32),
    )
    part = attend(early_kernel, "early", parts, (vmem, vmem), [], queries_across, order, early[0])
    last = join_pieces(last)
    last_pair, *part = together([swap(last, "col", 1)], *part)
    last = join_pieces([last, *last_pair], False)
    whole = jax.ShapeDtypeStruct(queries.shape, jnp.bfloat16)
    out_scratch = [pltpu.VMEM(queries.shape, jnp.bfloat16), pltpu.SemaphoreType.DMA((own_blocks, heads))]
    end = functools.partial(last_kernel, per, places[1])
    return attend(end, "last", whole, anywhere, out_scratch, queries_across, order, last[0], *part)


def solution(mesh):
    placed = (
        P(("groups", "col"), "row", None),
        P(("groups", "row"), "col", None),
        P(("groups", "row"), "col", None),
        P("groups", None, None, None),
        P("groups", None, None),
    )
    return jax.shard_map(
        per_device,
        mesh=mesh,
        in_specs=placed,
        out_specs=P(("groups", "col"), "row", None),
        check_vma=False,
    )
```

```python
import functools
import math

import jax
import jax.numpy as jnp
from jax import lax
from jax.experimental import pallas as pl
from jax.experimental.pallas import tpu as pltpu
from jax.sharding import PartitionSpec as P

BLOCK = 128
CORES = 2

floor_score = -1e30
floor_top = -1e20


def join_kernel(transpose, *refs):
    out_ref = refs[-1]
    first = 0
    for ref in refs[:-1]:
        if not transpose:
            out_ref[first : first + ref.shape[0]] = ref[...]
        for n in range(ref.shape[0] if transpose else 0):
            out_ref[first + n, :BLOCK, :] = ref[n, :BLOCK, :]
            out_ref[first + n, BLOCK:, :] = ref[n, BLOCK:, :].T
        first += ref.shape[0]


def prepare_kernel(per, places, dense, list_hbm, count_hbm, order_ref, active_ref, list_ref, count_ref, sems):
    own_blocks = order_ref.shape[0]
    panels, slots = list_ref.shape[1:]
    cols = lax.axis_size("col")
    col_index = lax.axis_index("col")
    row_index = lax.axis_index("row")
    first = row_index * own_blocks
    copies = (
        pltpu.make_async_copy(list_hbm.at[col_index, pl.ds(first, own_blocks)], list_ref, sems.at[0]),
        pltpu.make_async_copy(count_hbm.at[col_index, pl.ds(first, own_blocks)], count_ref, sems.at[1]),
    )
    for copy in copies:
        copy.start()
    for copy in copies:
        copy.wait()
    for s in range(own_blocks):
        diagonal = col_index * list_hbm.shape[1] + first + s
        for r in range(panels):
            for n in range(slots):
                active_ref[r * slots + n] = 0
            for n in reversed(range(slots)):
                active_ref[r * slots + list_ref[s, r, n]] = (n < count_ref[s, r]).astype(jnp.int32)
        for part, where in enumerate(places):
            total = jnp.int32(0)
            diagonal_slot = jnp.int32(-1)
            for n, (row_flip, col_flip) in enumerate(where):
                for k in range(per):
                    slot = n * per + k
                    block = ((row_index ^ row_flip) * cols + (col_index ^ col_flip)) * per + k
                    on_diagonal = block == diagonal
                    if dense:
                        reach = jnp.where(on_diagonal, 0, jnp.where(active_ref[block] > 0, BLOCK, -BLOCK))
                        order_ref[s, part, slot : slot + 1, :] = jnp.full((1, order_ref.shape[3]), reach, jnp.int32)
                        continue
                    order_ref[s, part, total] = slot
                    diagonal_slot = jnp.where(on_diagonal, slot, diagonal_slot)
                    total = total + jnp.where(on_diagonal, 0, active_ref[block])
            if dense:
                continue
            end = order_ref.shape[2] - 2
            here = diagonal_slot >= 0
            order_ref[s, part, total] = diagonal_slot
            order_ref[s, part, end + 1] = jnp.where(here, total, -1)
            total = total + here.astype(jnp.int32)
            order_ref[s, part, total] = 0
            order_ref[s, part, end] = total


def blockwise(array, fold):
    return fold(array.reshape(array.shape[0] // 8, 8, array.shape[1]), axis=0)


def dense_attention(reach, kv_ref, queries, score_ref):
    head_size, width = queries.shape
    slots = kv_ref.shape[0]
    factor = math.log2(math.e) / head_size**0.5
    key_at = lax.broadcasted_iota(jnp.int32, (BLOCK, width), 0)
    query_at = lax.broadcasted_iota(jnp.int32, (BLOCK, width), 1) % BLOCK
    keys = jnp.concatenate([kv_ref[slot, :BLOCK, :] for slot in range(slots)])
    found = jnp.dot(keys, queries, preferred_element_type=jnp.float32)
    top = jnp.full((8, width), floor_top, jnp.float32)
    for slot in range(slots):
        seen = query_at + reach[slot : slot + 1, :] >= key_at
        one = jnp.where(seen, found[slot * BLOCK : (slot + 1) * BLOCK], floor_score)
        score_ref[slot] = one
        top = jnp.maximum(top, blockwise(one, jnp.max))
    top = jnp.max(top, axis=0, keepdims=True) * factor
    denom = jnp.zeros((8, width), jnp.float32)
    rounded = []
    for slot in range(slots):
        one = jnp.exp2(score_ref[slot] * factor - top)
        denom = denom + blockwise(one, jnp.sum)
        rounded.append(one.astype(jnp.bfloat16))
    values = jnp.concatenate([kv_ref[slot, BLOCK:, :] for slot in range(slots)], axis=1)
    acc = jnp.dot(values, jnp.concatenate(rounded), preferred_element_type=jnp.float32)
    return acc, top, jnp.sum(denom, axis=0, keepdims=True)


def listed_attention(s, part, order_ref, kv_ref, queries, score_ref, acc_ref):
    head_size, width = queries.shape
    end = order_ref.shape[2] - 2
    factor = math.log2(math.e) / head_size**0.5
    total = order_ref[s, part, end]
    diagonal = order_ref[s, part, end + 1]
    pairs = (total + 1) // 2
    key_at = lax.broadcasted_iota(jnp.int32, (BLOCK, width), 0)
    query_at = lax.broadcasted_iota(jnp.int32, (BLOCK, width), 1) % BLOCK

    def score(p, top):
        pair = [order_ref[s, part, 2 * p + n] for n in range(2)]
        keys = jnp.concatenate([kv_ref[slot, :BLOCK, :] for slot in pair])
        found = jnp.dot(keys, queries, preferred_element_type=jnp.float32)
        for n in range(2):
            t = 2 * p + n
            reach = jnp.where(t == diagonal, 0, jnp.where(t < total, BLOCK, -BLOCK))
            one = jnp.where(query_at + reach >= key_at, found[n * BLOCK : (n + 1) * BLOCK], floor_score)
            score_ref[t] = one
            top = jnp.maximum(top, blockwise(one, jnp.max))
        return top

    top = lax.fori_loop(0, pairs, score, jnp.full((8, width), floor_top, jnp.float32))
    top = jnp.max(top, axis=0, keepdims=True) * factor
    acc_ref[...] = jnp.zeros_like(acc_ref)

    def mix(p, denom):
        pair = [order_ref[s, part, 2 * p + n] for n in range(2)]
        values = jnp.concatenate([kv_ref[slot, BLOCK:, :] for slot in pair], axis=1)
        weights = [jnp.exp2(score_ref[2 * p + n] * factor - top) for n in range(2)]
        rounded = jnp.concatenate([one.astype(jnp.bfloat16) for one in weights])
        acc_ref[...] += jnp.dot(values, rounded, preferred_element_type=jnp.float32)
        return denom + blockwise(weights[0] + weights[1], jnp.sum)

    denom = lax.fori_loop(0, pairs, mix, jnp.zeros((8, width), jnp.float32))
    return acc_ref[...], top, jnp.sum(denom, axis=0, keepdims=True)


def get_order(dense, order_ref, scratch):
    if dense:
        return order_ref
    held, sem = scratch
    copy = pltpu.make_async_copy(order_ref, held, sem)
    copy.start()
    copy.wait()
    return held


def attention(dense, s, part, order_ref, kv_ref, queries, score_ref, acc_ref):
    if dense:
        return dense_attention(order_ref[s, part], kv_ref, queries, score_ref)
    return listed_attention(s, part, order_ref, kv_ref, queries, score_ref, acc_ref)


def turn_kernel(heads, q_ref, qt_ref):
    own_blocks, head_size = qt_ref.shape[:2]
    for s in range(own_blocks):
        for h in range(heads):
            tile = q_ref[0, pl.ds(s * BLOCK, BLOCK), pl.ds(h * head_size, head_size)]
            qt_ref[s, :, pl.ds(h * BLOCK, BLOCK)] = tile.T


def early_kernel(heads, dense, qt_ref, order_in, kv_ref, acc_out, stats_out, score_ref, acc_ref, *scratch):
    order_ref = get_order(dense, order_in, scratch)
    for s in range(qt_ref.shape[0]):
        acc, top, denom = attention(dense, s, 0, order_ref, kv_ref, qt_ref[s], score_ref, acc_ref)
        acc_out[s] = acc
        stats_out[s, 0:1] = top
        stats_out[s, 1:2] = denom


def last_kernel(per, places, heads, dense, qt_ref, order_in, kv_ref, acc_in, stats_in, out_hbm,
                out_ref, out_sems, score_ref, acc_ref, *scratch):
    order_ref = get_order(dense, order_in, scratch)
    own_blocks, head_size, width = qt_ref.shape
    rows, cols = lax.axis_size("row"), lax.axis_size("col")
    row_index, col_index = lax.axis_index("row"), lax.axis_index("col")
    sources = [(row_index ^ row_flip) * cols + (col_index ^ col_flip) for row_flip, col_flip in places]
    earliest = functools.reduce(jnp.minimum, sources) * per

    for s in range(own_blocks):
        useful = earliest <= (col_index * rows + row_index) * own_blocks + s

        def finish(acc, scale):
            copies = []
            for h in range(heads):
                at = pl.ds(h * head_size, head_size)
                cut = slice(h * BLOCK, (h + 1) * BLOCK)
                one = acc_in[s, :, cut] * scale[:, cut]
                if acc is not None:
                    one = one + acc[:, cut]
                out_ref[0, pl.ds(s * BLOCK, BLOCK), at] = one.astype(out_ref.dtype).T
                place = (0, pl.ds(s * BLOCK, BLOCK), at)
                copies.append(pltpu.make_async_copy(out_ref.at[place], out_hbm.at[place], out_sems.at[s, h]))
                copies[-1].start()
            for copy in copies:
                copy.wait()

        @pl.when(useful)
        def _():
            acc, top, denom = attention(dense, s, 1, order_ref, kv_ref, qt_ref[s], score_ref, acc_ref)
            other_top, other_denom = stats_in[s, 0:1], stats_in[s, 1:2]
            overall = jnp.maximum(top, other_top)
            scale, other_scale = jnp.exp2(top - overall), jnp.exp2(other_top - overall)
            share = 1.0 / (scale * denom + other_scale * other_denom)
            finish(acc * (scale * share), other_scale * share)

        @pl.when(jnp.logical_not(useful))
        def _():
            finish(None, 1.0 / stats_in[s, 1:2])


def swap(piece, axis, flip):
    array, places = piece
    came = lax.ppermute(array, axis, [(i, i ^ flip) for i in range(lax.axis_size(axis))])
    if axis == "row":
        return came, [(r ^ flip, c) for r, c in places]
    return came, [(r, c ^ flip) for r, c in places]


def join_pieces(pieces, transpose=True):
    vmem = pl.BlockSpec(memory_space=pltpu.VMEM)
    first = pieces[0][0]
    blocks = sum(array.shape[0] for array, _ in pieces)
    array = pl.pallas_call(
        functools.partial(join_kernel, transpose),
        out_shape=jax.ShapeDtypeStruct((blocks,) + first.shape[1:], first.dtype),
        in_specs=[vmem] * len(pieces),
        out_specs=vmem,
        compiler_params=pltpu.CompilerParams(vmem_limit_bytes=4 * 1024 * 1024),
        name="join",
    )(*(array for array, _ in pieces))
    return array, [place for _, places in pieces for place in places]


def together(pieces, *others):
    arrays = lax.optimization_barrier([array for array, _ in pieces] + list(others))
    held = [(array, places) for array, (_, places) in zip(arrays, pieces)]
    return (held, *arrays[len(held) :]) if others else held


def across(piece, cols):
    pieces = [piece]
    flip = CORES
    while flip < cols:
        pieces += [swap(one, "col", flip) for one in pieces]
        flip *= 2
    return pieces[1:]


def per_device(queries, keys, values, block_list, block_count):
    head_size = keys.shape[2]
    heads = queries.shape[2] // head_size
    own_blocks = queries.shape[1] // BLOCK
    per = keys.shape[1] // BLOCK
    rows = lax.axis_size("row")
    cols = lax.axis_size("col")
    panels, slots = block_list.shape[2:]
    blocks = panels * slots
    vmem = pl.BlockSpec(memory_space=pltpu.VMEM)
    smem = pl.BlockSpec(memory_space=pltpu.SMEM)
    anywhere = pl.BlockSpec(memory_space=pl.ANY)
    small = pltpu.CompilerParams(vmem_limit_bytes=4 * 1024 * 1024)

    shape = (per, BLOCK, head_size)
    packed = jnp.concatenate([keys.reshape(shape), values.reshape(shape)], axis=1)

    own = (packed, [(0, 0)])
    flip = rows // 2
    while flip > 2:
        came = swap(own, "row", flip)
        own = jnp.concatenate([own[0], came[0]]), own[1] + came[1]
        flip //= 2
    near, far, opposite = (swap(own, "row", flip) for flip in (1, 3, 2))
    own_across = across(own, cols)
    near_across = [swap(piece, "row", 1) for piece in own_across]
    early_places = [place for _, where in (own, *own_across, near, *near_across, far, opposite) for place in where]
    late_places = [(r, c ^ flip) for flip in range(CORES, cols, CORES) for r, c in far[1] + opposite[1]]
    places = [where + [(r, c ^ 1) for r, c in where] for where in (early_places, late_places)]

    longest = max(len(where) for where in places) * per
    dense = longest <= 16
    width = heads * BLOCK
    order_shape = (own_blocks, len(places), longest, width) if dense else (own_blocks, len(places), longest + 3)
    order = pl.pallas_call(
        functools.partial(prepare_kernel, per, places, dense),
        out_shape=jax.ShapeDtypeStruct(order_shape, jnp.int32),
        in_specs=[anywhere, anywhere],
        out_specs=vmem if dense else smem,
        scratch_shapes=[
            pltpu.SMEM((blocks,), jnp.int32),
            pltpu.SMEM((own_blocks, panels, slots), jnp.int32),
            pltpu.SMEM((own_blocks, panels), jnp.int32),
            pltpu.SemaphoreType.DMA((2,)),
        ],
        compiler_params=small,
        name="prepare",
    )(block_list, block_count)
    (far,), order = together([far], order)
    far_across, queries = together(across(far, cols), queries)
    last = far_across + across(opposite, cols)
    halves = [join_pieces([own, *own_across]), join_pieces([near, *near_across]), join_pieces([far, opposite])]
    early = join_pieces(halves + [swap(half, "col", 1) for half in halves], False)

    def attend(kernel, name, out_shape, out_specs, scratch, *args):
        held = args[2].shape[0] + args[2].shape[0] % 2
        scratch = scratch + [
            pltpu.VMEM((held, BLOCK, width), jnp.float32),
            pltpu.VMEM((head_size, width), jnp.float32),
        ]
        if not dense:
            scratch += [pltpu.SMEM(order.shape, jnp.int32), pltpu.SemaphoreType.DMA]
        return pl.pallas_call(
            functools.partial(kernel, heads, dense),
            out_shape=out_shape,
            in_specs=[vmem, vmem if dense else anywhere] + [vmem] * (len(args) - 2),
            out_specs=out_specs,
            scratch_shapes=scratch,
            compiler_params=pltpu.CompilerParams(vmem_limit_bytes=2 * held * BLOCK * width * 4 + 8 * 1024 * 1024),
            name=name,
        )(*args)

    queries_across = pl.pallas_call(
        functools.partial(turn_kernel, heads),
        out_shape=jax.ShapeDtypeStruct((own_blocks, head_size, width), queries.dtype),
        in_specs=[vmem],
        out_specs=vmem,
        compiler_params=small,
        name="turn",
    )(queries)
    last, queries_across = together(last, queries_across)
    parts = (
        jax.ShapeDtypeStruct((own_blocks, head_size, width), jnp.float32),
        jax.ShapeDtypeStruct((own_blocks, 2, width), jnp.float32),
    )
    part = attend(early_kernel, "early", parts, (vmem, vmem), [], queries_across, order, early[0])
    last = join_pieces(last)
    last_pair, *part = together([swap(last, "col", 1)], *part)
    last = join_pieces([last, *last_pair], False)
    whole = jax.ShapeDtypeStruct(queries.shape, jnp.bfloat16)
    out_scratch = [pltpu.VMEM(queries.shape, jnp.bfloat16), pltpu.SemaphoreType.DMA((own_blocks, heads))]
    end = functools.partial(last_kernel, per, places[1])
    return attend(end, "last", whole, anywhere, out_scratch, queries_across, order, last[0], *part)


def solution(mesh):
    placed = (
        P(("groups", "col"), "row", None),
        P(("groups", "row"), "col", None),
        P(("groups", "row"), "col", None),
        P("groups", None, None, None),
        P("groups", None, None),
    )
    return jax.shard_map(
        per_device,
        mesh=mesh,
        in_specs=placed,
        out_specs=P(("groups", "col"), "row", None),
        check_vma=False,
    )
```

```python
import functools
import math

import jax
import jax.numpy as jnp
from jax import lax
from jax.experimental import pallas as pl
from jax.experimental.pallas import tpu as pltpu
from jax.sharding import PartitionSpec as P

BLOCK = 128
CORES = 2

floor_score = -1e30
floor_top = -1e20


def join_kernel(transpose, *refs):
    out_ref = refs[-1]
    first = 0
    for ref in refs[:-1]:
        if not transpose:
            out_ref[first : first + ref.shape[0]] = ref[...]
        for n in range(ref.shape[0] if transpose else 0):
            out_ref[first + n, :BLOCK, :] = ref[n, :BLOCK, :]
            out_ref[first + n, BLOCK:, :] = ref[n, BLOCK:, :].T
        first += ref.shape[0]


def prepare_kernel(per, places, dense, list_hbm, count_hbm, order_ref, active_ref, list_ref, count_ref, sems):
    own_blocks = order_ref.shape[0]
    panels, slots = list_ref.shape[1:]
    cols = lax.axis_size("col")
    col_index = lax.axis_index("col")
    row_index = lax.axis_index("row")
    first = row_index * own_blocks
    copies = (
        pltpu.make_async_copy(list_hbm.at[col_index, pl.ds(first, own_blocks)], list_ref, sems.at[0]),
        pltpu.make_async_copy(count_hbm.at[col_index, pl.ds(first, own_blocks)], count_ref, sems.at[1]),
    )
    for copy in copies:
        copy.start()
    for copy in copies:
        copy.wait()
    for s in range(own_blocks):
        diagonal = col_index * list_hbm.shape[1] + first + s
        for r in range(panels):
            for n in range(slots):
                active_ref[r * slots + n] = 0
            for n in reversed(range(slots)):
                active_ref[r * slots + list_ref[s, r, n]] = (n < count_ref[s, r]).astype(jnp.int32)
        for part, where in enumerate(places):
            total = jnp.int32(0)
            diagonal_slot = jnp.int32(-1)
            for n, (row_flip, col_flip) in enumerate(where):
                for k in range(per):
                    slot = n * per + k
                    block = ((row_index ^ row_flip) * cols + (col_index ^ col_flip)) * per + k
                    on_diagonal = block == diagonal
                    if dense:
                        reach = jnp.where(on_diagonal, 0, jnp.where(active_ref[block] > 0, BLOCK, -BLOCK))
                        order_ref[s, part, slot : slot + 1, :] = jnp.full((1, order_ref.shape[3]), reach, jnp.int32)
                        continue
                    order_ref[s, part, total] = slot
                    diagonal_slot = jnp.where(on_diagonal, slot, diagonal_slot)
                    total = total + jnp.where(on_diagonal, 0, active_ref[block])
            if dense:
                continue
            end = order_ref.shape[2] - 2
            here = diagonal_slot >= 0
            order_ref[s, part, total] = diagonal_slot
            order_ref[s, part, end + 1] = jnp.where(here, total, -1)
            total = total + here.astype(jnp.int32)
            order_ref[s, part, total] = 0
            order_ref[s, part, end] = total


def blockwise(array, fold):
    return fold(array.reshape(array.shape[0] // 8, 8, array.shape[1]), axis=0)


def dense_attention(reach, kv_ref, queries, score_ref):
    head_size, width = queries.shape
    slots = kv_ref.shape[0]
    factor = math.log2(math.e) / head_size**0.5
    key_at = lax.broadcasted_iota(jnp.int32, (BLOCK, width), 0)
    query_at = lax.broadcasted_iota(jnp.int32, (BLOCK, width), 1) % BLOCK
    keys = jnp.concatenate([kv_ref[slot, :BLOCK, :] for slot in range(slots)])
    found = jnp.dot(keys, queries, preferred_element_type=jnp.float32)
    top = jnp.full((8, width), floor_top, jnp.float32)
    for slot in range(slots):
        seen = query_at + reach[slot : slot + 1, :] >= key_at
        one = jnp.where(seen, found[slot * BLOCK : (slot + 1) * BLOCK], floor_score)
        score_ref[slot] = one
        top = jnp.maximum(top, blockwise(one, jnp.max))
    top = jnp.max(top, axis=0, keepdims=True) * factor
    denom = jnp.zeros((8, width), jnp.float32)
    rounded = []
    for slot in range(slots):
        one = jnp.exp2(score_ref[slot] * factor - top)
        denom = denom + blockwise(one, jnp.sum)
        rounded.append(one.astype(jnp.bfloat16))
    values = jnp.concatenate([kv_ref[slot, BLOCK:, :] for slot in range(slots)], axis=1)
    acc = jnp.dot(values, jnp.concatenate(rounded), preferred_element_type=jnp.float32)
    return acc, top, jnp.sum(denom, axis=0, keepdims=True)


def listed_attention(s, part, order_ref, kv_ref, queries, score_ref, acc_ref):
    head_size, width = queries.shape
    end = order_ref.shape[2] - 2
    factor = math.log2(math.e) / head_size**0.5
    total = order_ref[s, part, end]
    diagonal = order_ref[s, part, end + 1]
    pairs = (total + 1) // 2
    key_at = lax.broadcasted_iota(jnp.int32, (BLOCK, width), 0)
    query_at = lax.broadcasted_iota(jnp.int32, (BLOCK, width), 1) % BLOCK

    def score(p, top):
        pair = [order_ref[s, part, 2 * p + n] for n in range(2)]
        keys = jnp.concatenate([kv_ref[slot, :BLOCK, :] for slot in pair])
        found = jnp.dot(keys, queries, preferred_element_type=jnp.float32)
        for n in range(2):
            t = 2 * p + n
            reach = jnp.where(t == diagonal, 0, jnp.where(t < total, BLOCK, -BLOCK))
            one = jnp.where(query_at + reach >= key_at, found[n * BLOCK : (n + 1) * BLOCK], floor_score)
            score_ref[t] = one
            top = jnp.maximum(top, blockwise(one, jnp.max))
        return top

    top = lax.fori_loop(0, pairs, score, jnp.full((8, width), floor_top, jnp.float32))
    top = jnp.max(top, axis=0, keepdims=True) * factor
    acc_ref[...] = jnp.zeros_like(acc_ref)

    def mix(p, denom):
        pair = [order_ref[s, part, 2 * p + n] for n in range(2)]
        values = jnp.concatenate([kv_ref[slot, BLOCK:, :] for slot in pair], axis=1)
        weights = [jnp.exp2(score_ref[2 * p + n] * factor - top) for n in range(2)]
        rounded = jnp.concatenate([one.astype(jnp.bfloat16) for one in weights])
        acc_ref[...] += jnp.dot(values, rounded, preferred_element_type=jnp.float32)
        return denom + blockwise(weights[0] + weights[1], jnp.sum)

    denom = lax.fori_loop(0, pairs, mix, jnp.zeros((8, width), jnp.float32))
    return acc_ref[...], top, jnp.sum(denom, axis=0, keepdims=True)


def get_order(dense, order_ref, scratch):
    if dense:
        return order_ref
    held, sem = scratch
    copy = pltpu.make_async_copy(order_ref, held, sem)
    copy.start()
    copy.wait()
    return held


def attention(dense, s, part, order_ref, kv_ref, queries, score_ref, acc_ref):
    if dense:
        return dense_attention(order_ref[s, part], kv_ref, queries, score_ref)
    return listed_attention(s, part, order_ref, kv_ref, queries, score_ref, acc_ref)


def turn_kernel(heads, q_ref, qt_ref):
    own_blocks, head_size = qt_ref.shape[:2]
    for s in range(own_blocks):
        for h in range(heads):
            tile = q_ref[0, pl.ds(s * BLOCK, BLOCK), pl.ds(h * head_size, head_size)]
            qt_ref[s, :, pl.ds(h * BLOCK, BLOCK)] = tile.T


def early_kernel(heads, dense, qt_ref, order_in, kv_ref, acc_out, stats_out, score_ref, acc_ref, *scratch):
    order_ref = get_order(dense, order_in, scratch)
    for s in range(qt_ref.shape[0]):
        acc, top, denom = attention(dense, s, 0, order_ref, kv_ref, qt_ref[s], score_ref, acc_ref)
        acc_out[s] = acc
        stats_out[s, 0:1] = top
        stats_out[s, 1:2] = denom


def last_kernel(per, places, heads, dense, qt_ref, order_in, kv_ref, acc_in, stats_in, out_hbm,
                out_ref, out_sems, score_ref, acc_ref, *scratch):
    order_ref = get_order(dense, order_in, scratch)
    own_blocks, head_size, width = qt_ref.shape
    rows, cols = lax.axis_size("row"), lax.axis_size("col")
    row_index, col_index = lax.axis_index("row"), lax.axis_index("col")
    sources = [(row_index ^ row_flip) * cols + (col_index ^ col_flip) for row_flip, col_flip in places]
    earliest = functools.reduce(jnp.minimum, sources) * per

    for s in range(own_blocks):
        useful = earliest <= (col_index * rows + row_index) * own_blocks + s

        def finish(acc, scale):
            copies = []
            for h in range(heads):
                at = pl.ds(h * head_size, head_size)
                cut = slice(h * BLOCK, (h + 1) * BLOCK)
                one = acc_in[s, :, cut] * scale[:, cut]
                if acc is not None:
                    one = one + acc[:, cut]
                out_ref[0, pl.ds(s * BLOCK, BLOCK), at] = one.astype(out_ref.dtype).T
                place = (0, pl.ds(s * BLOCK, BLOCK), at)
                copies.append(pltpu.make_async_copy(out_ref.at[place], out_hbm.at[place], out_sems.at[s, h]))
                copies[-1].start()
            for copy in copies:
                copy.wait()

        @pl.when(useful)
        def _():
            acc, top, denom = attention(dense, s, 1, order_ref, kv_ref, qt_ref[s], score_ref, acc_ref)
            other_top, other_denom = stats_in[s, 0:1], stats_in[s, 1:2]
            overall = jnp.maximum(top, other_top)
            scale, other_scale = jnp.exp2(top - overall), jnp.exp2(other_top - overall)
            share = 1.0 / (scale * denom + other_scale * other_denom)
            finish(acc * (scale * share), other_scale * share)

        @pl.when(jnp.logical_not(useful))
        def _():
            finish(None, 1.0 / stats_in[s, 1:2])


def swap(piece, axis, flip):
    array, places = piece
    came = lax.ppermute(array, axis, [(i, i ^ flip) for i in range(lax.axis_size(axis))])
    if axis == "row":
        return came, [(r ^ flip, c) for r, c in places]
    return came, [(r, c ^ flip) for r, c in places]


def join_pieces(pieces, transpose=True):
    vmem = pl.BlockSpec(memory_space=pltpu.VMEM)
    first = pieces[0][0]
    blocks = sum(array.shape[0] for array, _ in pieces)
    array = pl.pallas_call(
        functools.partial(join_kernel, transpose),
        out_shape=jax.ShapeDtypeStruct((blocks,) + first.shape[1:], first.dtype),
        in_specs=[vmem] * len(pieces),
        out_specs=vmem,
        compiler_params=pltpu.CompilerParams(vmem_limit_bytes=4 * 1024 * 1024),
        name="join",
    )(*(array for array, _ in pieces))
    return array, [place for _, places in pieces for place in places]


def together(pieces, *others):
    arrays = lax.optimization_barrier([array for array, _ in pieces] + list(others))
    held = [(array, places) for array, (_, places) in zip(arrays, pieces)]
    return (held, *arrays[len(held) :]) if others else held


def across(piece, cols):
    pieces = [piece]
    flip = CORES
    while flip < cols:
        pieces += [swap(one, "col", flip) for one in pieces]
        flip *= 2
    return pieces[1:]


def per_device(queries, keys, values, block_list, block_count):
    head_size = keys.shape[2]
    heads = queries.shape[2] // head_size
    own_blocks = queries.shape[1] // BLOCK
    per = keys.shape[1] // BLOCK
    rows = lax.axis_size("row")
    cols = lax.axis_size("col")
    panels, slots = block_list.shape[2:]
    blocks = panels * slots
    vmem = pl.BlockSpec(memory_space=pltpu.VMEM)
    smem = pl.BlockSpec(memory_space=pltpu.SMEM)
    anywhere = pl.BlockSpec(memory_space=pl.ANY)
    small = pltpu.CompilerParams(vmem_limit_bytes=4 * 1024 * 1024)

    shape = (per, BLOCK, head_size)
    packed = jnp.concatenate([keys.reshape(shape), values.reshape(shape)], axis=1)

    own = (packed, [(0, 0)])
    flip = rows // 2
    while flip > 2:
        came = swap(own, "row", flip)
        own = jnp.concatenate([own[0], came[0]]), own[1] + came[1]
        flip //= 2
    near, far, opposite = (swap(own, "row", flip) for flip in (1, 3, 2))
    own_across = across(own, cols)
    near_across = [swap(piece, "row", 1) for piece in own_across]
    early_places = [place for _, where in (own, *own_across, near, *near_across, far, opposite) for place in where]
    late_places = [(r, c ^ flip) for flip in range(CORES, cols, CORES) for r, c in far[1] + opposite[1]]
    places = [where + [(r, c ^ 1) for r, c in where] for where in (early_places, late_places)]

    longest = max(len(where) for where in places) * per
    dense = longest <= 16
    width = heads * BLOCK
    order_shape = (own_blocks, len(places), longest, width) if dense else (own_blocks, len(places), longest + 3)
    order = pl.pallas_call(
        functools.partial(prepare_kernel, per, places, dense),
        out_shape=jax.ShapeDtypeStruct(order_shape, jnp.int32),
        in_specs=[anywhere, anywhere],
        out_specs=vmem if dense else smem,
        scratch_shapes=[
            pltpu.SMEM((blocks,), jnp.int32),
            pltpu.SMEM((own_blocks, panels, slots), jnp.int32),
            pltpu.SMEM((own_blocks, panels), jnp.int32),
            pltpu.SemaphoreType.DMA((2,)),
        ],
        compiler_params=small,
        name="prepare",
    )(block_list, block_count)
    far_across, queries, order = together(across(far, cols), queries, order)
    last = far_across + across(opposite, cols)
    halves = [join_pieces([own, *own_across]), join_pieces([near, *near_across]), join_pieces([far, opposite])]
    early = join_pieces(halves + [swap(half, "col", 1) for half in halves], False)

    def attend(kernel, name, out_shape, out_specs, scratch, *args):
        held = args[2].shape[0] + args[2].shape[0] % 2
        scratch = scratch + [
            pltpu.VMEM((held, BLOCK, width), jnp.float32),
            pltpu.VMEM((head_size, width), jnp.float32),
        ]
        if not dense:
            scratch += [pltpu.SMEM(order.shape, jnp.int32), pltpu.SemaphoreType.DMA]
        return pl.pallas_call(
            functools.partial(kernel, heads, dense),
            out_shape=out_shape,
            in_specs=[vmem, vmem if dense else anywhere] + [vmem] * (len(args) - 2),
            out_specs=out_specs,
            scratch_shapes=scratch,
            compiler_params=pltpu.CompilerParams(vmem_limit_bytes=2 * held * BLOCK * width * 4 + 8 * 1024 * 1024),
            name=name,
        )(*args)

    queries_across = pl.pallas_call(
        functools.partial(turn_kernel, heads),
        out_shape=jax.ShapeDtypeStruct((own_blocks, head_size, width), queries.dtype),
        in_specs=[vmem],
        out_specs=vmem,
        compiler_params=small,
        name="turn",
    )(queries)
    last, queries_across = together(last, queries_across)
    parts = (
        jax.ShapeDtypeStruct((own_blocks, head_size, width), jnp.float32),
        jax.ShapeDtypeStruct((own_blocks, 2, width), jnp.float32),
    )
    part = attend(early_kernel, "early", parts, (vmem, vmem), [], queries_across, order, early[0])
    last = join_pieces(last)
    last_pair, *part = together([swap(last, "col", 1)], *part)
    last = join_pieces([last, *last_pair], False)
    whole = jax.ShapeDtypeStruct(queries.shape, jnp.bfloat16)
    out_scratch = [pltpu.VMEM(queries.shape, jnp.bfloat16), pltpu.SemaphoreType.DMA((own_blocks, heads))]
    end = functools.partial(last_kernel, per, places[1])
    return attend(end, "last", whole, anywhere, out_scratch, queries_across, order, last[0], *part)


def solution(mesh):
    placed = (
        P(("groups", "col"), "row", None),
        P(("groups", "row"), "col", None),
        P(("groups", "row"), "col", None),
        P("groups", None, None, None),
        P("groups", None, None),
    )
    return jax.shard_map(
        per_device,
        mesh=mesh,
        in_specs=placed,
        out_specs=P(("groups", "col"), "row", None),
        check_vma=False,
    )
```

```python
import functools
import math

import jax
import jax.numpy as jnp
from jax import lax
from jax.experimental import pallas as pl
from jax.experimental.pallas import tpu as pltpu
from jax.sharding import PartitionSpec as P

BLOCK = 128
CORES = 2

floor_score = -1e30
floor_top = -1e20


def join_kernel(transpose, *refs):
    out_ref = refs[-1]
    first = 0
    for ref in refs[:-1]:
        if not transpose:
            out_ref[first : first + ref.shape[0]] = ref[...]
        for n in range(ref.shape[0] if transpose else 0):
            out_ref[first + n, :BLOCK, :] = ref[n, :BLOCK, :]
            out_ref[first + n, BLOCK:, :] = ref[n, BLOCK:, :].T
        first += ref.shape[0]


def prepare_kernel(per, places, dense, list_hbm, count_hbm, order_ref, active_ref, list_ref, count_ref, sems):
    own_blocks = order_ref.shape[0]
    panels, slots = list_ref.shape[1:]
    cols = lax.axis_size("col")
    col_index = lax.axis_index("col")
    row_index = lax.axis_index("row")
    first = row_index * own_blocks
    copies = (
        pltpu.make_async_copy(list_hbm.at[col_index, pl.ds(first, own_blocks)], list_ref, sems.at[0]),
        pltpu.make_async_copy(count_hbm.at[col_index, pl.ds(first, own_blocks)], count_ref, sems.at[1]),
    )
    for copy in copies:
        copy.start()
    for copy in copies:
        copy.wait()
    for s in range(own_blocks):
        diagonal = col_index * list_hbm.shape[1] + first + s
        for r in range(panels):
            for n in range(slots):
                active_ref[r * slots + n] = 0
            for n in reversed(range(slots)):
                active_ref[r * slots + list_ref[s, r, n]] = (n < count_ref[s, r]).astype(jnp.int32)
        for part, where in enumerate(places):
            total = jnp.int32(0)
            diagonal_slot = jnp.int32(-1)
            for n, (row_flip, col_flip) in enumerate(where):
                for k in range(per):
                    slot = n * per + k
                    block = ((row_index ^ row_flip) * cols + (col_index ^ col_flip)) * per + k
                    on_diagonal = block == diagonal
                    if dense:
                        reach = jnp.where(on_diagonal, 0, jnp.where(active_ref[block] > 0, BLOCK, -BLOCK))
                        order_ref[s, part, slot : slot + 1, :] = jnp.full((1, order_ref.shape[3]), reach, jnp.int32)
                        continue
                    order_ref[s, part, total] = slot
                    diagonal_slot = jnp.where(on_diagonal, slot, diagonal_slot)
                    total = total + jnp.where(on_diagonal, 0, active_ref[block])
            if dense:
                continue
            end = order_ref.shape[2] - 2
            here = diagonal_slot >= 0
            order_ref[s, part, total] = diagonal_slot
            order_ref[s, part, end + 1] = jnp.where(here, total, -1)
            total = total + here.astype(jnp.int32)
            order_ref[s, part, total] = 0
            order_ref[s, part, end] = total


def blockwise(array, fold):
    return fold(array.reshape(array.shape[0] // 8, 8, array.shape[1]), axis=0)


def dense_attention(reach, kv_ref, queries, score_ref):
    head_size, width = queries.shape
    slots = kv_ref.shape[0]
    factor = math.log2(math.e) / head_size**0.5
    key_at = lax.broadcasted_iota(jnp.int32, (BLOCK, width), 0)
    query_at = lax.broadcasted_iota(jnp.int32, (BLOCK, width), 1) % BLOCK
    keys = jnp.concatenate([kv_ref[slot, :BLOCK, :] for slot in range(slots)])
    found = jnp.dot(keys, queries, preferred_element_type=jnp.float32)
    top = jnp.full((8, width), floor_top, jnp.float32)
    for slot in range(slots):
        seen = query_at + reach[slot : slot + 1, :] >= key_at
        one = jnp.where(seen, found[slot * BLOCK : (slot + 1) * BLOCK], floor_score)
        score_ref[slot] = one
        top = jnp.maximum(top, blockwise(one, jnp.max))
    top = jnp.max(top, axis=0, keepdims=True) * factor
    denom = jnp.zeros((8, width), jnp.float32)
    rounded = []
    for slot in range(slots):
        one = jnp.exp2(score_ref[slot] * factor - top)
        denom = denom + blockwise(one, jnp.sum)
        rounded.append(one.astype(jnp.bfloat16))
    values = jnp.concatenate([kv_ref[slot, BLOCK:, :] for slot in range(slots)], axis=1)
    acc = jnp.dot(values, jnp.concatenate(rounded), preferred_element_type=jnp.float32)
    return acc, top, jnp.sum(denom, axis=0, keepdims=True)


def listed_attention(s, part, order_ref, kv_ref, queries, score_ref, acc_ref):
    head_size, width = queries.shape
    end = order_ref.shape[2] - 2
    factor = math.log2(math.e) / head_size**0.5
    total = order_ref[s, part, end]
    diagonal = order_ref[s, part, end + 1]
    pairs = (total + 1) // 2
    key_at = lax.broadcasted_iota(jnp.int32, (BLOCK, width), 0)
    query_at = lax.broadcasted_iota(jnp.int32, (BLOCK, width), 1) % BLOCK

    def score(p, top):
        pair = [order_ref[s, part, 2 * p + n] for n in range(2)]
        keys = jnp.concatenate([kv_ref[slot, :BLOCK, :] for slot in pair])
        found = jnp.dot(keys, queries, preferred_element_type=jnp.float32)
        for n in range(2):
            t = 2 * p + n
            reach = jnp.where(t == diagonal, 0, jnp.where(t < total, BLOCK, -BLOCK))
            one = jnp.where(query_at + reach >= key_at, found[n * BLOCK : (n + 1) * BLOCK], floor_score)
            score_ref[t] = one
            top = jnp.maximum(top, blockwise(one, jnp.max))
        return top

    top = lax.fori_loop(0, pairs, score, jnp.full((8, width), floor_top, jnp.float32))
    top = jnp.max(top, axis=0, keepdims=True) * factor
    acc_ref[...] = jnp.zeros_like(acc_ref)

    def mix(p, denom):
        pair = [order_ref[s, part, 2 * p + n] for n in range(2)]
        values = jnp.concatenate([kv_ref[slot, BLOCK:, :] for slot in pair], axis=1)
        weights = [jnp.exp2(score_ref[2 * p + n] * factor - top) for n in range(2)]
        rounded = jnp.concatenate([one.astype(jnp.bfloat16) for one in weights])
        acc_ref[...] += jnp.dot(values, rounded, preferred_element_type=jnp.float32)
        return denom + blockwise(weights[0] + weights[1], jnp.sum)

    denom = lax.fori_loop(0, pairs, mix, jnp.zeros((8, width), jnp.float32))
    return acc_ref[...], top, jnp.sum(denom, axis=0, keepdims=True)


def get_order(dense, order_ref, scratch):
    if dense:
        return order_ref
    held, sem = scratch
    copy = pltpu.make_async_copy(order_ref, held, sem)
    copy.start()
    copy.wait()
    return held


def attention(dense, s, part, order_ref, kv_ref, queries, score_ref, acc_ref):
    if dense:
        return dense_attention(order_ref[s, part], kv_ref, queries, score_ref)
    return listed_attention(s, part, order_ref, kv_ref, queries, score_ref, acc_ref)


def turn_kernel(heads, q_ref, qt_ref):
    own_blocks, head_size = qt_ref.shape[:2]
    for s in range(own_blocks):
        for h in range(heads):
            tile = q_ref[0, pl.ds(s * BLOCK, BLOCK), pl.ds(h * head_size, head_size)]
            qt_ref[s, :, pl.ds(h * BLOCK, BLOCK)] = tile.T


def early_kernel(heads, dense, qt_ref, order_in, kv_ref, acc_out, stats_out, score_ref, acc_ref, *scratch):
    order_ref = get_order(dense, order_in, scratch)
    for s in range(qt_ref.shape[0]):
        acc, top, denom = attention(dense, s, 0, order_ref, kv_ref, qt_ref[s], score_ref, acc_ref)
        acc_out[s] = acc
        stats_out[s, 0:1] = top
        stats_out[s, 1:2] = denom


def last_kernel(per, places, heads, dense, qt_ref, order_in, kv_ref, acc_in, stats_in, out_hbm,
                out_ref, out_sems, score_ref, acc_ref, *scratch):
    order_ref = get_order(dense, order_in, scratch)
    own_blocks, head_size, width = qt_ref.shape
    rows, cols = lax.axis_size("row"), lax.axis_size("col")
    row_index, col_index = lax.axis_index("row"), lax.axis_index("col")
    sources = [(row_index ^ row_flip) * cols + (col_index ^ col_flip) for row_flip, col_flip in places]
    earliest = functools.reduce(jnp.minimum, sources) * per

    for s in range(own_blocks):
        useful = earliest <= (col_index * rows + row_index) * own_blocks + s

        def finish(acc, scale):
            for h in range(heads):
                at = pl.ds(h * head_size, head_size)
                cut = slice(h * BLOCK, (h + 1) * BLOCK)
                one = acc_in[s, :, cut] * scale[:, cut]
                if acc is not None:
                    one = one + acc[:, cut]
                out_ref[0, pl.ds(s * BLOCK, BLOCK), at] = one.astype(out_ref.dtype).T
            place = (0, pl.ds(s * BLOCK, BLOCK))
            copy = pltpu.make_async_copy(out_ref.at[place], out_hbm.at[place], out_sems.at[s, 0])
            copy.start()
            copy.wait()

        @pl.when(useful)
        def _():
            acc, top, denom = attention(dense, s, 1, order_ref, kv_ref, qt_ref[s], score_ref, acc_ref)
            other_top, other_denom = stats_in[s, 0:1], stats_in[s, 1:2]
            overall = jnp.maximum(top, other_top)
            scale, other_scale = jnp.exp2(top - overall), jnp.exp2(other_top - overall)
            share = 1.0 / (scale * denom + other_scale * other_denom)
            finish(acc * (scale * share), other_scale * share)

        @pl.when(jnp.logical_not(useful))
        def _():
            finish(None, 1.0 / stats_in[s, 1:2])


def swap(piece, axis, flip):
    array, places = piece
    came = lax.ppermute(array, axis, [(i, i ^ flip) for i in range(lax.axis_size(axis))])
    if axis == "row":
        return came, [(r ^ flip, c) for r, c in places]
    return came, [(r, c ^ flip) for r, c in places]


def join_pieces(pieces, transpose=True):
    vmem = pl.BlockSpec(memory_space=pltpu.VMEM)
    first = pieces[0][0]
    blocks = sum(array.shape[0] for array, _ in pieces)
    array = pl.pallas_call(
        functools.partial(join_kernel, transpose),
        out_shape=jax.ShapeDtypeStruct((blocks,) + first.shape[1:], first.dtype),
        in_specs=[vmem] * len(pieces),
        out_specs=vmem,
        compiler_params=pltpu.CompilerParams(vmem_limit_bytes=4 * 1024 * 1024),
        name="join",
    )(*(array for array, _ in pieces))
    return array, [place for _, places in pieces for place in places]


def together(pieces, *others):
    arrays = lax.optimization_barrier([array for array, _ in pieces] + list(others))
    held = [(array, places) for array, (_, places) in zip(arrays, pieces)]
    return (held, *arrays[len(held) :]) if others else held


def across(piece, cols):
    pieces = [piece]
    flip = CORES
    while flip < cols:
        pieces += [swap(one, "col", flip) for one in pieces]
        flip *= 2
    return pieces[1:]


def per_device(queries, keys, values, block_list, block_count):
    head_size = keys.shape[2]
    heads = queries.shape[2] // head_size
    own_blocks = queries.shape[1] // BLOCK
    per = keys.shape[1] // BLOCK
    rows = lax.axis_size("row")
    cols = lax.axis_size("col")
    panels, slots = block_list.shape[2:]
    blocks = panels * slots
    vmem = pl.BlockSpec(memory_space=pltpu.VMEM)
    smem = pl.BlockSpec(memory_space=pltpu.SMEM)
    anywhere = pl.BlockSpec(memory_space=pl.ANY)
    small = pltpu.CompilerParams(vmem_limit_bytes=4 * 1024 * 1024)

    shape = (per, BLOCK, head_size)
    packed = jnp.concatenate([keys.reshape(shape), values.reshape(shape)], axis=1)

    own = (packed, [(0, 0)])
    flip = rows // 2
    while flip > 2:
        came = swap(own, "row", flip)
        own = jnp.concatenate([own[0], came[0]]), own[1] + came[1]
        flip //= 2
    near, far, opposite = (swap(own, "row", flip) for flip in (1, 2, 3))
    own_across = across(own, cols)
    near_across = [swap(piece, "row", 1) for piece in own_across]
    early_places = [place for _, where in (own, *own_across, near, *near_across, far, opposite) for place in where]
    late_places = [(r, c ^ flip) for flip in range(CORES, cols, CORES) for r, c in far[1] + opposite[1]]
    places = [where + [(r, c ^ 1) for r, c in where] for where in (early_places, late_places)]

    longest = max(len(where) for where in places) * per
    dense = longest <= 16
    width = heads * BLOCK
    order_shape = (own_blocks, len(places), longest, width) if dense else (own_blocks, len(places), longest + 3)
    order = pl.pallas_call(
        functools.partial(prepare_kernel, per, places, dense),
        out_shape=jax.ShapeDtypeStruct(order_shape, jnp.int32),
        in_specs=[anywhere, anywhere],
        out_specs=vmem if dense else smem,
        scratch_shapes=[
            pltpu.SMEM((blocks,), jnp.int32),
            pltpu.SMEM((own_blocks, panels, slots), jnp.int32),
            pltpu.SMEM((own_blocks, panels), jnp.int32),
            pltpu.SemaphoreType.DMA((2,)),
        ],
        compiler_params=small,
        name="prepare",
    )(block_list, block_count)
    (far,), order = together([far], order)
    far_across, queries = together(across(far, cols), queries)
    last = far_across + across(opposite, cols)
    halves = [join_pieces([own, *own_across]), join_pieces([near, *near_across]), join_pieces([far, opposite])]
    early = join_pieces(halves + [swap(half, "col", 1) for half in halves], False)

    def attend(kernel, name, out_shape, out_specs, scratch, *args):
        held = args[2].shape[0] + args[2].shape[0] % 2
        scratch = scratch + [
            pltpu.VMEM((held, BLOCK, width), jnp.float32),
            pltpu.VMEM((head_size, width), jnp.float32),
        ]
        if not dense:
            scratch += [pltpu.SMEM(order.shape, jnp.int32), pltpu.SemaphoreType.DMA]
        return pl.pallas_call(
            functools.partial(kernel, heads, dense),
            out_shape=out_shape,
            in_specs=[vmem, vmem if dense else anywhere] + [vmem] * (len(args) - 2),
            out_specs=out_specs,
            scratch_shapes=scratch,
            compiler_params=pltpu.CompilerParams(vmem_limit_bytes=2 * held * BLOCK * width * 4 + 8 * 1024 * 1024),
            name=name,
        )(*args)

    queries_across = pl.pallas_call(
        functools.partial(turn_kernel, heads),
        out_shape=jax.ShapeDtypeStruct((own_blocks, head_size, width), queries.dtype),
        in_specs=[vmem],
        out_specs=vmem,
        compiler_params=small,
        name="turn",
    )(queries)
    last, queries_across = together(last, queries_across)
    parts = (
        jax.ShapeDtypeStruct((own_blocks, head_size, width), jnp.float32),
        jax.ShapeDtypeStruct((own_blocks, 2, width), jnp.float32),
    )
    part = attend(early_kernel, "early", parts, (vmem, vmem), [], queries_across, order, early[0])
    last = join_pieces(last)
    last_pair, *part = together([swap(last, "col", 1)], *part)
    last = join_pieces([last, *last_pair], False)
    whole = jax.ShapeDtypeStruct(queries.shape, jnp.bfloat16)
    out_scratch = [pltpu.VMEM(queries.shape, jnp.bfloat16), pltpu.SemaphoreType.DMA((own_blocks, heads))]
    end = functools.partial(last_kernel, per, places[1])
    return attend(end, "last", whole, anywhere, out_scratch, queries_across, order, last[0], *part)


def solution(mesh):
    placed = (
        P(("groups", "col"), "row", None),
        P(("groups", "row"), "col", None),
        P(("groups", "row"), "col", None),
        P("groups", None, None, None),
        P("groups", None, None),
    )
    return jax.shard_map(
        per_device,
        mesh=mesh,
        in_specs=placed,
        out_specs=P(("groups", "col"), "row", None),
        check_vma=False,
    )
```
